32 devices in a mesh: img: 2 (over x), gz: 8 (over z, y), gy: 2 (over core).
Axes of the slice: x: 2, y: 2, z: 4, core: 2. Of those that a mesh axis runs over, the one named last changes fastest.
Arguments:
- initial_block: float32 [32, 16, 32, 384], P('img', 'gz', 'gy'), parts along dimension 0, may hold values from -6 to 6, as said below
- concentration: float32 [32, 32, 384], P(('img', 'gz'), 'gy'), parts along dimension 0, may hold values from -1.2 to 1.2
- stiffness: float32 [16, 32, 384], P('gz', 'gy'), may hold values from 0.02 to 0.2
Outputs:
- ritz_values: float32 [16], P('img'), parts along dimension 0
- mode_density: float32 [32, 32, 384], P(('img', 'gz'), 'gy'), parts along dimension 0
- residual_density: float32 [32, 32, 384], P(('img', 'gz'), 'gy'), parts along dimension 0
The draws below stay inside these ranges and needn't reach their ends.
There are 2 independent parts, one for each index of `img`. The reference program is written for one: setup_inputs(seed, part) draws one part's arguments, and reference() takes and returns one part's arrays. A program takes and returns all parts, laid end to end along the dimension named above; an argument that names none is the same for every part. Nothing has to cross between parts.
Inputs may be any that keep to these rules, and one draw needn't show every extreme that they name: `initial_block`: the 16 starting vectors are linearly independent.
All inputs are finite; a program needn't handle non-finite values.
Results may differ from the reference program's by a relative error of at most 0.0003.
Values sent between devices are 32-bit elements; how exact they have to be, the bound alone decides.
No kernel may reach another device: no remote copies, remote signals or barrier semaphores. Data moves between devices by JAX's collectives and lax.ppermute only.
A program may use at most 64 MiB of HBM per device.

```python
import math
import jax
import jax.numpy as jnp
from jax import lax

NX = 384
BLOCK = 16
MODES = 8
ITERS = 2
NZ = 16
NY = 32


def parity_table():
    indices = jnp.arange(16, dtype=jnp.int32)
    common_bits = jnp.bitwise_and(indices[:, None], indices[None, :])
    bit_count = jnp.zeros((16, 16), jnp.int32)
    for bit_place in range(4):
        bit_count = bit_count + jnp.bitwise_and(jnp.right_shift(common_bits, bit_place), 1)
    return 1.0 - 2.0 * jnp.bitwise_and(bit_count, 1).astype(jnp.float32)


def draw_initial_block(key, part):
    key = jax.random.fold_in(key, 11)
    sign_key, order_key, phase_key, jitter_key = jax.random.split(key, 4)
    half_root = math.sqrt(0.5)
    quarter_turn = 0.5 * math.pi
    wave_table = [(0, 0, 0, -1, 0.0, half_root), (0, 0, 1, 0, 0.0, 1.0), (0, 0, 1, 0, quarter_turn, 1.0), (0, 1, 0, 1, 0.0, 1.0), (0, 1, 0, 1, quarter_turn, 1.0), (1, 0, 0, 2, 0.0, 1.0), (1, 0, 0, 2, quarter_turn, 1.0), (0, 0, 2, 3, 0.0, 1.0), (0, 1, 2, 4, 0.0, 1.0), (0, 1, 2, 4, quarter_turn, 1.0), (1, 0, 2, 5, 0.0, 1.0), (1, 0, 2, 5, quarter_turn, 1.0), (0, 2, 2, 6, 0.0, 1.0), (0, 0, 3, 7, 0.0, 1.0), (0, 0, 3, 7, quarter_turn, 1.0), (0, 0, 4, -1, 0.0, half_root)]
    sign_bits = jax.random.randint(sign_key, (2, 16), 0, 2).astype(jnp.float32)
    row_signs = 2.0 * sign_bits[0] - 1.0
    column_signs = 2.0 * sign_bits[1] - 1.0
    column_order = jax.random.permutation(order_key, 16)
    hadamard = parity_table()[:, column_order]
    mixing = 0.25 * row_signs[:, None] * column_signs[None, :] * hadamard
    phases = jax.random.uniform(phase_key, (8,), jnp.float32, -math.pi, math.pi)
    z_index = jnp.arange(NZ, dtype=jnp.int32)[:, None, None]
    y_index = jnp.arange(NY, dtype=jnp.int32)[None, :, None]
    x_index = jnp.arange(NX, dtype=jnp.int32)[None, None, :]
    waves_mixed = jnp.zeros((16, NZ, NY, NX), jnp.float32)
    for column, (z_steps, y_steps, x_steps, phase_slot, offset, amplitude) in enumerate(wave_table):
        eighths = (z_steps * z_index + y_steps * y_index + x_steps * x_index) % 8
        if phase_slot >= 0:
            phase_now = phases[phase_slot] + offset
        else:
            phase_now = jnp.float32(offset)
        plane_wave = amplitude * jnp.cos(eighths.astype(jnp.float32) * (math.pi / 4.0) + phase_now)
        waves_mixed = waves_mixed + mixing[:, column][:, None, None, None] * plane_wave[None]
    jitter = 0.35 * jax.random.truncated_normal(jitter_key, -5.0, 5.0, (16, NZ, NY, NX), jnp.float32)
    return waves_mixed + jitter


def steps_of(key, shape, pieces, least, top_value):
    factor_of, own = 1.0, jax.random.fold_in(key, 6)
    for position, parts in pieces:
        steps = jnp.exp(jax.random.uniform(jax.random.fold_in(own, position), (parts,), jnp.float32, least / len(pieces), top_value / len(pieces)))
        factor_of = factor_of * jnp.repeat(steps, shape[position] // parts).reshape([-1 if axis == position else 1 for axis in range(len(shape))])
    return factor_of


def setup_inputs(seed: int = 0, part: int = 0) -> dict:
    streams_of = jax.random.split(jax.random.key(seed), 4)
    own_keys = jax.random.split(jax.random.fold_in(streams_of[3], part), 4)
    initial_block = draw_initial_block(jax.random.fold_in(jax.random.fold_in(streams_of[3], part), 71), part)
    concentration = jnp.clip(jax.random.uniform(own_keys[1], (NZ, NY, NX), jnp.float32, -1.2, 1.2) * steps_of(own_keys[1], (NZ, NY, NX), ((0, 8), (1, 2)), -0.4, 0.0), -1.2, 1.2)
    stiffness = jnp.clip(jnp.exp(math.log(0.2) - 2.3025851 * jax.random.uniform(streams_of[2], (NZ, NY, NX), jnp.float32) ** steps_of(streams_of[2], (NZ, NY, NX), ((0, 8), (1, 2)), -0.2, 0.2)), 0.02, 0.2)
    return dict(initial_block=initial_block, concentration=concentration, stiffness=stiffness)


def second_difference(field, axis):
    return jnp.roll(field, -1, axis) + jnp.roll(field, 1, axis) - 2.0 * field

def hessian(vector, curvature, stiffness):
    total = curvature * vector
    for axis in (0, 1, 2):
        flux = stiffness * second_difference(vector, axis)
        total = total + second_difference(flux, axis)
    return total

def reference(initial_block, concentration, stiffness):
    highest = lax.Precision.HIGHEST
    curvature = 3.0 * concentration * concentration - 1.0
    precondition = curvature + 2.0
    for axis in (0, 1, 2):
        precondition = precondition + (jnp.roll(stiffness, -1, axis) + jnp.roll(stiffness, 1, axis) + 4.0 * stiffness)
    cells_total = concentration.shape[0] * concentration.shape[1] * concentration.shape[2]
    scale_factor = jnp.float32(cells_total / MODES)
    identity = jnp.eye(BLOCK, dtype=jnp.float32)
    search = initial_block
    ritz_all = jnp.zeros((BLOCK,), jnp.float32)
    modes = search[:MODES]
    residuals = search[:MODES]
    for iteration in range(ITERS):
        gram_matrix = jnp.einsum('azyx,bzyx->ab', search, search, precision=highest)
        lower_factor = jnp.linalg.cholesky(gram_matrix)
        lower_inverse = lax.linalg.triangular_solve(lower_factor, identity, left_side=True, lower=True)
        orthonormal = jnp.einsum('ab,bzyx->azyx', lower_inverse, search, precision=highest)
        images = lax.map(lambda vector: hessian(vector, curvature, stiffness), orthonormal)
        projected = jnp.einsum('azyx,bzyx->ab', orthonormal, images, precision=highest)
        projected = 0.5 * (projected + projected.T)
        ritz_all, ritz_vectors = jnp.linalg.eigh(projected)
        combination = ritz_vectors[:, :MODES]
        modes = jnp.einsum('azyx,aj->jzyx', orthonormal, combination, precision=highest)
        mode_images = jnp.einsum('azyx,aj->jzyx', images, combination, precision=highest)
        residuals = mode_images - ritz_all[:MODES, None, None, None] * modes
        corrections = residuals / precondition
        search = jnp.concatenate([modes, corrections], axis=0)
    mode_density = scale_factor * jnp.sum(modes * modes, axis=0)
    residual_density = scale_factor * jnp.sum(residuals * residuals, axis=0)
    return (ritz_all[:MODES], mode_density, residual_density)
```

```python
import functools

import jax
import jax.numpy as jnp
from jax import lax
from jax.experimental import pallas as pl
from jax.experimental.pallas import tpu as pltpu
from jax.sharding import PartitionSpec as P

BLOCK = 16
MODES = 8
ITERS = 2
HALF = BLOCK // 2
LANES = 128
MAX_SWEEPS = 14
HIGHEST = lax.Precision.HIGHEST


def neighbour_layers(x, axis, dim, first, last):
    size = lax.axis_size(axis)
    up = [(i, (i + 1) % size) for i in range(size)]
    down = [(j, i) for i, j in up]
    before = lax.ppermute(last, axis, up)
    after = lax.ppermute(first, axis, down)
    return before, after


def edge(x, dim, start, stop):
    return lax.slice_in_dim(x, start, stop, axis=dim)


def grid_sum(x):
    axes = ("gz", "gy")
    total = lax.axis_size("gz") * lax.axis_size("gy")
    if total & (total - 1):
        return lax.psum(x, axes)
    mask = 1
    while mask < total:
        one = lax.ppermute(x, axes, [(i, i ^ mask) for i in range(total)])
        if 2 * mask < total:
            two = lax.ppermute(x, axes, [(i, i ^ (2 * mask)) for i in range(total)])
            three = lax.ppermute(x, axes, [(i, i ^ (3 * mask)) for i in range(total)])
            x = (x + one) + (two + three)
        else:
            x = x + one
        mask *= 4
    return x


def tournament():
    players = list(range(BLOCK))
    rounds = []
    for _ in range(BLOCK - 1):
        rounds.append([(players[k], players[BLOCK - 1 - k]) for k in range(HALF)])
        players = [players[0], players[-1]] + players[1:-1]
    return rounds


def every_sublane(x):
    x = x + pltpu.roll(x, 4, 0)
    x = x + pltpu.roll(x, 2, 0)
    return x + pltpu.roll(x, 1, 0)


def small_kernel(gram_ref, stiff_ref, theta_ref, mix_ref):
    rows = lax.broadcasted_iota(jnp.int32, (BLOCK, LANES), 0)
    lanes = lax.broadcasted_iota(jnp.int32, (BLOCK, LANES), 1)
    unit = jnp.where(rows == lanes, 1.0, 0.0).astype(jnp.float32)
    pad = jnp.zeros((BLOCK, LANES - BLOCK), jnp.float32)
    work = jnp.concatenate([gram_ref[...], pad], axis=1)
    inverse = unit
    for k in range(BLOCK):
        pivot = work[k : k + 1, :]
        pivot_inverse = inverse[k : k + 1, :]
        scale = 1.0 / work[k : k + 1, k : k + 1]
        factor = jnp.where(rows[:, :1] > k, work[:, k : k + 1] * scale, 0.0)
        root = lax.sqrt(scale)
        work = work - factor * pivot
        inverse = inverse - factor * pivot_inverse
        inverse = jnp.where(rows == k, inverse * root, inverse)
    lower_inverse = inverse[:, :BLOCK]
    half_way = jnp.dot(
        lower_inverse, stiff_ref[...], precision=HIGHEST, preferred_element_type=jnp.float32
    )
    projected = lax.dot_general(
        half_way,
        lower_inverse,
        (((1,), (1,)), ((), ())),
        precision=HIGHEST,
        preferred_element_type=jnp.float32,
    )
    eye = unit[:, :BLOCK]
    mean = jnp.sum(jnp.sum(projected * eye, axis=1, keepdims=True), axis=0, keepdims=True) / BLOCK
    traceless = projected - mean * eye
    spread = jnp.sum(
        jnp.sum(traceless * traceless, axis=1, keepdims=True), axis=0, keepdims=True
    )
    scale = 1.25 * jnp.sqrt(spread) + 1e-30
    shifted = eye + traceless / scale

    upper = []
    lower = []
    for k in range(BLOCK):
        column = jnp.broadcast_to(shifted[:, k : k + 1], (BLOCK, LANES))
        upper.append(column[:8])
        lower.append(column[8:])

    def sweep(carry):
        count, _, upper, lower = carry
        upper, lower = list(upper), list(lower)
        norms = [
            every_sublane(upper[k] * upper[k] + lower[k] * lower[k]) for k in range(BLOCK)
        ]
        worst = jnp.zeros((8, LANES), jnp.float32)
        for pairs in tournament():
            for i, j in pairs:
                ui, uj, li, lj = upper[i], upper[j], lower[i], lower[j]
                g = every_sublane(ui * uj + li * lj)
                a, b = norms[i], norms[j]
                d = b - a
                g2 = g * g
                h2 = d * d + 4.0 * g2
                worst = jnp.maximum(worst, g2)
                live = h2 > 1e-28
                ih = lax.rsqrt(jnp.maximum(h2, 1e-28))
                positive = d >= 0.0
                dd = jnp.abs(d)
                c2 = jnp.where(live, 0.5 + 0.5 * dd * ih, 1.0)
                ic = lax.rsqrt(c2)
                c = c2 * ic
                signed = jnp.where(positive, g, -g)
                s = jnp.where(live, signed * ih * ic, 0.0)
                move = 0.5 * (h2 * ih - dd)
                move = jnp.where(positive, move, -move)
                upper[i] = c * ui - s * uj
                lower[i] = c * li - s * lj
                upper[j] = s * ui + c * uj
                lower[j] = s * li + c * lj
                norms[i] = a - move
                norms[j] = b + move
        return count + 1, jnp.max(worst), tuple(upper), tuple(lower)

    def unfinished(carry):
        count, worst, _, _ = carry
        return jnp.logical_and(count < MAX_SWEEPS, worst > 1e-8)

    _, _, upper, lower = lax.while_loop(
        unfinished, sweep, (jnp.int32(0), jnp.float32(1.0), tuple(upper), tuple(lower))
    )
    squares = [every_sublane(upper[k] * upper[k] + lower[k] * lower[k]) for k in range(BLOCK)]
    lane = lanes[:8]
    theta = jnp.zeros((8, LANES), jnp.float32)
    vectors_upper = jnp.zeros((8, LANES), jnp.float32)
    vectors_lower = jnp.zeros((8, LANES), jnp.float32)
    for k in range(BLOCK):
        rank = jnp.zeros((8, LANES), jnp.int32)
        for other in range(BLOCK):
            if other < k:
                rank = rank + jnp.where(squares[other] <= squares[k], 1, 0)
            elif other > k:
                rank = rank + jnp.where(squares[other] < squares[k], 1, 0)
        here = lane == rank
        inverse_norm = lax.rsqrt(squares[k])
        theta = jnp.where(here, squares[k] * inverse_norm, theta)
        vectors_upper = jnp.where(here, upper[k] * inverse_norm, vectors_upper)
        vectors_lower = jnp.where(here, lower[k] * inverse_norm, vectors_lower)
    theta_ref[...] = mean + scale * (theta - 1.0)
    vectors = jnp.concatenate([vectors_upper, vectors_lower], axis=0)
    mix_ref[...] = lax.dot_general(
        lower_inverse,
        vectors,
        (((0,), (0,)), ((), ())),
        precision=HIGHEST,
        preferred_element_type=jnp.float32,
    )


def ritz_pairs(gram, stiff):
    theta, mix = pl.pallas_call(
        small_kernel,
        out_shape=(
            jax.ShapeDtypeStruct((8, LANES), jnp.float32),
            jax.ShapeDtypeStruct((BLOCK, LANES), jnp.float32),
        ),
        in_specs=[pl.BlockSpec(memory_space=pltpu.VMEM)] * 2,
        out_specs=[pl.BlockSpec(memory_space=pltpu.VMEM)] * 2,
        name="ritz_pairs",
    )(gram, stiff)
    return theta[0, :MODES], mix[:, :MODES]


def difference(before, x, after, dim):
    length = x.shape[dim]
    padded = jnp.concatenate([before, x, after], axis=dim)
    return edge(padded, dim, 2, 2 + length) + edge(padded, dim, 0, length) - 2.0 * x


def x_difference(field):
    axis = field.ndim - 1
    return jnp.roll(field, -1, axis) + jnp.roll(field, 1, axis) - 2.0 * field


def weighted_gram(block, near, curvature, stiffness):
    (z_before, z_after), (y_before, y_after) = near
    terms = [
        (block, curvature),
        (difference(z_before, block, z_after, 1), stiffness),
        (difference(y_before, block, y_after, 2), stiffness),
        (x_difference(block), stiffness),
    ]
    total = 0.0
    for field, weight in terms:
        total = total + jnp.einsum("azyx,bzyx->ab", field * weight, field, precision=HIGHEST)
    return total


def hessian(block, near, far, curvature, stiffness, stiff_near):
    total = curvature * block + x_difference(stiffness * x_difference(block))
    for axis in (0, 1):
        dim = axis + 1
        before, after = near[axis]
        far_before, far_after = far[axis]
        rim_before, rim_after = stiff_near[axis]
        wide = jnp.concatenate([before, block, after], axis=dim)
        weights = jnp.concatenate([rim_before, stiffness, rim_after], axis=axis)
        flux = weights * difference(far_before, wide, far_after, dim)
        length = block.shape[dim]
        total = total + (
            edge(flux, dim, 2, 2 + length)
            + edge(flux, dim, 0, length)
            - 2.0 * edge(flux, dim, 1, 1 + length)
        )
    return total


def near_layers(block):
    nz, ny = block.shape[1], block.shape[2]
    return (
        neighbour_layers(block, "gz", 1, edge(block, 1, 0, 1), edge(block, 1, nz - 1, nz)),
        neighbour_layers(block, "gy", 2, edge(block, 2, 0, 1), edge(block, 2, ny - 1, ny)),
    )


def far_layers(block):
    nz, ny = block.shape[1], block.shape[2]
    return (
        neighbour_layers(block, "gz", 1, edge(block, 1, 1, 2), edge(block, 1, nz - 2, nz - 1)),
        neighbour_layers(block, "gy", 2, edge(block, 2, 1, 2), edge(block, 2, ny - 2, ny - 1)),
    )


def combine(mix, block):
    return jnp.einsum("azyx,aj->jzyx", block, mix, precision=HIGHEST)


def combine_pairs(mix, pairs):
    return tuple(tuple(combine(mix, part) for part in pair) for pair in pairs)


def local(initial_block, concentration, stiffness):
    nz, ny, nx = concentration.shape
    curvature = 3.0 * concentration * concentration - 1.0
    cells_total = nz * ny * nx * lax.axis_size("gz") * lax.axis_size("gy")
    scale_factor = jnp.float32(cells_total / MODES)

    near = near_layers(initial_block)
    held, near = lax.optimization_barrier((initial_block, near))
    far = far_layers(held)
    stiff_near = (
        neighbour_layers(stiffness, "gz", 0, stiffness[:1], stiffness[nz - 1 :]),
        neighbour_layers(stiffness, "gy", 1, stiffness[:, :1], stiffness[:, ny - 1 :]),
    )
    precondition = curvature + 2.0
    for axis in (0, 1):
        before, after = stiff_near[axis]
        wide = jnp.concatenate([before, stiffness, after], axis=axis)
        length = stiffness.shape[axis]
        precondition = precondition + (
            edge(wide, axis, 2, 2 + length) + edge(wide, axis, 0, length) + 4.0 * stiffness
        )
    precondition = precondition + (
        jnp.roll(stiffness, -1, 2) + jnp.roll(stiffness, 1, 2) + 4.0 * stiffness
    )

    gram = jnp.einsum("azyx,bzyx->ab", initial_block, initial_block, precision=HIGHEST)
    stiff = weighted_gram(initial_block, near, curvature, stiffness)
    sums = grid_sum(jnp.concatenate([gram, stiff], axis=1))
    theta, mix = ritz_pairs(sums[:, :BLOCK], sums[:, BLOCK:])

    modes = combine(mix, initial_block)
    mode_images = hessian(
        modes, combine_pairs(mix, near), combine_pairs(mix, far), curvature, stiffness, stiff_near
    )
    residuals = mode_images - theta[:, None, None, None] * modes
    corrections = residuals / precondition
    search = jnp.concatenate([modes, corrections], axis=0)

    near = near_layers(corrections)
    held, near = lax.optimization_barrier((corrections, near))
    far = far_layers(held)
    gram = jnp.einsum("azyx,bzyx->ab", search, search, precision=HIGHEST)
    cross = jnp.einsum("azyx,bzyx->ab", mode_images, search, precision=HIGHEST)
    low = weighted_gram(corrections, near, curvature, stiffness)
    stiff = jnp.concatenate(
        [cross, jnp.concatenate([cross[:, MODES:].T, low], axis=1)], axis=0
    )
    sums = grid_sum(jnp.concatenate([gram, stiff], axis=1))
    theta, mix = ritz_pairs(sums[:, :BLOCK], sums[:, BLOCK:])

    correction_images = hessian(corrections, near, far, curvature, stiffness, stiff_near)
    images = jnp.concatenate([mode_images, correction_images], axis=0)
    modes = combine(mix, search)
    residuals = combine(mix, images) - theta[:, None, None, None] * modes
    mode_density = scale_factor * jnp.sum(modes * modes, axis=0)
    residual_density = scale_factor * jnp.sum(residuals * residuals, axis=0)
    return (theta, mode_density, residual_density)


def solution(mesh):
    return jax.shard_map(
        local,
        mesh=mesh,
        in_specs=(P("img", "gz", "gy", None), P(("img", "gz"), "gy", None), P("gz", "gy", None)),
        out_specs=(P("img"), P(("img", "gz"), "gy", None), P(("img", "gz"), "gy", None)),
        check_vma=False,
    )
```

```python
import functools

import jax
import jax.numpy as jnp
from jax import lax
from jax.experimental import pallas as pl
from jax.experimental.pallas import tpu as pltpu
from jax.sharding import PartitionSpec as P

BLOCK = 16
MODES = 8
HALF = BLOCK // 2
LANES = 128
MAX_SWEEPS = 14
HIGHEST = lax.Precision.HIGHEST
VMEM = pl.BlockSpec(memory_space=pltpu.VMEM)


def call(kernel, out_shapes, args, scratch=(), flops=1000000, name=None):
    out_shape = tuple(jax.ShapeDtypeStruct(s, jnp.float32) for s in out_shapes)
    moved = 4 * sum(x.size for x in list(args) + list(out_shape))
    return pl.pallas_call(
        kernel,
        out_shape=out_shape,
        in_specs=[VMEM] * len(args),
        out_specs=[VMEM] * len(out_shape),
        scratch_shapes=list(scratch),
        compiler_params=pltpu.CompilerParams(vmem_limit_bytes=40 * 1024 * 1024),
        cost_estimate=pl.CostEstimate(flops=flops, bytes_accessed=moved, transcendentals=0),
        name=name,
    )(*args)


def from_next(x):
    size = lax.axis_size("gz")
    return lax.ppermute(x, "gz", [((i + 1) % size, i) for i in range(size)])


def from_previous(x):
    size = lax.axis_size("gz")
    return lax.ppermute(x, "gz", [(i, (i + 1) % size) for i in range(size)])


def edge(x, dim, start, stop):
    return lax.slice_in_dim(x, start, stop, axis=dim)


def rows_beside(x, dim):
    size = lax.axis_size("gy")
    length = x.shape[dim]
    first = edge(x, dim, 0, 2)
    last = edge(x, dim, length - 2, length)
    if size == 2:
        rows = jnp.concatenate([last, first], axis=dim)
        return lax.ppermute(rows, "gy", [(0, 1), (1, 0)])
    before = lax.ppermute(last, "gy", [(i, (i + 1) % size) for i in range(size)])
    after = lax.ppermute(first, "gy", [((i + 1) % size, i) for i in range(size)])
    return jnp.concatenate([before, after], axis=dim)


def all_terms(copies):
    return lax.all_to_all(copies, ("gz", "gy"), 0, 0, tiled=True)


def spread_rows(x, k):
    return jnp.broadcast_to(x[k : k + 1, :], (8, LANES))


def every_row(x):
    x = x + pltpu.roll(x, 4, 0)
    x = x + pltpu.roll(x, 2, 0)
    return x + pltpu.roll(x, 1, 0)


def packed_sums(tiles, row):
    low4, low2, low1 = row < 4, (row & 2) == 0, (row & 1) == 0
    tiles = [
        jnp.where(low4, tiles[k], tiles[k + 4])
        + pltpu.roll(jnp.where(low4, tiles[k + 4], tiles[k]), 4, 0)
        for k in range(4)
    ]

    def fold(a, b, low, step):
        other = jnp.where(low, b, a)
        moved = jnp.where(low, pltpu.roll(other, 8 - step, 0), pltpu.roll(other, step, 0))
        return jnp.where(low, a, b) + moved

    tiles = [fold(tiles[k], tiles[k + 2], low2, 2) for k in range(2)]
    return fold(tiles[0], tiles[1], low1, 1)


def tournament():
    players = list(range(BLOCK))
    rounds = []
    for _ in range(BLOCK - 1):
        rounds.append([(players[k], players[BLOCK - 1 - k]) for k in range(HALF)])
        players = [players[0], players[-1]] + players[1:-1]
    return rounds


def ritz_kernel(terms_ref, theta_ref, theta_rows_ref, mix_ref):
    tiles = [terms_ref[k : k + 8, :] for k in range(0, terms_ref.shape[0], 8)]
    while len(tiles) > 1:
        tiles = [sum(tiles[k : k + 2]) for k in range(0, len(tiles), 2)]
    total = tiles[0]
    row = lax.broadcasted_iota(jnp.int32, (8, LANES), 0)
    lane = lax.broadcasted_iota(jnp.int32, (8, LANES), 1)

    def columns(upper, lower):
        return (
            [jnp.broadcast_to(upper[:, k : k + 1], (8, LANES)) for k in range(BLOCK)],
            [jnp.broadcast_to(lower[:, k : k + 1], (8, LANES)) for k in range(BLOCK)],
        )

    def entry(upper, lower, k):
        return spread_rows(upper, k) if k < 8 else spread_rows(lower, k - 8)

    gram_u, gram_l = columns(total[:, :BLOCK], total[:, BLOCK : 2 * BLOCK])
    zero = jnp.zeros((8, LANES), jnp.float32)
    inverse_u = [jnp.where(row == k, 1.0, 0.0).astype(jnp.float32) for k in range(8)] + [zero] * 8
    inverse_l = [zero] * 8 + [
        jnp.where(row == k, 1.0, 0.0).astype(jnp.float32) for k in range(8)
    ]
    for k in range(BLOCK):
        root = lax.rsqrt(entry(gram_u[k], gram_l[k], k))
        gram_u[k] = gram_u[k] * root
        gram_l[k] = gram_l[k] * root
        inverse_u[k] = inverse_u[k] * root
        inverse_l[k] = inverse_l[k] * root
        for i in range(k + 1, BLOCK):
            factor = entry(gram_u[k], gram_l[k], i)
            if i < 8:
                gram_u[i] = gram_u[i] - factor * gram_u[k]
            gram_l[i] = gram_l[i] - factor * gram_l[k]
            inverse_u[i] = inverse_u[i] - factor * inverse_u[k]
            if k >= 8:
                inverse_l[i] = inverse_l[i] - factor * inverse_l[k]
    transposed_u, transposed_l = zero, zero
    for k in range(BLOCK):
        transposed_u = jnp.where(lane == k, inverse_u[k], transposed_u)
        transposed_l = jnp.where(lane == k, inverse_l[k], transposed_l)
    transposed = jnp.concatenate([transposed_u, transposed_l], axis=0)[:, :BLOCK]

    dot = functools.partial(
        lax.dot_general, precision=HIGHEST, preferred_element_type=jnp.float32
    )
    stiff = jnp.concatenate(
        [total[:, 2 * BLOCK : 3 * BLOCK], total[:, 3 * BLOCK : 4 * BLOCK]], axis=0
    )
    half_way = dot(stiff, transposed, (((1,), (0,)), ((), ())))
    projected = dot(transposed, half_way, (((0,), (0,)), ((), ())))

    upper, lower = columns(projected[:8], projected[8:])
    diagonal = zero
    for k in range(8):
        diagonal = diagonal + jnp.where(row == k, upper[k] + lower[k + 8], 0.0)
    mean = every_row(diagonal) * (1.0 / BLOCK)
    size = zero
    for k in range(8):
        upper[k] = upper[k] - jnp.where(row == k, mean, 0.0)
        lower[k + 8] = lower[k + 8] - jnp.where(row == k, mean, 0.0)
    for k in range(BLOCK):
        size = size + (upper[k] * upper[k] + lower[k] * lower[k])
    scale = 1.25 * jnp.sqrt(every_row(size)) + 1e-30
    shrink = 1.0 / scale
    for k in range(BLOCK):
        upper[k] = upper[k] * shrink
        lower[k] = lower[k] * shrink
    for k in range(8):
        upper[k] = upper[k] + jnp.where(row == k, 1.0, 0.0)
        lower[k + 8] = lower[k + 8] + jnp.where(row == k, 1.0, 0.0)

    def squares(upper, lower):
        top = packed_sums([upper[k] * upper[k] + lower[k] * lower[k] for k in range(8)], row)
        bottom = packed_sums(
            [upper[15 - k] * upper[15 - k] + lower[15 - k] * lower[15 - k] for k in range(8)], row
        )
        return top, bottom

    def sweep(carry):
        count, _, upper, lower = carry
        upper, lower = list(upper), list(lower)
        top, bottom = squares(upper, lower)
        worst = zero
        for pairs in tournament():
            g = packed_sums([upper[i] * upper[j] + lower[i] * lower[j] for i, j in pairs], row)
            d = bottom - top
            g2 = g * g
            worst = jnp.maximum(worst, g2)
            dd = jnp.maximum(jnp.abs(d), 1e-18)
            ih = lax.rsqrt(dd * dd + 4.0 * g2)
            c2 = 0.5 + (0.5 * dd) * ih
            ic = lax.rsqrt(c2)
            c = c2 * ic
            s = jnp.where(d >= 0.0, g, -g) * (ih * ic)
            move = (s * ic) * g
            top = top - move
            bottom = bottom + move
            for k, (i, j) in enumerate(pairs):
                ck, sk = spread_rows(c, k), spread_rows(s, k)
                ui, uj, li, lj = upper[i], upper[j], lower[i], lower[j]
                upper[i] = ck * ui - sk * uj
                lower[i] = ck * li - sk * lj
                upper[j] = sk * ui + ck * uj
                lower[j] = sk * li + ck * lj
            next_top = jnp.where(
                row == 0, top, jnp.where(row == 1, pltpu.roll(bottom, 1, 0), pltpu.roll(top, 1, 0))
            )
            bottom = jnp.where(row == 7, top, pltpu.roll(bottom, 7, 0))
            top = next_top
        return count + 1, jnp.max(worst), tuple(upper), tuple(lower)

    def unfinished(carry):
        count, worst, _, _ = carry
        return jnp.logical_and(count < MAX_SWEEPS, worst > 1e-8)

    _, _, upper, lower = lax.while_loop(
        unfinished, sweep, (jnp.int32(0), jnp.float32(1.0), tuple(upper), tuple(lower))
    )

    top, bottom = squares(upper, lower)
    rank_top, rank_bottom = zero, zero
    for k in range(BLOCK):
        mine = spread_rows(top, k) if k < 8 else spread_rows(bottom, 15 - k)
        before_top = (mine < top) | ((mine == top) & (k < row))
        before_bottom = (mine < bottom) | ((mine == bottom) & (k < 15 - row))
        rank_top = rank_top + jnp.where(before_top, 1.0, 0.0)
        rank_bottom = rank_bottom + jnp.where(before_bottom, 1.0, 0.0)
    inverse_top, inverse_bottom = lax.rsqrt(top), lax.rsqrt(bottom)
    value_top, value_bottom = top * inverse_top, bottom * inverse_bottom
    lane_float = lane.astype(jnp.float32)
    theta = zero
    vectors_u, vectors_l = zero, zero
    for k in range(BLOCK):

        def of(first, second):
            return spread_rows(first, k) if k < 8 else spread_rows(second, 15 - k)

        here = lane_float == of(rank_top, rank_bottom)
        inverse_norm = of(inverse_top, inverse_bottom)
        theta = jnp.where(here, of(value_top, value_bottom), theta)
        vectors_u = jnp.where(here, upper[k] * inverse_norm, vectors_u)
        vectors_l = jnp.where(here, lower[k] * inverse_norm, vectors_l)
    theta = mean + scale * (theta - 1.0)
    theta_ref[...] = theta
    on_row = jnp.sum(jnp.where(row == lane, theta, 0.0), axis=1, keepdims=True)
    theta_rows_ref[...] = jnp.broadcast_to(on_row, (8, LANES))
    vectors = jnp.concatenate([vectors_u, vectors_l], axis=0)
    mix = dot(transposed, vectors, (((1,), (0,)), ((), ())))
    for j in range(MODES):
        mix_ref[j] = jnp.broadcast_to(mix[:, j : j + 1], (BLOCK, LANES))


def ritz_pairs(terms):
    return call(
        ritz_kernel,
        [(8, LANES), (8, LANES), (MODES, BLOCK, LANES)],
        [terms],
        flops=10000000,
        name="ritz_pairs",
    )


def inner(a, b):
    return lax.dot_general(
        a, b, (((1,), (1,)), ((), ())), precision=HIGHEST, preferred_element_type=jnp.float32
    )


def folded(products, offset):
    height, width = products.shape
    row = lax.broadcasted_iota(jnp.int32, (height, width), 0)
    column = lax.broadcasted_iota(jnp.int32, (height, width), 1)
    same = jnp.where((row & 7) == (column & 7), products, 0.0)
    sums = jnp.sum(same.reshape(height // 8, 8, width), axis=1)
    row = lax.broadcasted_iota(jnp.int32, (width, LANES), 0)
    lane = lax.broadcasted_iota(jnp.int32, (width, LANES), 1)
    place = jnp.where((row >> 3) + offset == lane, 1.0, 0.0).astype(jnp.float32)
    return jnp.dot(sums, place, precision=HIGHEST, preferred_element_type=jnp.float32)


def rows_of(x):
    return x.reshape(x.shape[0] * x.shape[1], x.shape[2])


def store_y_differences(source_ref, beside_ref, wide_ref, change_ref, z):
    count, _, ny, _ = source_ref.shape

    @pl.loop(0, count)
    def _(a):
        wide_ref[6:8, :] = beside_ref[a, z, :2]
        wide_ref[8 : 8 + ny, :] = source_ref[a, z]
        wide_ref[8 + ny : 10 + ny, :] = beside_ref[a, z, 2:]
        wide = wide_ref[...]
        change = roll(wide, -1, 0) + roll(wide, 1, 0) - 2.0 * wide
        change_ref[a] = change[8 : 8 + ny]


def plane_stiff(field, change, curvature, stiffness):
    rows = rows_of(field)
    along_x = roll(rows, -1, 1) + roll(rows, 1, 1) - 2.0 * rows
    weight = jnp.broadcast_to(stiffness[None], field.shape)
    weight = rows_of(weight)
    along_y = rows_of(change)
    bent = rows_of(field * curvature[None])
    return inner(bent, rows) + inner(along_x * weight, along_x) + inner(along_y * weight, along_y)


def first_local_kernel(block_ref, beside_ref, curvature_ref, stiffness_ref, tile_ref, wide_ref, change_ref):
    nz, ny, nx = curvature_ref.shape
    wide_ref[...] = jnp.zeros(wide_ref.shape, jnp.float32)
    gram = jnp.zeros((8 * BLOCK, 8 * BLOCK), jnp.float32)
    stiff = jnp.zeros((8 * BLOCK, 8 * BLOCK), jnp.float32)
    for z in range(nz):
        store_y_differences(block_ref, beside_ref, wide_ref, change_ref, z)
        for start in range(0, ny, 8):
            part = slice(start, start + 8)
            field = block_ref[:, z, part, :]
            rows = rows_of(field)
            gram = gram + inner(rows, rows)
            stiff = stiff + plane_stiff(
                field, change_ref[:, part, :], curvature_ref[z, part, :], stiffness_ref[z, part, :]
            )
    half = 8 * HALF
    tile_ref[...] = (
        folded(gram[:half], 0)
        + folded(gram[half:], BLOCK)
        + folded(stiff[:half], 2 * BLOCK)
        + folded(stiff[half:], 3 * BLOCK)
    )


def first_local(block, beside, curvature, stiffness):
    nz, ny, nx = curvature.shape
    (tile,) = call(
        first_local_kernel,
        [(8, LANES)],
        [block, beside, curvature, stiffness],
        scratch=[
            pltpu.VMEM((ny + 16, nx), jnp.float32),
            pltpu.VMEM((BLOCK, ny, nx), jnp.float32),
        ],
        flops=100000000,
        name="first_local",
    )
    return tile


def second_local_kernel(
    modes_ref, images_ref, corrections_ref, beside_ref, curvature_ref, stiffness_ref,
    tile_ref, wide_ref, change_ref,
):
    nz, ny, nx = curvature_ref.shape
    wide_ref[...] = jnp.zeros(wide_ref.shape, jnp.float32)
    half = 8 * HALF
    gram = jnp.zeros((2 * half, 2 * half), jnp.float32)
    cross = jnp.zeros((half, 2 * half), jnp.float32)
    back = jnp.zeros((half, half), jnp.float32)
    low = jnp.zeros((half, half), jnp.float32)
    for z in range(nz):
        store_y_differences(corrections_ref, beside_ref, wide_ref, change_ref, z)
        for start in range(0, ny, 8):
            part = slice(start, start + 8)
            field = corrections_ref[:, z, part, :]
            second = rows_of(field)
            rows = jnp.concatenate([rows_of(modes_ref[:, z, part, :]), second], axis=0)
            images = rows_of(images_ref[:, z, part, :])
            gram = gram + inner(rows, rows)
            cross = cross + inner(images, rows)
            back = back + inner(second, images)
            low = low + plane_stiff(
                field, change_ref[:, part, :], curvature_ref[z, part, :], stiffness_ref[z, part, :]
            )
    tile_ref[...] = (
        folded(gram[:half], 0)
        + folded(gram[half:], BLOCK)
        + folded(cross, 2 * BLOCK)
        + (folded(back, 3 * BLOCK) + folded(low, 3 * BLOCK + HALF))
    )


def second_local(modes, images, corrections, beside, curvature, stiffness):
    nz, ny, nx = curvature.shape
    (tile,) = call(
        second_local_kernel,
        [(8, LANES)],
        [modes, images, corrections, beside, curvature, stiffness],
        scratch=[
            pltpu.VMEM((ny + 16, nx), jnp.float32),
            pltpu.VMEM((HALF, ny, nx), jnp.float32),
        ],
        flops=80000000,
        name="second_local",
    )
    return tile


def across_kernel(block_ref, after_ref, layers_ref, tile_ref, copies_ref):
    count, nz, ny, nx = block_ref.shape
    half = 8 * HALF
    stiff = jnp.zeros((8 * count, 8 * count), jnp.float32)

    def layer(k, part):
        return block_ref[:, k, part, :] if k < nz else after_ref[:, k - nz, part, :]

    for z in range(1, nz + 1):
        for start in range(0, ny, 8):
            part = slice(start, start + 8)
            change = (layer(z + 1, part) + layer(z - 1, part)) - 2.0 * layer(z, part)
            weight = layers_ref[z + 1, part, :]
            stiff = stiff + inner(rows_of(change * weight[None]), rows_of(change))
    tile = tile_ref[...]
    if count == BLOCK:
        tile = tile + folded(stiff[:half], 2 * BLOCK) + folded(stiff[half:], 3 * BLOCK)
    else:
        tile = tile + folded(stiff, 3 * BLOCK + HALF)
    for k in range(0, copies_ref.shape[0], 8):
        copies_ref[k : k + 8, :] = tile


def across(block, after, layers, tile):
    total = lax.axis_size("gz") * lax.axis_size("gy")
    (copies,) = call(
        across_kernel,
        [(8 * total, LANES)],
        [block, after, layers, tile],
        flops=25000000,
        name="across",
    )
    return copies


def roll(x, shift, axis):
    return pltpu.roll(x, shift % x.shape[axis], axis)


def apply_hessian(before, own, after, wide, curvature, stiff_layers, stiff_wide, layer):
    layers = before[-2:] + own + after[:2]

    def flux(k):
        middle = layers[k + 2]
        return stiff_layers(k + 1) * ((layers[k + 3] + layers[k + 1]) - 2.0 * middle)

    field = own[layer]
    total = curvature * field + (flux(layer + 1) + flux(layer - 1) - 2.0 * flux(layer))
    change = roll(field, -1, 1) + roll(field, 1, 1) - 2.0 * field
    change = stiff_layers(layer + 1) * change
    total = total + (roll(change, -1, 1) + roll(change, 1, 1) - 2.0 * change)
    change = stiff_wide * (roll(wide, -1, 0) + roll(wide, 1, 0) - 2.0 * wide)
    change = roll(change, -1, 0) + roll(change, 1, 0) - 2.0 * change
    rows = field.shape[0]
    return total + change[8 : 8 + rows]


def update_kernel(
    mix_ref, theta_ref, block_ref, before_ref, after_ref, beside_ref,
    curvature_ref, inverse_ref, stiff_layers_ref, stiff_wide_ref,
    modes_ref, images_ref, corrections_ref, layers_ref, wide_ref,
):
    nz, ny, nx = curvature_ref.shape
    wide_ref[...] = jnp.zeros(wide_ref.shape, jnp.float32)
    for source, offset in ((before_ref, 0), (block_ref, nz), (after_ref, 2 * nz)):

        @pl.loop(0, nz)
        def _(z, source=source, offset=offset):
            for start in range(0, nx, LANES):
                lanes = slice(start, start + LANES)
                parts = [source[a, z, :, lanes] for a in range(BLOCK)]
                for j in range(MODES):
                    mixed = mix_ref[j, 0:1, :] * parts[0]
                    for a in range(1, BLOCK):
                        mixed = mixed + mix_ref[j, a : a + 1, :] * parts[a]
                    layers_ref[j, offset + z, :, lanes] = mixed
                    if source is block_ref:
                        wide_ref[j, z, 8 : 8 + ny, lanes] = mixed

    @pl.loop(0, nz)
    def _(z):
        for start in range(0, nx, LANES):
            lanes = slice(start, start + LANES)
            parts = [beside_ref[a, z, :, lanes] for a in range(BLOCK)]
            for j in range(MODES):
                mixed = mix_ref[j, 0:1, :] * parts[0]
                for a in range(1, BLOCK):
                    mixed = mixed + mix_ref[j, a : a + 1, :] * parts[a]
                wide_ref[j, z, 6:8, lanes] = mixed[:2]
                wide_ref[j, z, 8 + ny : 10 + ny, lanes] = mixed[2:]

    @pl.loop(0, MODES)
    def _(j):
        layers = [layers_ref[j, k] for k in range(3 * nz)]
        theta = jnp.broadcast_to(theta_ref[pl.ds(j, 1), :1], (1, nx))
        for z in range(nz):
            image = apply_hessian(
                layers[:nz], layers[nz : 2 * nz], layers[2 * nz :], wide_ref[j, z],
                curvature_ref[z], lambda k: stiff_layers_ref[k], stiff_wide_ref[z], z,
            )
            mode = layers[nz + z]
            images_ref[j, z] = image
            modes_ref[j, z] = mode
            corrections_ref[j, z] = (image - theta * mode) * inverse_ref[z]


def update(mix, theta_rows, block, before, after, beside, fields):
    curvature, inverse, stiff_layers, stiff_wide = fields
    nz, ny, nx = curvature.shape
    return call(
        update_kernel,
        [(MODES, nz, ny, nx)] * 3,
        [mix, theta_rows, block, before, after, beside, curvature, inverse, stiff_layers, stiff_wide],
        scratch=[
            pltpu.VMEM((MODES, 3 * nz, ny, nx), jnp.float32),
            pltpu.VMEM((MODES, nz, ny + 16, nx), jnp.float32),
        ],
        name="update",
    )


def images_kernel(
    block_ref, before_ref, after_ref, beside_ref,
    curvature_ref, stiff_layers_ref, stiff_wide_ref, images_ref, wide_ref,
):
    nz, ny, nx = curvature_ref.shape
    wide_ref[...] = jnp.zeros(wide_ref.shape, jnp.float32)

    @pl.loop(0, MODES)
    def _(j):
        for z in range(nz):
            wide_ref[z, 6:8, :] = beside_ref[j, z, :2]
            wide_ref[z, 8 : 8 + ny, :] = block_ref[j, z]
            wide_ref[z, 8 + ny : 10 + ny, :] = beside_ref[j, z, 2:]
        before = [before_ref[j, z] for z in range(nz)]
        own = [block_ref[j, z] for z in range(nz)]
        after = [after_ref[j, z] for z in range(nz)]
        for z in range(nz):
            images_ref[j, z] = apply_hessian(
                before, own, after, wide_ref[z],
                curvature_ref[z], lambda k: stiff_layers_ref[k], stiff_wide_ref[z], z,
            )


def images_of(block, before, after, beside, fields):
    curvature, _, stiff_layers, stiff_wide = fields
    nz, ny, nx = curvature.shape
    (images,) = call(
        images_kernel,
        [(MODES, nz, ny, nx)],
        [block, before, after, beside, curvature, stiff_layers, stiff_wide],
        scratch=[pltpu.VMEM((nz, ny + 16, nx), jnp.float32)],
        name="images",
    )
    return images


def density_kernel(
    factor, mix_ref, theta_ref, modes_ref, corrections_ref, first_ref, second_ref,
    mode_density_ref, residual_density_ref,
):
    nz, ny, nx = mode_density_ref.shape

    @pl.loop(0, nz)
    def _(z):
        for start in range(0, nx, LANES):
            lanes = slice(start, start + LANES)
            vectors = [modes_ref[a, z, :, lanes] for a in range(MODES)]
            vectors = vectors + [corrections_ref[a, z, :, lanes] for a in range(MODES)]
            images = [first_ref[a, z, :, lanes] for a in range(MODES)]
            images = images + [second_ref[a, z, :, lanes] for a in range(MODES)]
            mode_sum = jnp.zeros((ny, LANES), jnp.float32)
            residual_sum = jnp.zeros((ny, LANES), jnp.float32)
            for j in range(MODES):
                mode = mix_ref[j, 0:1, :] * vectors[0]
                image = mix_ref[j, 0:1, :] * images[0]
                for a in range(1, BLOCK):
                    mode = mode + mix_ref[j, a : a + 1, :] * vectors[a]
                    image = image + mix_ref[j, a : a + 1, :] * images[a]
                residual = image - theta_ref[j : j + 1, :] * mode
                mode_sum = mode_sum + mode * mode
                residual_sum = residual_sum + residual * residual
            mode_density_ref[z, :, lanes] = factor * mode_sum
            residual_density_ref[z, :, lanes] = factor * residual_sum


def densities(factor, mix, theta_rows, modes, corrections, first, second):
    shape = modes.shape[1:]
    return call(
        functools.partial(density_kernel, factor),
        [shape, shape],
        [mix, theta_rows, modes, corrections, first, second],
        name="densities",
    )


def local(initial_block, concentration, stiffness):
    nz, ny, nx = concentration.shape
    cells_total = nz * ny * nx * lax.axis_size("gz") * lax.axis_size("gy")
    curvature = 3.0 * concentration * concentration - 1.0

    after = from_next(initial_block)
    beside = rows_beside(initial_block, 2)
    tile = first_local(initial_block, beside, curvature, stiffness)

    late, tile = lax.optimization_barrier((stiffness, tile))
    next_stiffness = from_next(late)
    previous_stiffness = from_previous(late)
    beside_stiffness = rows_beside(late, 1)
    layers = jnp.concatenate([previous_stiffness[nz - 1 :], stiffness, next_stiffness[:1]], axis=0)
    blank = jnp.zeros((nz, 6, nx), jnp.float32)
    wide = jnp.concatenate(
        [blank, beside_stiffness[:, :2], stiffness, beside_stiffness[:, 2:], blank], axis=1
    )
    precondition = (curvature + 2.0) + 12.0 * stiffness
    precondition = precondition + (layers[2:] + layers[:-2])
    precondition = precondition + (wide[:, 9 : 9 + ny] + wide[:, 7 : 7 + ny])
    precondition = precondition + (jnp.roll(stiffness, -1, 2) + jnp.roll(stiffness, 1, 2))
    fields = (curvature, 1.0 / precondition, layers, wide)

    held, after, tile, fields = lax.optimization_barrier((initial_block, after, tile, fields))
    layers = fields[2]
    before = from_previous(held)
    terms = all_terms(across(initial_block, after, layers, tile))
    _, theta_rows, mix = ritz_pairs(terms)
    modes, mode_images, corrections = update(
        mix, theta_rows, initial_block, before, after, beside, fields
    )

    after = from_next(corrections)
    beside = rows_beside(corrections, 2)
    tile = second_local(modes, mode_images, corrections, beside, curvature, stiffness)
    held, after, tile = lax.optimization_barrier((corrections, after, tile))
    before = from_previous(held)
    terms = all_terms(across(corrections, after, layers, tile))
    theta, theta_rows, mix = ritz_pairs(terms)
    correction_images = images_of(corrections, before, after, beside, fields)
    mode_density, residual_density = densities(
        float(cells_total / MODES), mix, theta_rows, modes, corrections, mode_images, correction_images
    )
    return (theta[0, :MODES], mode_density, residual_density)


def solution(mesh):
    return jax.shard_map(
        local,
        mesh=mesh,
        in_specs=(P("img", "gz", "gy", None), P(("img", "gz"), "gy", None), P("gz", "gy", None)),
        out_specs=(P("img"), P(("img", "gz"), "gy", None), P(("img", "gz"), "gy", None)),
        check_vma=False,
    )
```

```python
import functools

import jax
import jax.numpy as jnp
from jax import lax
from jax.experimental import pallas as pl
from jax.experimental.pallas import tpu as pltpu
from jax.sharding import PartitionSpec as P

BLOCK = 16
MODES = 8
HALF = BLOCK // 2
LANES = 128
MAX_SWEEPS = 14
HIGHEST = lax.Precision.HIGHEST
VMEM = pl.BlockSpec(memory_space=pltpu.VMEM)


def call(kernel, out_shapes, args, scratch=(), flops=1000000, name=None):
    out_shape = tuple(jax.ShapeDtypeStruct(s, jnp.float32) for s in out_shapes)
    moved = 4 * sum(x.size for x in list(args) + list(out_shape))
    return pl.pallas_call(
        kernel,
        out_shape=out_shape,
        in_specs=[VMEM] * len(args),
        out_specs=[VMEM] * len(out_shape),
        scratch_shapes=list(scratch),
        compiler_params=pltpu.CompilerParams(vmem_limit_bytes=40 * 1024 * 1024),
        cost_estimate=pl.CostEstimate(flops=flops, bytes_accessed=moved, transcendentals=0),
        name=name,
    )(*args)


def from_next(x):
    size = lax.axis_size("gz")
    return lax.ppermute(x, "gz", [((i + 1) % size, i) for i in range(size)])


def from_previous(x):
    size = lax.axis_size("gz")
    return lax.ppermute(x, "gz", [(i, (i + 1) % size) for i in range(size)])


def edge(x, dim, start, stop):
    return lax.slice_in_dim(x, start, stop, axis=dim)


def rows_beside(x, dim):
    size = lax.axis_size("gy")
    length = x.shape[dim]
    first = edge(x, dim, 0, 2)
    last = edge(x, dim, length - 2, length)
    if size == 2:
        rows = jnp.concatenate([last, first], axis=dim)
        return lax.ppermute(rows, "gy", [(0, 1), (1, 0)])
    before = lax.ppermute(last, "gy", [(i, (i + 1) % size) for i in range(size)])
    after = lax.ppermute(first, "gy", [((i + 1) % size, i) for i in range(size)])
    return jnp.concatenate([before, after], axis=dim)


def all_terms(copies):
    return lax.all_to_all(copies, ("gz", "gy"), 0, 0, tiled=True)


def spread_rows(x, k):
    return jnp.broadcast_to(x[k : k + 1, :], (8, LANES))


def every_row(x):
    x = x + pltpu.roll(x, 4, 0)
    x = x + pltpu.roll(x, 2, 0)
    return x + pltpu.roll(x, 1, 0)


def packed_sums(tiles, row):
    low4, low2, low1 = row < 4, (row & 2) == 0, (row & 1) == 0
    tiles = [
        jnp.where(low4, tiles[k], tiles[k + 4])
        + pltpu.roll(jnp.where(low4, tiles[k + 4], tiles[k]), 4, 0)
        for k in range(4)
    ]

    def fold(a, b, low, step):
        other = jnp.where(low, b, a)
        moved = jnp.where(low, pltpu.roll(other, 8 - step, 0), pltpu.roll(other, step, 0))
        return jnp.where(low, a, b) + moved

    tiles = [fold(tiles[k], tiles[k + 2], low2, 2) for k in range(2)]
    return fold(tiles[0], tiles[1], low1, 1)


def tournament():
    players = list(range(BLOCK))
    rounds = []
    for _ in range(BLOCK - 1):
        rounds.append([(players[k], players[BLOCK - 1 - k]) for k in range(HALF)])
        players = [players[0], players[-1]] + players[1:-1]
    return rounds


def ritz_kernel(terms_ref, theta_ref, theta_rows_ref, mix_ref):
    tiles = [terms_ref[k : k + 8, :] for k in range(0, terms_ref.shape[0], 8)]
    while len(tiles) > 1:
        tiles = [sum(tiles[k : k + 2]) for k in range(0, len(tiles), 2)]
    total = tiles[0]
    row = lax.broadcasted_iota(jnp.int32, (8, LANES), 0)
    lane = lax.broadcasted_iota(jnp.int32, (8, LANES), 1)

    def columns(upper, lower):
        return (
            [jnp.broadcast_to(upper[:, k : k + 1], (8, LANES)) for k in range(BLOCK)],
            [jnp.broadcast_to(lower[:, k : k + 1], (8, LANES)) for k in range(BLOCK)],
        )

    def entry(upper, lower, k):
        return spread_rows(upper, k) if k < 8 else spread_rows(lower, k - 8)

    gram_u, gram_l = columns(total[:, :BLOCK], total[:, BLOCK : 2 * BLOCK])
    zero = jnp.zeros((8, LANES), jnp.float32)
    inverse_u = [jnp.where(row == k, 1.0, 0.0).astype(jnp.float32) for k in range(8)] + [zero] * 8
    inverse_l = [zero] * 8 + [
        jnp.where(row == k, 1.0, 0.0).astype(jnp.float32) for k in range(8)
    ]
    for k in range(BLOCK):
        root = lax.rsqrt(entry(gram_u[k], gram_l[k], k))
        gram_u[k] = gram_u[k] * root
        gram_l[k] = gram_l[k] * root
        inverse_u[k] = inverse_u[k] * root
        inverse_l[k] = inverse_l[k] * root
        for i in range(k + 1, BLOCK):
            factor = entry(gram_u[k], gram_l[k], i)
            if i < 8:
                gram_u[i] = gram_u[i] - factor * gram_u[k]
            gram_l[i] = gram_l[i] - factor * gram_l[k]
            inverse_u[i] = inverse_u[i] - factor * inverse_u[k]
            if k >= 8:
                inverse_l[i] = inverse_l[i] - factor * inverse_l[k]
    transposed_u, transposed_l = zero, zero
    for k in range(BLOCK):
        transposed_u = jnp.where(lane == k, inverse_u[k], transposed_u)
        transposed_l = jnp.where(lane == k, inverse_l[k], transposed_l)
    transposed = jnp.concatenate([transposed_u, transposed_l], axis=0)[:, :BLOCK]

    dot = functools.partial(
        lax.dot_general, precision=HIGHEST, preferred_element_type=jnp.float32
    )
    stiff = jnp.concatenate(
        [total[:, 2 * BLOCK : 3 * BLOCK], total[:, 3 * BLOCK : 4 * BLOCK]], axis=0
    )
    half_way = dot(stiff, transposed, (((1,), (0,)), ((), ())))
    projected = dot(transposed, half_way, (((0,), (0,)), ((), ())))

    upper, lower = columns(projected[:8], projected[8:])
    diagonal = zero
    for k in range(8):
        diagonal = diagonal + jnp.where(row == k, upper[k] + lower[k + 8], 0.0)
    mean = every_row(diagonal) * (1.0 / BLOCK)
    size = zero
    for k in range(8):
        upper[k] = upper[k] - jnp.where(row == k, mean, 0.0)
        lower[k + 8] = lower[k + 8] - jnp.where(row == k, mean, 0.0)
    for k in range(BLOCK):
        size = size + (upper[k] * upper[k] + lower[k] * lower[k])
    scale = 1.25 * jnp.sqrt(every_row(size)) + 1e-30
    shrink = 1.0 / scale
    for k in range(BLOCK):
        upper[k] = upper[k] * shrink
        lower[k] = lower[k] * shrink
    for k in range(8):
        upper[k] = upper[k] + jnp.where(row == k, 1.0, 0.0)
        lower[k + 8] = lower[k + 8] + jnp.where(row == k, 1.0, 0.0)

    def squares(upper, lower):
        top = packed_sums([upper[k] * upper[k] + lower[k] * lower[k] for k in range(8)], row)
        bottom = packed_sums(
            [upper[15 - k] * upper[15 - k] + lower[15 - k] * lower[15 - k] for k in range(8)], row
        )
        return top, bottom

    def sweep(carry):
        count, _, upper, lower = carry
        upper, lower = list(upper), list(lower)
        top, bottom = squares(upper, lower)
        worst = zero
        for pairs in tournament():
            g = packed_sums([upper[i] * upper[j] + lower[i] * lower[j] for i, j in pairs], row)
            d = bottom - top
            g2 = g * g
            worst = jnp.maximum(worst, g2)
            dd = jnp.maximum(jnp.abs(d), 1e-18)
            ih = lax.rsqrt(dd * dd + 4.0 * g2)
            c2 = 0.5 + (0.5 * dd) * ih
            ic = lax.rsqrt(c2)
            c = c2 * ic
            s = jnp.where(d >= 0.0, g, -g) * (ih * ic)
            move = (s * ic) * g
            top = top - move
            bottom = bottom + move
            for k, (i, j) in enumerate(pairs):
                ck, sk = spread_rows(c, k), spread_rows(s, k)
                ui, uj, li, lj = upper[i], upper[j], lower[i], lower[j]
                upper[i] = ck * ui - sk * uj
                lower[i] = ck * li - sk * lj
                upper[j] = sk * ui + ck * uj
                lower[j] = sk * li + ck * lj
            next_top = jnp.where(
                row == 0, top, jnp.where(row == 1, pltpu.roll(bottom, 1, 0), pltpu.roll(top, 1, 0))
            )
            bottom = jnp.where(row == 7, top, pltpu.roll(bottom, 7, 0))
            top = next_top
        return count + 1, jnp.max(worst), tuple(upper), tuple(lower)

    def unfinished(carry):
        count, worst, _, _ = carry
        return jnp.logical_and(count < MAX_SWEEPS, worst > 1e-8)

    _, _, upper, lower = lax.while_loop(
        unfinished, sweep, (jnp.int32(0), jnp.float32(1.0), tuple(upper), tuple(lower))
    )

    top, bottom = squares(upper, lower)
    rank_top, rank_bottom = zero, zero
    for k in range(BLOCK):
        mine = spread_rows(top, k) if k < 8 else spread_rows(bottom, 15 - k)
        before_top = (mine < top) | ((mine == top) & (k < row))
        before_bottom = (mine < bottom) | ((mine == bottom) & (k < 15 - row))
        rank_top = rank_top + jnp.where(before_top, 1.0, 0.0)
        rank_bottom = rank_bottom + jnp.where(before_bottom, 1.0, 0.0)
    inverse_top, inverse_bottom = lax.rsqrt(top), lax.rsqrt(bottom)
    value_top, value_bottom = top * inverse_top, bottom * inverse_bottom
    lane_float = lane.astype(jnp.float32)
    theta = zero
    vectors_u, vectors_l = zero, zero
    for k in range(BLOCK):

        def of(first, second):
            return spread_rows(first, k) if k < 8 else spread_rows(second, 15 - k)

        here = lane_float == of(rank_top, rank_bottom)
        inverse_norm = of(inverse_top, inverse_bottom)
        theta = jnp.where(here, of(value_top, value_bottom), theta)
        vectors_u = jnp.where(here, upper[k] * inverse_norm, vectors_u)
        vectors_l = jnp.where(here, lower[k] * inverse_norm, vectors_l)
    theta = mean + scale * (theta - 1.0)
    theta_ref[...] = theta[0, :MODES]
    on_row = jnp.sum(jnp.where(row == lane, theta, 0.0), axis=1, keepdims=True)
    theta_rows_ref[...] = jnp.broadcast_to(on_row, (8, LANES))
    vectors = jnp.concatenate([vectors_u, vectors_l], axis=0)
    mix = dot(transposed, vectors, (((1,), (0,)), ((), ())))
    for j in range(MODES):
        mix_ref[j] = jnp.broadcast_to(mix[:, j : j + 1], (BLOCK, LANES))


def ritz_pairs(terms):
    return call(
        ritz_kernel,
        [(MODES,), (8, LANES), (MODES, BLOCK, LANES)],
        [terms],
        flops=10000000,
        name="ritz_pairs",
    )


def inner(a, b):
    return lax.dot_general(
        a, b, (((1,), (1,)), ((), ())), precision=HIGHEST, preferred_element_type=jnp.float32
    )


def folded(products, offset):
    height, width = products.shape
    row = lax.broadcasted_iota(jnp.int32, (height, width), 0)
    column = lax.broadcasted_iota(jnp.int32, (height, width), 1)
    same = jnp.where((row & 7) == (column & 7), products, 0.0)
    sums = jnp.sum(same.reshape(height // 8, 8, width), axis=1)
    row = lax.broadcasted_iota(jnp.int32, (width, LANES), 0)
    lane = lax.broadcasted_iota(jnp.int32, (width, LANES), 1)
    place = jnp.where((row >> 3) + offset == lane, 1.0, 0.0).astype(jnp.float32)
    return jnp.dot(sums, place, precision=HIGHEST, preferred_element_type=jnp.float32)


def rows_of(x):
    return x.reshape(x.shape[0] * x.shape[1], x.shape[2])


def store_y_differences(source_ref, beside_ref, wide_ref, change_ref, z):
    count, _, ny, _ = source_ref.shape

    @pl.loop(0, count)
    def _(a):
        wide_ref[6:8, :] = beside_ref[a, z, :2]
        wide_ref[8 : 8 + ny, :] = source_ref[a, z]
        wide_ref[8 + ny : 10 + ny, :] = beside_ref[a, z, 2:]
        wide = wide_ref[...]
        change = roll(wide, -1, 0) + roll(wide, 1, 0) - 2.0 * wide
        change_ref[a] = change[8 : 8 + ny]


def plane_stiff(field, change, curvature, stiffness):
    rows = rows_of(field)
    along_x = roll(rows, -1, 1) + roll(rows, 1, 1) - 2.0 * rows
    weight = jnp.broadcast_to(stiffness[None], field.shape)
    weight = rows_of(weight)
    along_y = rows_of(change)
    bent = rows_of(field * curvature[None])
    return inner(bent, rows) + inner(along_x * weight, along_x) + inner(along_y * weight, along_y)


def first_local_kernel(block_ref, beside_ref, curvature_ref, stiffness_ref, tile_ref, wide_ref, change_ref):
    nz, ny, nx = curvature_ref.shape
    wide_ref[...] = jnp.zeros(wide_ref.shape, jnp.float32)
    gram = jnp.zeros((8 * BLOCK, 8 * BLOCK), jnp.float32)
    stiff = jnp.zeros((8 * BLOCK, 8 * BLOCK), jnp.float32)
    for z in range(nz):
        store_y_differences(block_ref, beside_ref, wide_ref, change_ref, z)
        for start in range(0, ny, 8):
            part = slice(start, start + 8)
            field = block_ref[:, z, part, :]
            rows = rows_of(field)
            gram = gram + inner(rows, rows)
            stiff = stiff + plane_stiff(
                field, change_ref[:, part, :], curvature_ref[z, part, :], stiffness_ref[z, part, :]
            )
    half = 8 * HALF
    tile_ref[...] = (
        folded(gram[:half], 0)
        + folded(gram[half:], BLOCK)
        + folded(stiff[:half], 2 * BLOCK)
        + folded(stiff[half:], 3 * BLOCK)
    )


def first_local(block, beside, curvature, stiffness):
    nz, ny, nx = curvature.shape
    (tile,) = call(
        first_local_kernel,
        [(8, LANES)],
        [block, beside, curvature, stiffness],
        scratch=[
            pltpu.VMEM((ny + 16, nx), jnp.float32),
            pltpu.VMEM((BLOCK, ny, nx), jnp.float32),
        ],
        flops=100000000,
        name="first_local",
    )
    return tile


def second_local_kernel(
    modes_ref, images_ref, corrections_ref, beside_ref, curvature_ref, stiffness_ref,
    tile_ref, wide_ref, change_ref,
):
    nz, ny, nx = curvature_ref.shape
    wide_ref[...] = jnp.zeros(wide_ref.shape, jnp.float32)
    half = 8 * HALF
    gram = jnp.zeros((2 * half, 2 * half), jnp.float32)
    cross = jnp.zeros((half, 2 * half), jnp.float32)
    back = jnp.zeros((half, half), jnp.float32)
    low = jnp.zeros((half, half), jnp.float32)
    for z in range(nz):
        store_y_differences(corrections_ref, beside_ref, wide_ref, change_ref, z)
        for start in range(0, ny, 8):
            part = slice(start, start + 8)
            field = corrections_ref[:, z, part, :]
            second = rows_of(field)
            rows = jnp.concatenate([rows_of(modes_ref[:, z, part, :]), second], axis=0)
            images = rows_of(images_ref[:, z, part, :])
            gram = gram + inner(rows, rows)
            cross = cross + inner(images, rows)
            back = back + inner(second, images)
            low = low + plane_stiff(
                field, change_ref[:, part, :], curvature_ref[z, part, :], stiffness_ref[z, part, :]
            )
    tile_ref[...] = (
        folded(gram[:half], 0)
        + folded(gram[half:], BLOCK)
        + folded(cross, 2 * BLOCK)
        + (folded(back, 3 * BLOCK) + folded(low, 3 * BLOCK + HALF))
    )


def second_local(modes, images, corrections, beside, curvature, stiffness):
    nz, ny, nx = curvature.shape
    (tile,) = call(
        second_local_kernel,
        [(8, LANES)],
        [modes, images, corrections, beside, curvature, stiffness],
        scratch=[
            pltpu.VMEM((ny + 16, nx), jnp.float32),
            pltpu.VMEM((HALF, ny, nx), jnp.float32),
        ],
        flops=80000000,
        name="second_local",
    )
    return tile


def across_kernel(block_ref, after_ref, layers_ref, tile_ref, copies_ref):
    count, nz, ny, nx = block_ref.shape
    half = 8 * HALF
    stiff = jnp.zeros((8 * count, 8 * count), jnp.float32)

    def layer(k, part):
        return block_ref[:, k, part, :] if k < nz else after_ref[:, k - nz, part, :]

    for z in range(1, nz + 1):
        for start in range(0, ny, 8):
            part = slice(start, start + 8)
            change = (layer(z + 1, part) + layer(z - 1, part)) - 2.0 * layer(z, part)
            weight = layers_ref[z + 1, part, :]
            stiff = stiff + inner(rows_of(change * weight[None]), rows_of(change))
    tile = tile_ref[...]
    if count == BLOCK:
        tile = tile + folded(stiff[:half], 2 * BLOCK) + folded(stiff[half:], 3 * BLOCK)
    else:
        tile = tile + folded(stiff, 3 * BLOCK + HALF)
    for k in range(0, copies_ref.shape[0], 8):
        copies_ref[k : k + 8, :] = tile


def across(block, after, layers, tile):
    total = lax.axis_size("gz") * lax.axis_size("gy")
    (copies,) = call(
        across_kernel,
        [(8 * total, LANES)],
        [block, after, layers, tile],
        flops=25000000,
        name="across",
    )
    return copies


def roll(x, shift, axis):
    return pltpu.roll(x, shift % x.shape[axis], axis)


def apply_hessian(before, own, after, wide, curvature, stiff_layers, stiff_wide, layer):
    layers = before[-2:] + own + after[:2]

    def flux(k):
        middle = layers[k + 2]
        return stiff_layers(k + 1) * ((layers[k + 3] + layers[k + 1]) - 2.0 * middle)

    field = own[layer]
    total = curvature * field + (flux(layer + 1) + flux(layer - 1) - 2.0 * flux(layer))
    change = roll(field, -1, 1) + roll(field, 1, 1) - 2.0 * field
    change = stiff_layers(layer + 1) * change
    total = total + (roll(change, -1, 1) + roll(change, 1, 1) - 2.0 * change)
    change = stiff_wide * (roll(wide, -1, 0) + roll(wide, 1, 0) - 2.0 * wide)
    change = roll(change, -1, 0) + roll(change, 1, 0) - 2.0 * change
    rows = field.shape[0]
    return total + change[8 : 8 + rows]


def update_kernel(
    mix_ref, theta_ref, block_ref, before_ref, after_ref, beside_ref,
    curvature_ref, inverse_ref, stiff_layers_ref, stiff_wide_ref,
    modes_ref, images_ref, corrections_ref, layers_ref, wide_ref,
):
    nz, ny, nx = curvature_ref.shape
    wide_ref[...] = jnp.zeros(wide_ref.shape, jnp.float32)
    for source, offset in ((before_ref, 0), (block_ref, nz), (after_ref, 2 * nz)):

        @pl.loop(0, nz)
        def _(z, source=source, offset=offset):
            for start in range(0, nx, LANES):
                lanes = slice(start, start + LANES)
                parts = [source[a, z, :, lanes] for a in range(BLOCK)]
                for j in range(MODES):
                    mixed = mix_ref[j, 0:1, :] * parts[0]
                    for a in range(1, BLOCK):
                        mixed = mixed + mix_ref[j, a : a + 1, :] * parts[a]
                    layers_ref[j, offset + z, :, lanes] = mixed
                    if source is block_ref:
                        wide_ref[j, z, 8 : 8 + ny, lanes] = mixed

    @pl.loop(0, nz)
    def _(z):
        for start in range(0, nx, LANES):
            lanes = slice(start, start + LANES)
            parts = [beside_ref[a, z, :, lanes] for a in range(BLOCK)]
            for j in range(MODES):
                mixed = mix_ref[j, 0:1, :] * parts[0]
                for a in range(1, BLOCK):
                    mixed = mixed + mix_ref[j, a : a + 1, :] * parts[a]
                wide_ref[j, z, 6:8, lanes] = mixed[:2]
                wide_ref[j, z, 8 + ny : 10 + ny, lanes] = mixed[2:]

    @pl.loop(0, MODES)
    def _(j):
        layers = [layers_ref[j, k] for k in range(3 * nz)]
        theta = jnp.broadcast_to(theta_ref[pl.ds(j, 1), :1], (1, nx))
        for z in range(nz):
            image = apply_hessian(
                layers[:nz], layers[nz : 2 * nz], layers[2 * nz :], wide_ref[j, z],
                curvature_ref[z], lambda k: stiff_layers_ref[k], stiff_wide_ref[z], z,
            )
            mode = layers[nz + z]
            images_ref[j, z] = image
            modes_ref[j, z] = mode
            corrections_ref[j, z] = (image - theta * mode) * inverse_ref[z]


def update(mix, theta_rows, block, before, after, beside, fields):
    curvature, inverse, stiff_layers, stiff_wide = fields
    nz, ny, nx = curvature.shape
    return call(
        update_kernel,
        [(MODES, nz, ny, nx)] * 3,
        [mix, theta_rows, block, before, after, beside, curvature, inverse, stiff_layers, stiff_wide],
        scratch=[
            pltpu.VMEM((MODES, 3 * nz, ny, nx), jnp.float32),
            pltpu.VMEM((MODES, nz, ny + 16, nx), jnp.float32),
        ],
        name="update",
    )


def images_kernel(
    block_ref, before_ref, after_ref, beside_ref,
    curvature_ref, stiff_layers_ref, stiff_wide_ref, images_ref, wide_ref,
):
    nz, ny, nx = curvature_ref.shape
    wide_ref[...] = jnp.zeros(wide_ref.shape, jnp.float32)

    @pl.loop(0, MODES)
    def _(j):
        for z in range(nz):
            wide_ref[z, 6:8, :] = beside_ref[j, z, :2]
            wide_ref[z, 8 : 8 + ny, :] = block_ref[j, z]
            wide_ref[z, 8 + ny : 10 + ny, :] = beside_ref[j, z, 2:]
        before = [before_ref[j, z] for z in range(nz)]
        own = [block_ref[j, z] for z in range(nz)]
        after = [after_ref[j, z] for z in range(nz)]
        for z in range(nz):
            images_ref[j, z] = apply_hessian(
                before, own, after, wide_ref[z],
                curvature_ref[z], lambda k: stiff_layers_ref[k], stiff_wide_ref[z], z,
            )


def images_of(block, before, after, beside, fields):
    curvature, _, stiff_layers, stiff_wide = fields
    nz, ny, nx = curvature.shape
    (images,) = call(
        images_kernel,
        [(MODES, nz, ny, nx)],
        [block, before, after, beside, curvature, stiff_layers, stiff_wide],
        scratch=[pltpu.VMEM((nz, ny + 16, nx), jnp.float32)],
        name="images",
    )
    return images


def density_kernel(
    factor, mix_ref, theta_ref, modes_ref, corrections_ref, first_ref, second_ref,
    mode_density_ref, residual_density_ref,
):
    nz, ny, nx = mode_density_ref.shape

    @pl.loop(0, nz)
    def _(z):
        for start in range(0, nx, LANES):
            lanes = slice(start, start + LANES)
            vectors = [modes_ref[a, z, :, lanes] for a in range(MODES)]
            vectors = vectors + [corrections_ref[a, z, :, lanes] for a in range(MODES)]
            images = [first_ref[a, z, :, lanes] for a in range(MODES)]
            images = images + [second_ref[a, z, :, lanes] for a in range(MODES)]
            mode_sum = jnp.zeros((ny, LANES), jnp.float32)
            residual_sum = jnp.zeros((ny, LANES), jnp.float32)
            for j in range(MODES):
                mode = mix_ref[j, 0:1, :] * vectors[0]
                image = mix_ref[j, 0:1, :] * images[0]
                for a in range(1, BLOCK):
                    mode = mode + mix_ref[j, a : a + 1, :] * vectors[a]
                    image = image + mix_ref[j, a : a + 1, :] * images[a]
                residual = image - theta_ref[j : j + 1, :] * mode
                mode_sum = mode_sum + mode * mode
                residual_sum = residual_sum + residual * residual
            mode_density_ref[z, :, lanes] = factor * mode_sum
            residual_density_ref[z, :, lanes] = factor * residual_sum


def densities(factor, mix, theta_rows, modes, corrections, first, second):
    shape = modes.shape[1:]
    return call(
        functools.partial(density_kernel, factor),
        [shape, shape],
        [mix, theta_rows, modes, corrections, first, second],
        name="densities",
    )


def local(initial_block, concentration, stiffness):
    nz, ny, nx = concentration.shape
    cells_total = nz * ny * nx * lax.axis_size("gz") * lax.axis_size("gy")
    curvature = 3.0 * concentration * concentration - 1.0

    after = from_next(initial_block)
    beside = rows_beside(initial_block, 2)
    tile = first_local(initial_block, beside, curvature, stiffness)

    late, tile = lax.optimization_barrier((stiffness, tile))
    next_stiffness = from_next(late)
    previous_stiffness = from_previous(late)
    beside_stiffness = rows_beside(late, 1)
    layers = jnp.concatenate([previous_stiffness[nz - 1 :], stiffness, next_stiffness[:1]], axis=0)
    blank = jnp.zeros((nz, 6, nx), jnp.float32)
    wide = jnp.concatenate(
        [blank, beside_stiffness[:, :2], stiffness, beside_stiffness[:, 2:], blank], axis=1
    )
    precondition = (curvature + 2.0) + 12.0 * stiffness
    precondition = precondition + (layers[2:] + layers[:-2])
    precondition = precondition + (wide[:, 9 : 9 + ny] + wide[:, 7 : 7 + ny])
    precondition = precondition + (jnp.roll(stiffness, -1, 2) + jnp.roll(stiffness, 1, 2))
    fields = (curvature, 1.0 / precondition, layers, wide)

    held, after, tile, fields = lax.optimization_barrier((initial_block, after, tile, fields))
    layers = fields[2]
    terms = all_terms(across(held, after, layers, tile))
    held, terms = lax.optimization_barrier((initial_block, terms))
    before = from_previous(held)
    _, theta_rows, mix = ritz_pairs(terms)
    modes, mode_images, corrections = update(
        mix, theta_rows, initial_block, before, after, beside, fields
    )

    after = from_next(corrections)
    beside = rows_beside(corrections, 2)
    tile = second_local(modes, mode_images, corrections, beside, curvature, stiffness)
    held, after, tile = lax.optimization_barrier((corrections, after, tile))
    terms = all_terms(across(held, after, layers, tile))
    held, terms = lax.optimization_barrier((corrections, terms))
    before = from_previous(held)
    theta, theta_rows, mix = ritz_pairs(terms)
    correction_images = images_of(corrections, before, after, beside, fields)
    mode_density, residual_density = densities(
        float(cells_total / MODES), mix, theta_rows, modes, corrections, mode_images, correction_images
    )
    return (theta, mode_density, residual_density)


def solution(mesh):
    return jax.shard_map(
        local,
        mesh=mesh,
        in_specs=(P("img", "gz", "gy", None), P(("img", "gz"), "gy", None), P("gz", "gy", None)),
        out_specs=(P("img"), P(("img", "gz"), "gy", None), P(("img", "gz"), "gy", None)),
        check_vma=False,
    )
```

```python
import functools

import jax
import jax.numpy as jnp
from jax import lax
from jax.experimental import pallas as pl
from jax.experimental.pallas import tpu as pltpu
from jax.sharding import PartitionSpec as P

BLOCK = 16
MODES = 8
HALF = BLOCK // 2
LANES = 128
MAX_SWEEPS = 14
HIGHEST = lax.Precision.HIGHEST
VMEM = pl.BlockSpec(memory_space=pltpu.VMEM)


def call(kernel, out_shapes, args, scratch=(), flops=1000000, name=None):
    out_shape = tuple(jax.ShapeDtypeStruct(s, jnp.float32) for s in out_shapes)
    moved = 4 * sum(x.size for x in list(args) + list(out_shape))
    return pl.pallas_call(
        kernel,
        out_shape=out_shape,
        in_specs=[VMEM] * len(args),
        out_specs=[VMEM] * len(out_shape),
        scratch_shapes=list(scratch),
        compiler_params=pltpu.CompilerParams(vmem_limit_bytes=40 * 1024 * 1024),
        cost_estimate=pl.CostEstimate(flops=flops, bytes_accessed=moved, transcendentals=0),
        name=name,
    )(*args)


def pair_swap(x):
    return lax.ppermute(x, "gz", [(i, i ^ 1) for i in range(lax.axis_size("gz"))])


def core_swap(x):
    return lax.ppermute(x, "gy", [(0, 1), (1, 0)])


def from_beyond(x):
    size = lax.axis_size("gz")
    return lax.ppermute(x, "gz", [((i + (2 if i % 2 == 0 else size - 2)) % size, i) for i in range(size)])


def from_behind(x):
    size = lax.axis_size("gz")
    return lax.ppermute(x, "gz", [((i + (size - 2 if i % 2 == 0 else 2)) % size, i) for i in range(size)])


def grid_sum(x):
    axes = ("gz", "gy")
    total = lax.axis_size("gz") * lax.axis_size("gy")
    if total & (total - 1):
        return lax.psum(x, axes)
    mask = 1
    while mask < total:
        x = x + lax.ppermute(x, axes, [(i, i ^ mask) for i in range(total)])
        mask *= 2
    return x


def spread_rows(x, k):
    return jnp.broadcast_to(x[k : k + 1, :], (8, LANES))


def every_row(x):
    x = x + pltpu.roll(x, 4, 0)
    x = x + pltpu.roll(x, 2, 0)
    return x + pltpu.roll(x, 1, 0)


def packed_sums(tiles, row):
    low4, low2, low1 = row < 4, (row & 2) == 0, (row & 1) == 0
    tiles = [
        jnp.where(low4, tiles[k], tiles[k + 4])
        + pltpu.roll(jnp.where(low4, tiles[k + 4], tiles[k]), 4, 0)
        for k in range(4)
    ]

    def fold(a, b, low, step):
        other = jnp.where(low, b, a)
        moved = jnp.where(low, pltpu.roll(other, 8 - step, 0), pltpu.roll(other, step, 0))
        return jnp.where(low, a, b) + moved

    tiles = [fold(tiles[k], tiles[k + 2], low2, 2) for k in range(2)]
    return fold(tiles[0], tiles[1], low1, 1)


def tournament():
    players = list(range(BLOCK))
    rounds = []
    for _ in range(BLOCK - 1):
        rounds.append([(players[k], players[BLOCK - 1 - k]) for k in range(HALF)])
        players = [players[0], players[-1]] + players[1:-1]
    return rounds


def ritz_kernel(pencil_ref, theta_ref, theta_rows_ref, mix_ref):
    total = pencil_ref[...]
    row = lax.broadcasted_iota(jnp.int32, (8, LANES), 0)
    lane = lax.broadcasted_iota(jnp.int32, (8, LANES), 1)

    def columns(upper, lower):
        return (
            [jnp.broadcast_to(upper[:, k : k + 1], (8, LANES)) for k in range(BLOCK)],
            [jnp.broadcast_to(lower[:, k : k + 1], (8, LANES)) for k in range(BLOCK)],
        )

    def entry(upper, lower, k):
        return spread_rows(upper, k) if k < 8 else spread_rows(lower, k - 8)

    gram_u, gram_l = columns(total[:, :BLOCK], total[:, BLOCK : 2 * BLOCK])
    zero = jnp.zeros((8, LANES), jnp.float32)
    inverse_u = [jnp.where(row == k, 1.0, 0.0).astype(jnp.float32) for k in range(8)] + [zero] * 8
    inverse_l = [zero] * 8 + [
        jnp.where(row == k, 1.0, 0.0).astype(jnp.float32) for k in range(8)
    ]
    for k in range(BLOCK):
        root = lax.rsqrt(entry(gram_u[k], gram_l[k], k))
        gram_u[k] = gram_u[k] * root
        gram_l[k] = gram_l[k] * root
        inverse_u[k] = inverse_u[k] * root
        inverse_l[k] = inverse_l[k] * root
        for i in range(k + 1, BLOCK):
            factor = entry(gram_u[k], gram_l[k], i)
            if i < 8:
                gram_u[i] = gram_u[i] - factor * gram_u[k]
            gram_l[i] = gram_l[i] - factor * gram_l[k]
            inverse_u[i] = inverse_u[i] - factor * inverse_u[k]
            if k >= 8:
                inverse_l[i] = inverse_l[i] - factor * inverse_l[k]
    transposed_u, transposed_l = zero, zero
    for k in range(BLOCK):
        transposed_u = jnp.where(lane == k, inverse_u[k], transposed_u)
        transposed_l = jnp.where(lane == k, inverse_l[k], transposed_l)
    transposed = jnp.concatenate([transposed_u, transposed_l], axis=0)[:, :BLOCK]

    dot = functools.partial(
        lax.dot_general, precision=HIGHEST, preferred_element_type=jnp.float32
    )
    stiff = jnp.concatenate(
        [total[:, 2 * BLOCK : 3 * BLOCK], total[:, 3 * BLOCK : 4 * BLOCK]], axis=0
    )
    half_way = dot(stiff, transposed, (((1,), (0,)), ((), ())))
    projected = dot(transposed, half_way, (((0,), (0,)), ((), ())))

    upper, lower = columns(projected[:8], projected[8:])
    diagonal = zero
    for k in range(8):
        diagonal = diagonal + jnp.where(row == k, upper[k] + lower[k + 8], 0.0)
    mean = every_row(diagonal) * (1.0 / BLOCK)
    size = zero
    for k in range(8):
        upper[k] = upper[k] - jnp.where(row == k, mean, 0.0)
        lower[k + 8] = lower[k + 8] - jnp.where(row == k, mean, 0.0)
    for k in range(BLOCK):
        size = size + (upper[k] * upper[k] + lower[k] * lower[k])
    scale = 1.25 * jnp.sqrt(every_row(size)) + 1e-30
    shrink = 1.0 / scale
    for k in range(BLOCK):
        upper[k] = upper[k] * shrink
        lower[k] = lower[k] * shrink
    for k in range(8):
        upper[k] = upper[k] + jnp.where(row == k, 1.0, 0.0)
        lower[k + 8] = lower[k + 8] + jnp.where(row == k, 1.0, 0.0)

    def squares(upper, lower):
        top = packed_sums([upper[k] * upper[k] + lower[k] * lower[k] for k in range(8)], row)
        bottom = packed_sums(
            [upper[15 - k] * upper[15 - k] + lower[15 - k] * lower[15 - k] for k in range(8)], row
        )
        return top, bottom

    def sweep(carry):
        count, _, upper, lower = carry
        upper, lower = list(upper), list(lower)
        top, bottom = squares(upper, lower)
        worst = zero
        for pairs in tournament():
            g = packed_sums([upper[i] * upper[j] + lower[i] * lower[j] for i, j in pairs], row)
            d = bottom - top
            g2 = g * g
            worst = jnp.maximum(worst, g2)
            dd = jnp.maximum(jnp.abs(d), 1e-18)
            ih = lax.rsqrt(dd * dd + 4.0 * g2)
            c2 = 0.5 + (0.5 * dd) * ih
            ic = lax.rsqrt(c2)
            c = c2 * ic
            s = jnp.where(d >= 0.0, g, -g) * (ih * ic)
            move = (s * ic) * g
            top = top - move
            bottom = bottom + move
            for k, (i, j) in enumerate(pairs):
                ck, sk = spread_rows(c, k), spread_rows(s, k)
                ui, uj, li, lj = upper[i], upper[j], lower[i], lower[j]
                upper[i] = ck * ui - sk * uj
                lower[i] = ck * li - sk * lj
                upper[j] = sk * ui + ck * uj
                lower[j] = sk * li + ck * lj
            next_top = jnp.where(
                row == 0, top, jnp.where(row == 1, pltpu.roll(bottom, 1, 0), pltpu.roll(top, 1, 0))
            )
            bottom = jnp.where(row == 7, top, pltpu.roll(bottom, 7, 0))
            top = next_top
        return count + 1, jnp.max(worst), tuple(upper), tuple(lower)

    def unfinished(carry):
        count, worst, _, _ = carry
        return jnp.logical_and(count < MAX_SWEEPS, worst > 1e-8)

    _, _, upper, lower = lax.while_loop(
        unfinished, sweep, (jnp.int32(0), jnp.float32(1.0), tuple(upper), tuple(lower))
    )

    top, bottom = squares(upper, lower)
    rank_top, rank_bottom = zero, zero
    for k in range(BLOCK):
        mine = spread_rows(top, k) if k < 8 else spread_rows(bottom, 15 - k)
        before_top = (mine < top) | ((mine == top) & (k < row))
        before_bottom = (mine < bottom) | ((mine == bottom) & (k < 15 - row))
        rank_top = rank_top + jnp.where(before_top, 1.0, 0.0)
        rank_bottom = rank_bottom + jnp.where(before_bottom, 1.0, 0.0)
    inverse_top, inverse_bottom = lax.rsqrt(top), lax.rsqrt(bottom)
    value_top, value_bottom = top * inverse_top, bottom * inverse_bottom
    lane_float = lane.astype(jnp.float32)
    theta = zero
    vectors_u, vectors_l = zero, zero
    for k in range(BLOCK):

        def of(first, second):
            return spread_rows(first, k) if k < 8 else spread_rows(second, 15 - k)

        here = lane_float == of(rank_top, rank_bottom)
        inverse_norm = of(inverse_top, inverse_bottom)
        theta = jnp.where(here, of(value_top, value_bottom), theta)
        vectors_u = jnp.where(here, upper[k] * inverse_norm, vectors_u)
        vectors_l = jnp.where(here, lower[k] * inverse_norm, vectors_l)
    theta = mean + scale * (theta - 1.0)
    theta_ref[...] = theta[0, :MODES]
    on_row = jnp.sum(jnp.where(row == lane, theta, 0.0), axis=1, keepdims=True)
    theta_rows_ref[...] = jnp.broadcast_to(on_row, (8, LANES))
    vectors = jnp.concatenate([vectors_u, vectors_l], axis=0)
    mix = dot(transposed, vectors, (((1,), (0,)), ((), ())))
    for j in range(MODES):
        mix_ref[j] = jnp.broadcast_to(mix[:, j : j + 1], (BLOCK, LANES))


def ritz_pairs(pencil):
    return call(
        ritz_kernel,
        [(MODES,), (8, LANES), (MODES, BLOCK, LANES)],
        [pencil],
        flops=10000000,
        name="ritz_pairs",
    )


def inner(a, b):
    return lax.dot_general(
        a, b, (((1,), (1,)), ((), ())), precision=HIGHEST, preferred_element_type=jnp.float32
    )


def folded(products, offset):
    height, width = products.shape
    row = lax.broadcasted_iota(jnp.int32, (height, width), 0)
    column = lax.broadcasted_iota(jnp.int32, (height, width), 1)
    same = jnp.where((row & 7) == (column & 7), products, 0.0)
    sums = jnp.sum(same.reshape(height // 8, 8, width), axis=1)
    row = lax.broadcasted_iota(jnp.int32, (width, LANES), 0)
    lane = lax.broadcasted_iota(jnp.int32, (width, LANES), 1)
    place = jnp.where((row >> 3) + offset == lane, 1.0, 0.0).astype(jnp.float32)
    return jnp.dot(sums, place, precision=HIGHEST, preferred_element_type=jnp.float32)


def rows_of(x):
    return x.reshape(x.shape[0] * x.shape[1], x.shape[2])


def roll(x, shift, axis):
    return pltpu.roll(x, shift % x.shape[axis], axis)


def store_y_differences(source_ref, beside_ref, wide_ref, change_ref, z):
    count, _, ny, _ = source_ref.shape

    @pl.loop(0, count)
    def _(a):
        wide_ref[6:8, :] = beside_ref[a, z, :2]
        wide_ref[8 : 8 + ny, :] = source_ref[a, z]
        wide_ref[8 + ny : 10 + ny, :] = beside_ref[a, z, 2:]
        wide = wide_ref[...]
        change = roll(wide, -1, 0) + roll(wide, 1, 0) - 2.0 * wide
        change_ref[a] = change[8 : 8 + ny]


def second_x(rows):
    return roll(rows, -1, 1) + roll(rows, 1, 1) - 2.0 * rows


def prepare_kernel(flags_ref, block_ref, stiffness_ref, concentration_ref, mine_ref, other_ref):
    nz, ny, _ = concentration_ref.shape
    half = ny // 2
    odd = flags_ref[0] > 0.5
    high = flags_ref[1] > 0.5

    def split(source, a):
        for z in range(nz):
            layer = [
                jnp.where(odd, source(nz - 1 - z)[part], source(z)[part])
                for part in (slice(0, half), slice(half, ny))
            ]
            mine_ref[a, z] = jnp.where(high, layer[1], layer[0])
            other_ref[a, nz - 1 - z] = jnp.where(high, layer[0], layer[1])

    @pl.loop(0, BLOCK)
    def _(a):
        split(lambda z: block_ref[a, z], a)

    split(lambda z: stiffness_ref[z], BLOCK)
    split(lambda z: concentration_ref[z], BLOCK + 1)


def first_local_kernel(block_ref, beside_ref, curvature_ref, stiffness_ref, tile_ref, wide_ref, change_ref):
    nz, ny, nx = curvature_ref.shape
    wide_ref[...] = jnp.zeros(wide_ref.shape, jnp.float32)
    gram = jnp.zeros((8 * BLOCK, 8 * BLOCK), jnp.float32)
    stiff = jnp.zeros((8 * BLOCK, 8 * BLOCK), jnp.float32)
    for z in range(nz):
        store_y_differences(block_ref, beside_ref, wide_ref, change_ref, z)
        for start in range(0, ny, 8):
            part = slice(start, start + 8)
            field = block_ref[:, z, part, :]
            weight = stiffness_ref[z, part, :][None]
            rows = rows_of(field)
            along_x = second_x(rows)
            along_y = change_ref[:, part, :]
            gram = gram + inner(rows, rows)
            stiff = stiff + inner(rows_of(field * curvature_ref[z, part, :][None]), rows)
            stiff = stiff + inner(rows_of(along_x.reshape(field.shape) * weight), along_x)
            stiff = stiff + inner(rows_of(along_y * weight), rows_of(along_y))
    half = 8 * HALF
    tile_ref[...] = (
        folded(gram[:half], 0)
        + folded(gram[half:], BLOCK)
        + folded(stiff[:half], 2 * BLOCK)
        + folded(stiff[half:], 3 * BLOCK)
    )


def edges(flags_ref, field, layers):
    high = flags_ref[1][:2] > 0.5
    to_pair, to_core = [], []
    for u in range(layers):
        first, last = field(u)[:2], field(u)[-2:]
        to_pair.append(jnp.where(high, first, last))
        to_core.append(jnp.where(high, last, first))
    return to_pair[::-1], to_core


def first_across_kernel(flags_ref, mine_ref, theirs_ref, beyond_ref, tile_ref, sum_ref, pair_ref, core_ref):
    nz, ny = mine_ref.shape[1:3]
    half = 8 * HALF
    stiff = jnp.zeros((8 * BLOCK, 8 * BLOCK), jnp.float32)
    sources = [(mine_ref, z) for z in range(nz)] + [(theirs_ref, z) for z in range(nz)]
    sources = sources + [(beyond_ref, z) for z in range(2)]
    for u in range(1, 2 * nz + 1):
        for start in range(0, ny, 8):
            part = slice(start, start + 8)

            def layer(k):
                source, z = sources[k]
                return source[:BLOCK, z, part, :]

            source, z = sources[u]
            change = (layer(u + 1) + layer(u - 1)) - 2.0 * layer(u)
            weight = source[BLOCK, z, part, :]
            stiff = stiff + inner(rows_of(change * weight[None]), rows_of(change))
    sum_ref[...] = (
        tile_ref[...] + folded(stiff[:half], 2 * BLOCK) + folded(stiff[half:], 3 * BLOCK)
    )

    @pl.loop(0, BLOCK + 1)
    def _(a):
        field = lambda u: sources[u][0][a, sources[u][1]]
        to_pair, to_core = edges(flags_ref, field, 2 * nz)
        for u in range(2 * nz):
            pair_ref[a, 2 * u : 2 * u + 2, :] = to_pair[u]
            core_ref[a, 2 * u : 2 * u + 2, :] = to_core[u]


def apply_hessian(field, layers, stiff_layers, u, curvature, wide, stiff_wide):
    def flux(k):
        return stiff_layers(k) * ((layers(k + 1) + layers(k - 1)) - 2.0 * layers(k))

    total = curvature * field + (flux(u + 1) + flux(u - 1) - 2.0 * flux(u))
    change = second_x(stiff_layers(u) * second_x(field))
    total = total + change
    change = stiff_wide * (roll(wide, -1, 0) + roll(wide, 1, 0) - 2.0 * wide)
    change = roll(change, -1, 0) + roll(change, 1, 0) - 2.0 * change
    return total + change[8 : 8 + field.shape[0]]


def store_wide(wide_ref, index, flags_ref, field, pair_rows, core_rows):
    ny = field.shape[0]
    high = flags_ref[1][:2] > 0.5
    wide_ref[index, 6:8, :] = jnp.where(high, pair_rows, core_rows)
    wide_ref[index, 8 : 8 + ny, :] = field
    wide_ref[index, 8 + ny : 10 + ny, :] = jnp.where(high, core_rows, pair_rows)


def update_kernel(
    flags_ref, mix_ref, theta_ref, mine_ref, theirs_ref, behind_ref, beyond_ref, pair_ref, core_ref,
    modes_ref, images_ref, near_ref, far_ref, to_pair_ref, to_core_ref,
    curvature_ref, stiff_layers_ref, stiff_wide_ref,
    mixed_ref, mixed_pair_ref, mixed_core_ref, wide_ref, inverse_ref,
):
    depth, ny, nx = curvature_ref.shape
    nz = depth // 2
    wide_ref[...] = jnp.zeros(wide_ref.shape, jnp.float32)
    stiff_wide_ref[...] = jnp.zeros(stiff_wide_ref.shape, jnp.float32)
    sources = [(behind_ref, nz - 2), (behind_ref, nz - 1)]
    sources = sources + [(mine_ref, z) for z in range(nz)] + [(theirs_ref, z) for z in range(nz)]
    sources = sources + [(beyond_ref, 0), (beyond_ref, 1)]
    tiles = [(source, z, mixed_ref, k) for k, (source, z) in enumerate(sources)]
    tiles = tiles + [(pair_ref, None, mixed_pair_ref, None), (core_ref, None, mixed_core_ref, None)]
    for source, z, target, k in tiles:
        for start in range(0, nx, LANES):
            lanes = slice(start, start + LANES)
            if z is None:
                parts = [source[a, :, lanes] for a in range(BLOCK)]
            else:
                parts = [source[a, z, :, lanes] for a in range(BLOCK)]
            for j in range(MODES):
                mixed = mix_ref[j, 0:1, :] * parts[0]
                for a in range(1, BLOCK):
                    mixed = mixed + mix_ref[j, a : a + 1, :] * parts[a]
                if z is None:
                    target[j, :, lanes] = mixed
                else:
                    target[j, k, :, lanes] = mixed

    for k in range(depth + 2):
        source, z = sources[k + 1]
        stiff_layers_ref[k] = source[BLOCK, z]
    for u in range(depth):
        rows = slice(2 * u, 2 * u + 2)
        stiff = stiff_layers_ref[u + 1]
        store_wide(stiff_wide_ref, u, flags_ref, stiff, pair_ref[BLOCK, rows, :], core_ref[BLOCK, rows, :])
        source, z = sources[u + 2]
        concentration = source[BLOCK + 1, z]
        curvature = 3.0 * concentration * concentration - 1.0
        curvature_ref[u] = curvature
        total = (curvature + 2.0) + 12.0 * stiff
        total = total + (stiff_layers_ref[u] + stiff_layers_ref[u + 2])
        total = total + (stiff_wide_ref[u, 7 : 7 + ny, :] + stiff_wide_ref[u, 9 : 9 + ny, :])
        total = total + (roll(stiff, -1, 1) + roll(stiff, 1, 1))
        inverse_ref[u] = 1.0 / total

    @pl.loop(0, MODES)
    def _(j):
        theta = jnp.broadcast_to(theta_ref[pl.ds(j, 1), :1], (1, nx))
        corrections = []
        for u in range(depth):
            rows = slice(2 * u, 2 * u + 2)
            mode = mixed_ref[j, u + 2]
            store_wide(wide_ref, u, flags_ref, mode, mixed_pair_ref[j, rows, :], mixed_core_ref[j, rows, :])
            image = apply_hessian(
                mode, lambda k: mixed_ref[j, k + 2], lambda k: stiff_layers_ref[k + 1], u,
                curvature_ref[u], wide_ref[u], stiff_wide_ref[u],
            )
            images_ref[j, u] = image
            modes_ref[j, u] = mode
            correction = (image - theta * mode) * inverse_ref[u]
            corrections.append(correction)
            if u < nz:
                near_ref[j, u] = correction
            else:
                far_ref[j, u - nz] = correction
        to_pair, to_core = edges(flags_ref, lambda u: corrections[u], depth)
        for u in range(depth):
            to_pair_ref[j, 2 * u : 2 * u + 2, :] = to_pair[u]
            to_core_ref[j, 2 * u : 2 * u + 2, :] = to_core[u]


def second_local_kernel(modes_ref, images_ref, near_ref, far_ref, curvature_ref, stiff_layers_ref, tile_ref):
    depth, ny, nx = curvature_ref.shape
    nz = depth // 2
    half = 8 * HALF
    gram = jnp.zeros((2 * half, 2 * half), jnp.float32)
    cross = jnp.zeros((half, 2 * half), jnp.float32)
    back = jnp.zeros((half, half), jnp.float32)
    low = jnp.zeros((half, half), jnp.float32)
    for u in range(depth):
        for start in range(0, ny, 8):
            part = slice(start, start + 8)
            field = near_ref[:, u, part, :] if u < nz else far_ref[:, u - nz, part, :]
            weight = stiff_layers_ref[u + 1, part, :][None]
            second = rows_of(field)
            rows = jnp.concatenate([rows_of(modes_ref[:, u, part, :]), second], axis=0)
            images = rows_of(images_ref[:, u, part, :])
            along_x = second_x(second)
            gram = gram + inner(rows, rows)
            cross = cross + inner(images, rows)
            back = back + inner(second, images)
            low = low + inner(rows_of(field * curvature_ref[u, part, :][None]), second)
            low = low + inner(rows_of(along_x.reshape(field.shape) * weight), along_x)
    tile_ref[...] = (
        folded(gram[:half], 0)
        + folded(gram[half:], BLOCK)
        + folded(cross, 2 * BLOCK)
        + (folded(back, 3 * BLOCK) + folded(low, 3 * BLOCK + HALF))
    )


def second_across_kernel(
    flags_ref, near_ref, far_ref, beyond_ref, pair_ref, core_ref, stiff_layers_ref, tile_ref,
    sum_ref, wide_ref, change_ref,
):
    nz, ny = near_ref.shape[1:3]
    depth = 2 * nz
    wide_ref[...] = jnp.zeros(wide_ref.shape, jnp.float32)
    sources = [(near_ref, z) for z in range(nz)] + [(far_ref, z) for z in range(nz)]
    sources = sources + [(beyond_ref, 0), (beyond_ref, 1)]

    @pl.loop(0, MODES)
    def _(j):
        for u in range(depth):
            source, z = sources[u]
            rows = slice(2 * u, 2 * u + 2)
            store_wide(wide_ref, u, flags_ref, source[j, z], pair_ref[j, rows, :], core_ref[j, rows, :])
            wide = wide_ref[u]
            change = roll(wide, -1, 0) + roll(wide, 1, 0) - 2.0 * wide
            change_ref[j, u] = change[8 : 8 + ny]

    low = jnp.zeros((8 * MODES, 8 * MODES), jnp.float32)
    for u in range(depth):
        for start in range(0, ny, 8):
            part = slice(start, start + 8)

            def layer(k):
                source, z = sources[k]
                return source[:, z, part, :]

            change = change_ref[:, u, part, :]
            weight = stiff_layers_ref[u + 1, part, :][None]
            low = low + inner(rows_of(change * weight), rows_of(change))
            change = (layer(u + 2) + layer(u)) - 2.0 * layer(u + 1)
            weight = stiff_layers_ref[u + 2, part, :][None]
            low = low + inner(rows_of(change * weight), rows_of(change))
    sum_ref[...] = tile_ref[...] + folded(low, 3 * BLOCK + HALF)


def images_kernel(
    flags_ref, near_ref, far_ref, behind_ref, beyond_ref, pair_ref, core_ref,
    curvature_ref, stiff_layers_ref, stiff_wide_ref, images_ref, wide_ref,
):
    depth, ny, nx = curvature_ref.shape
    nz = depth // 2
    wide_ref[...] = jnp.zeros(wide_ref.shape, jnp.float32)
    sources = [(behind_ref, nz - 2), (behind_ref, nz - 1)]
    sources = sources + [(near_ref, z) for z in range(nz)] + [(far_ref, z) for z in range(nz)]
    sources = sources + [(beyond_ref, 0), (beyond_ref, 1)]

    @pl.loop(0, MODES)
    def _(j):
        layers = [source[j, z] for source, z in sources]
        for u in range(depth):
            rows = slice(2 * u, 2 * u + 2)
            store_wide(wide_ref, u, flags_ref, layers[u + 2], pair_ref[j, rows, :], core_ref[j, rows, :])
            images_ref[j, u] = apply_hessian(
                layers[u + 2], lambda k: layers[k + 2], lambda k: stiff_layers_ref[k + 1], u,
                curvature_ref[u], wide_ref[u], stiff_wide_ref[u],
            )


def density_kernel(
    factor, mix_ref, theta_ref, modes_ref, near_ref, far_ref, first_ref, second_ref, mine_ref, theirs_ref,
):
    depth, ny, nx = modes_ref.shape[1:]
    nz = depth // 2
    for u in range(depth):
        for start in range(0, nx, LANES):
            lanes = slice(start, start + LANES)
            vectors = [modes_ref[a, u, :, lanes] for a in range(MODES)]
            if u < nz:
                vectors = vectors + [near_ref[a, u, :, lanes] for a in range(MODES)]
            else:
                vectors = vectors + [far_ref[a, u - nz, :, lanes] for a in range(MODES)]
            images = [first_ref[a, u, :, lanes] for a in range(MODES)]
            images = images + [second_ref[a, u, :, lanes] for a in range(MODES)]
            mode_sum = jnp.zeros((ny, LANES), jnp.float32)
            residual_sum = jnp.zeros((ny, LANES), jnp.float32)
            for j in range(MODES):
                mode = mix_ref[j, 0:1, :] * vectors[0]
                image = mix_ref[j, 0:1, :] * images[0]
                for a in range(1, BLOCK):
                    mode = mode + mix_ref[j, a : a + 1, :] * vectors[a]
                    image = image + mix_ref[j, a : a + 1, :] * images[a]
                residual = image - theta_ref[j : j + 1, :] * mode
                mode_sum = mode_sum + mode * mode
                residual_sum = residual_sum + residual * residual
            for k, total in ((0, mode_sum), (1, residual_sum)):
                if u < nz:
                    mine_ref[k, u, :, lanes] = factor * total
                else:
                    theirs_ref[k, depth - 1 - u, :, lanes] = factor * total


def merge_kernel(flags_ref, mine_ref, other_ref, modes_ref, residuals_ref):
    nz, ny, _ = modes_ref.shape
    half = ny // 2
    odd = flags_ref[0] > 0.5
    high = flags_ref[1] > 0.5
    for k, target in ((0, modes_ref), (1, residuals_ref)):
        for z in range(nz):
            mine = jnp.where(odd, mine_ref[k, nz - 1 - z], mine_ref[k, z])
            other = jnp.where(odd, other_ref[k, nz - 1 - z], other_ref[k, z])
            target[z, :half, :] = jnp.where(high, other, mine)
            target[z, half:, :] = jnp.where(high, mine, other)


def local(initial_block, concentration, stiffness):
    nz, ny, nx = concentration.shape
    half = ny // 2
    depth = 2 * nz
    cells_total = nz * ny * nx * lax.axis_size("gz") * lax.axis_size("gy")
    odd = lax.axis_index("gz") % 2
    high = 1 - (odd ^ lax.axis_index("gy"))
    flags = jnp.broadcast_to(
        jnp.stack([odd, high]).astype(jnp.float32)[:, None, None], (2, half, nx)
    )
    halves = (BLOCK + 2, nz, half, nx)
    vector_rows = (BLOCK + 1, 2 * depth, nx)
    plane = (depth, half, nx)
    wide = (depth, half + 16, nx)
    mode_plane = (MODES,) + plane
    mode_half = (MODES, nz, half, nx)
    mode_rows = (MODES, 2 * depth, nx)

    mine, other = call(
        prepare_kernel, [halves, halves], [flags, initial_block, stiffness, concentration], name="prepare"
    )
    theirs = pair_swap(other)
    beyond = from_beyond(mine[:, :2])
    edge_rows = jnp.concatenate([initial_block[:, :, ny - 2 :], initial_block[:, :, :2]], axis=2)
    beside = core_swap(edge_rows)
    curvature = 3.0 * concentration * concentration - 1.0
    (tile,) = call(
        first_local_kernel,
        [(8, LANES)],
        [initial_block, beside, curvature, stiffness],
        scratch=[pltpu.VMEM((ny + 16, nx), jnp.float32), pltpu.VMEM((BLOCK, ny, nx), jnp.float32)],
        flops=100000000,
        name="first_local",
    )
    theirs, beyond, tile = lax.optimization_barrier((theirs, beyond, tile))
    tile, to_pair, to_core = call(
        first_across_kernel,
        [(8, LANES), vector_rows, vector_rows],
        [flags, mine, theirs, beyond, tile],
        flops=25000000,
        name="first_across",
    )
    pencil = grid_sum(tile)
    pencil, held, to_pair, to_core = lax.optimization_barrier((pencil, theirs, to_pair, to_core))
    behind = from_behind(held[:, nz - 2 :])
    pair_rows = pair_swap(to_pair)
    core_rows = core_swap(to_core)
    _, theta_rows, mix = ritz_pairs(pencil)

    (
        modes, mode_images, near, far, to_pair, to_core, curvature, stiff_layers, stiff_wide,
    ) = call(
        update_kernel,
        [mode_plane, mode_plane, mode_half, mode_half, mode_rows, mode_rows]
        + [plane, (depth + 2, half, nx), wide],
        [flags, mix, theta_rows, mine, theirs, behind, beyond, pair_rows, core_rows],
        scratch=[
            pltpu.VMEM((MODES, depth + 4, half, nx), jnp.float32),
            pltpu.VMEM(mode_rows, jnp.float32),
            pltpu.VMEM(mode_rows, jnp.float32),
            pltpu.VMEM(wide, jnp.float32),
            pltpu.VMEM(plane, jnp.float32),
        ],
        name="update",
    )

    beyond = from_beyond(near[:, :2])
    pair_rows = pair_swap(to_pair)
    core_rows = core_swap(to_core)
    (tile,) = call(
        second_local_kernel,
        [(8, LANES)],
        [modes, mode_images, near, far, curvature, stiff_layers],
        flops=80000000,
        name="second_local",
    )
    beyond, pair_rows, core_rows, tile = lax.optimization_barrier((beyond, pair_rows, core_rows, tile))
    (tile,) = call(
        second_across_kernel,
        [(8, LANES)],
        [flags, near, far, beyond, pair_rows, core_rows, stiff_layers, tile],
        scratch=[pltpu.VMEM(wide, jnp.float32), pltpu.VMEM(mode_plane, jnp.float32)],
        flops=25000000,
        name="second_across",
    )
    pencil = grid_sum(tile)
    pencil, held = lax.optimization_barrier((pencil, far))
    behind = from_behind(held[:, nz - 2 :])
    theta, theta_rows, mix = ritz_pairs(pencil)
    (correction_images,) = call(
        images_kernel,
        [mode_plane],
        [flags, near, far, behind, beyond, pair_rows, core_rows, curvature, stiff_layers, stiff_wide],
        scratch=[pltpu.VMEM(wide, jnp.float32)],
        name="images",
    )
    mine, theirs = call(
        functools.partial(density_kernel, float(cells_total / MODES)),
        [(2, nz, half, nx)] * 2,
        [mix, theta_rows, modes, near, far, mode_images, correction_images],
        name="densities",
    )
    mode_density, residual_density = call(
        merge_kernel, [(nz, ny, nx)] * 2, [flags, mine, pair_swap(theirs)], name="merge"
    )
    return (theta, mode_density, residual_density)


def solution(mesh):
    return jax.shard_map(
        local,
        mesh=mesh,
        in_specs=(P("img", "gz", "gy", None), P(("img", "gz"), "gy", None), P("gz", "gy", None)),
        out_specs=(P("img"), P(("img", "gz"), "gy", None), P(("img", "gz"), "gy", None)),
        check_vma=False,
    )
```

```python
import functools

import jax
import jax.numpy as jnp
from jax import lax
from jax.experimental import pallas as pl
from jax.experimental.pallas import tpu as pltpu
from jax.sharding import PartitionSpec as P

BLOCK = 16
MODES = 8
HALF = BLOCK // 2
LANES = 128
MAX_SWEEPS = 14
HIGHEST = lax.Precision.HIGHEST
VMEM = pl.BlockSpec(memory_space=pltpu.VMEM)


def call(kernel, out_shapes, args, scratch=(), flops=1000000, name=None):
    out_shape = tuple(jax.ShapeDtypeStruct(s, jnp.float32) for s in out_shapes)
    moved = 4 * sum(x.size for x in list(args) + list(out_shape))
    return pl.pallas_call(
        kernel,
        out_shape=out_shape,
        in_specs=[VMEM] * len(args),
        out_specs=[VMEM] * len(out_shape),
        scratch_shapes=list(scratch),
        compiler_params=pltpu.CompilerParams(vmem_limit_bytes=40 * 1024 * 1024),
        cost_estimate=pl.CostEstimate(flops=flops, bytes_accessed=moved, transcendentals=0),
        name=name,
    )(*args)


def pair_swap(x):
    return lax.ppermute(x, "gz", [(i, i ^ 1) for i in range(lax.axis_size("gz"))])


def core_swap(x):
    return lax.ppermute(x, "gy", [(0, 1), (1, 0)])


def from_beyond(x):
    size = lax.axis_size("gz")
    return lax.ppermute(x, "gz", [((i + (2 if i % 2 == 0 else size - 2)) % size, i) for i in range(size)])


def from_behind(x):
    size = lax.axis_size("gz")
    return lax.ppermute(x, "gz", [((i + (size - 2 if i % 2 == 0 else 2)) % size, i) for i in range(size)])


def grid_sum(x, later=()):
    axes = ("gz", "gy")
    total = lax.axis_size("gz") * lax.axis_size("gy")
    if total & (total - 1):
        return lax.psum(x, axes), later
    mask = 1
    while mask < total:
        if 2 * mask == total:
            x, later = lax.optimization_barrier((x, later))
        x = x + lax.ppermute(x, axes, [(i, i ^ mask) for i in range(total)])
        mask *= 2
    return x, later


def spread_rows(x, k):
    return jnp.broadcast_to(x[k : k + 1, :], (8, LANES))


def every_row(x):
    x = x + pltpu.roll(x, 4, 0)
    x = x + pltpu.roll(x, 2, 0)
    return x + pltpu.roll(x, 1, 0)


def packed_sums(tiles, row):
    low4, low2, low1 = row < 4, (row & 2) == 0, (row & 1) == 0
    tiles = [
        jnp.where(low4, tiles[k], tiles[k + 4])
        + pltpu.roll(jnp.where(low4, tiles[k + 4], tiles[k]), 4, 0)
        for k in range(4)
    ]

    def fold(a, b, low, step):
        other = jnp.where(low, b, a)
        moved = jnp.where(low, pltpu.roll(other, 8 - step, 0), pltpu.roll(other, step, 0))
        return jnp.where(low, a, b) + moved

    tiles = [fold(tiles[k], tiles[k + 2], low2, 2) for k in range(2)]
    return fold(tiles[0], tiles[1], low1, 1)


def tournament():
    players = list(range(BLOCK))
    rounds = []
    for _ in range(BLOCK - 1):
        rounds.append([(players[k], players[BLOCK - 1 - k]) for k in range(HALF)])
        players = [players[0], players[-1]] + players[1:-1]
    return rounds


def ritz_kernel(pencil_ref, theta_ref, theta_rows_ref, mix_ref):
    total = pencil_ref[...]
    row = lax.broadcasted_iota(jnp.int32, (8, LANES), 0)
    lane = lax.broadcasted_iota(jnp.int32, (8, LANES), 1)

    def columns(upper, lower):
        return (
            [jnp.broadcast_to(upper[:, k : k + 1], (8, LANES)) for k in range(BLOCK)],
            [jnp.broadcast_to(lower[:, k : k + 1], (8, LANES)) for k in range(BLOCK)],
        )

    def entry(upper, lower, k):
        return spread_rows(upper, k) if k < 8 else spread_rows(lower, k - 8)

    gram_u, gram_l = columns(total[:, :BLOCK], total[:, BLOCK : 2 * BLOCK])
    zero = jnp.zeros((8, LANES), jnp.float32)
    inverse_u = [jnp.where(row == k, 1.0, 0.0).astype(jnp.float32) for k in range(8)] + [zero] * 8
    inverse_l = [zero] * 8 + [
        jnp.where(row == k, 1.0, 0.0).astype(jnp.float32) for k in range(8)
    ]
    for k in range(BLOCK):
        root = lax.rsqrt(entry(gram_u[k], gram_l[k], k))
        gram_u[k] = gram_u[k] * root
        gram_l[k] = gram_l[k] * root
        inverse_u[k] = inverse_u[k] * root
        inverse_l[k] = inverse_l[k] * root
        for i in range(k + 1, BLOCK):
            factor = entry(gram_u[k], gram_l[k], i)
            if i < 8:
                gram_u[i] = gram_u[i] - factor * gram_u[k]
            gram_l[i] = gram_l[i] - factor * gram_l[k]
            inverse_u[i] = inverse_u[i] - factor * inverse_u[k]
            if k >= 8:
                inverse_l[i] = inverse_l[i] - factor * inverse_l[k]
    transposed_u, transposed_l = zero, zero
    for k in range(BLOCK):
        transposed_u = jnp.where(lane == k, inverse_u[k], transposed_u)
        transposed_l = jnp.where(lane == k, inverse_l[k], transposed_l)
    transposed = jnp.concatenate([transposed_u, transposed_l], axis=0)[:, :BLOCK]

    dot = functools.partial(
        lax.dot_general, precision=HIGHEST, preferred_element_type=jnp.float32
    )
    stiff = jnp.concatenate(
        [total[:, 2 * BLOCK : 3 * BLOCK], total[:, 3 * BLOCK : 4 * BLOCK]], axis=0
    )
    half_way = dot(stiff, transposed, (((1,), (0,)), ((), ())))
    projected = dot(transposed, half_way, (((0,), (0,)), ((), ())))

    upper, lower = columns(projected[:8], projected[8:])
    diagonal = zero
    for k in range(8):
        diagonal = diagonal + jnp.where(row == k, upper[k] + lower[k + 8], 0.0)
    mean = every_row(diagonal) * (1.0 / BLOCK)
    size = zero
    for k in range(8):
        upper[k] = upper[k] - jnp.where(row == k, mean, 0.0)
        lower[k + 8] = lower[k + 8] - jnp.where(row == k, mean, 0.0)
    for k in range(BLOCK):
        size = size + (upper[k] * upper[k] + lower[k] * lower[k])
    scale = 1.25 * jnp.sqrt(every_row(size)) + 1e-30
    shrink = 1.0 / scale
    for k in range(BLOCK):
        upper[k] = upper[k] * shrink
        lower[k] = lower[k] * shrink
    for k in range(8):
        upper[k] = upper[k] + jnp.where(row == k, 1.0, 0.0)
        lower[k + 8] = lower[k + 8] + jnp.where(row == k, 1.0, 0.0)

    def squares(upper, lower):
        top = packed_sums([upper[k] * upper[k] + lower[k] * lower[k] for k in range(8)], row)
        bottom = packed_sums(
            [upper[15 - k] * upper[15 - k] + lower[15 - k] * lower[15 - k] for k in range(8)], row
        )
        return top, bottom

    def sweep(carry):
        count, _, upper, lower = carry
        upper, lower = list(upper), list(lower)
        top, bottom = squares(upper, lower)
        worst = zero
        for pairs in tournament():
            g = packed_sums([upper[i] * upper[j] + lower[i] * lower[j] for i, j in pairs], row)
            d = bottom - top
            g2 = g * g
            worst = jnp.maximum(worst, g2)
            dd = jnp.maximum(jnp.abs(d), 1e-18)
            ih = lax.rsqrt(dd * dd + 4.0 * g2)
            c2 = 0.5 + (0.5 * dd) * ih
            ic = lax.rsqrt(c2)
            c = c2 * ic
            s = jnp.where(d >= 0.0, g, -g) * (ih * ic)
            move = (s * ic) * g
            top = top - move
            bottom = bottom + move
            for k, (i, j) in enumerate(pairs):
                ck, sk = spread_rows(c, k), spread_rows(s, k)
                ui, uj, li, lj = upper[i], upper[j], lower[i], lower[j]
                upper[i] = ck * ui - sk * uj
                lower[i] = ck * li - sk * lj
                upper[j] = sk * ui + ck * uj
                lower[j] = sk * li + ck * lj
            next_top = jnp.where(
                row == 0, top, jnp.where(row == 1, pltpu.roll(bottom, 1, 0), pltpu.roll(top, 1, 0))
            )
            bottom = jnp.where(row == 7, top, pltpu.roll(bottom, 7, 0))
            top = next_top
        return count + 1, jnp.max(worst), tuple(upper), tuple(lower)

    def unfinished(carry):
        count, worst, _, _ = carry
        return jnp.logical_and(count < MAX_SWEEPS, worst > 1.6e-7)

    _, _, upper, lower = lax.while_loop(
        unfinished, sweep, (jnp.int32(0), jnp.float32(1.0), tuple(upper), tuple(lower))
    )

    top, bottom = squares(upper, lower)
    rank_top, rank_bottom = zero, zero
    for k in range(BLOCK):
        mine = spread_rows(top, k) if k < 8 else spread_rows(bottom, 15 - k)
        before_top = (mine < top) | ((mine == top) & (k < row))
        before_bottom = (mine < bottom) | ((mine == bottom) & (k < 15 - row))
        rank_top = rank_top + jnp.where(before_top, 1.0, 0.0)
        rank_bottom = rank_bottom + jnp.where(before_bottom, 1.0, 0.0)
    inverse_top, inverse_bottom = lax.rsqrt(top), lax.rsqrt(bottom)
    value_top, value_bottom = top * inverse_top, bottom * inverse_bottom
    lane_float = lane.astype(jnp.float32)
    theta = zero
    vectors_u, vectors_l = zero, zero
    for k in range(BLOCK):

        def of(first, second):
            return spread_rows(first, k) if k < 8 else spread_rows(second, 15 - k)

        here = lane_float == of(rank_top, rank_bottom)
        inverse_norm = of(inverse_top, inverse_bottom)
        theta = jnp.where(here, of(value_top, value_bottom), theta)
        vectors_u = jnp.where(here, upper[k] * inverse_norm, vectors_u)
        vectors_l = jnp.where(here, lower[k] * inverse_norm, vectors_l)
    theta = mean + scale * (theta - 1.0)
    theta_ref[...] = theta[0, :MODES]
    on_row = jnp.sum(jnp.where(row == lane, theta, 0.0), axis=1, keepdims=True)
    theta_rows_ref[...] = jnp.broadcast_to(on_row, (8, LANES))
    vectors = jnp.concatenate([vectors_u, vectors_l], axis=0)
    mix = dot(transposed, vectors, (((1,), (0,)), ((), ())))
    for j in range(MODES):
        mix_ref[j] = jnp.broadcast_to(mix[:, j : j + 1], (BLOCK, LANES))


def ritz_pairs(pencil):
    return call(
        ritz_kernel,
        [(MODES,), (8, LANES), (MODES, BLOCK, LANES)],
        [pencil],
        flops=10000000,
        name="ritz_pairs",
    )


def inner(a, b):
    return lax.dot_general(
        a, b, (((1,), (1,)), ((), ())), precision=HIGHEST, preferred_element_type=jnp.float32
    )


def folded(products, offset):
    height, width = products.shape
    row = lax.broadcasted_iota(jnp.int32, (height, width), 0)
    column = lax.broadcasted_iota(jnp.int32, (height, width), 1)
    same = jnp.where((row & 7) == (column & 7), products, 0.0)
    sums = jnp.sum(same.reshape(height // 8, 8, width), axis=1)
    row = lax.broadcasted_iota(jnp.int32, (width, LANES), 0)
    lane = lax.broadcasted_iota(jnp.int32, (width, LANES), 1)
    place = jnp.where((row >> 3) + offset == lane, 1.0, 0.0).astype(jnp.float32)
    return jnp.dot(sums, place, precision=HIGHEST, preferred_element_type=jnp.float32)


def rows_of(x):
    return x.reshape(x.shape[0] * x.shape[1], x.shape[2])


def roll(x, shift, axis):
    return pltpu.roll(x, shift % x.shape[axis], axis)


def store_y_differences(source_ref, beside_ref, wide_ref, change_ref, z):
    count, _, ny, _ = source_ref.shape

    @pl.loop(0, count)
    def _(a):
        wide_ref[6:8, :] = beside_ref[a, z, :2]
        wide_ref[8 : 8 + ny, :] = source_ref[a, z]
        wide_ref[8 + ny : 10 + ny, :] = beside_ref[a, z, 2:]
        wide = wide_ref[...]
        change = roll(wide, -1, 0) + roll(wide, 1, 0) - 2.0 * wide
        change_ref[a] = change[8 : 8 + ny]


def second_x(rows):
    return roll(rows, -1, 1) + roll(rows, 1, 1) - 2.0 * rows


def is_odd():
    return lax.rem(lax.axis_index("gz"), 2)


def is_high():
    return lax.rem(1 + is_odd() + lax.axis_index("gy"), 2)


def prepare_kernel(block_ref, stiffness_ref, concentration_ref, mine_ref, other_ref, arrived):
    nz, ny, _ = concentration_ref.shape
    half = ny // 2
    odd, high = is_odd(), is_high()
    upper = pl.ds(pl.multiple_of(half * high, half), half)
    lower = pl.ds(pl.multiple_of(half * (1 - high), half), half)
    copies = []
    for z in range(nz):
        inward = z + odd * (nz - 1 - 2 * z)
        outward = nz - 1 - inward
        for layer, rows, target in ((inward, upper, mine_ref), (outward, lower, other_ref)):
            moves = (
                (block_ref.at[:, layer, rows, :], target.at[0:BLOCK, z]),
                (stiffness_ref.at[layer, rows, :], target.at[BLOCK, z]),
                (concentration_ref.at[layer, rows, :], target.at[BLOCK + 1, z]),
            )
            for source, place in moves:
                copies.append(pltpu.make_async_copy(source, place, arrived.at[len(copies)]))
    for copy in copies:
        copy.start()
    for copy in copies:
        copy.wait()


def prepare(block, stiffness, concentration):
    nz, ny, nx = concentration.shape
    shape = jax.ShapeDtypeStruct((BLOCK + 2, nz, ny // 2, nx), jnp.float32)
    return pl.pallas_call(
        prepare_kernel,
        out_shape=(shape, shape),
        in_specs=[pl.BlockSpec(memory_space=pltpu.HBM)] * 3,
        out_specs=[VMEM] * 2,
        scratch_shapes=[pltpu.SemaphoreType.DMA((6 * nz,))],
        compiler_params=pltpu.CompilerParams(vmem_limit_bytes=62 * 1024 * 1024),
        name="prepare",
    )(block, stiffness, concentration)


def first_local_kernel(block_ref, beside_ref, curvature_ref, stiffness_ref, tile_ref, wide_ref, change_ref):
    nz, ny, nx = curvature_ref.shape
    wide_ref[...] = jnp.zeros(wide_ref.shape, jnp.float32)
    gram = jnp.zeros((8 * BLOCK, 8 * BLOCK), jnp.float32)
    stiff = jnp.zeros((8 * BLOCK, 8 * BLOCK), jnp.float32)
    for z in range(nz):
        store_y_differences(block_ref, beside_ref, wide_ref, change_ref, z)
        for start in range(0, ny, 8):
            part = slice(start, start + 8)
            field = block_ref[:, z, part, :]
            weight = stiffness_ref[z, part, :][None]
            rows = rows_of(field)
            along_x = second_x(rows)
            along_y = change_ref[:, part, :]
            gram = gram + inner(rows, rows)
            stiff = stiff + inner(rows_of(field * curvature_ref[z, part, :][None]), rows)
            stiff = stiff + inner(rows_of(along_x.reshape(field.shape) * weight), along_x)
            stiff = stiff + inner(rows_of(along_y * weight), rows_of(along_y))
    half = 8 * HALF
    tile_ref[...] = (
        folded(gram[:half], 0)
        + folded(gram[half:], BLOCK)
        + folded(stiff[:half], 2 * BLOCK)
        + folded(stiff[half:], 3 * BLOCK)
    )


def edges(field, layers):
    high = is_high() == 1
    to_pair, to_core = [], []
    for u in range(layers):
        first, last = field(u)[:2], field(u)[-2:]
        to_pair.append(jnp.where(high, first, last))
        to_core.append(jnp.where(high, last, first))
    return to_pair[::-1], to_core


def edges_kernel(mine_ref, theirs_ref, pair_ref, core_ref):
    nz = mine_ref.shape[1]

    @pl.loop(0, BLOCK + 1)
    def _(a):
        field = lambda u: mine_ref[a, u] if u < nz else theirs_ref[a, u - nz]
        to_pair, to_core = edges(field, 2 * nz)
        for u in range(2 * nz):
            pair_ref[a, 2 * u : 2 * u + 2, :] = to_pair[u]
            core_ref[a, 2 * u : 2 * u + 2, :] = to_core[u]


def first_across_kernel(mine_ref, theirs_ref, beyond_ref, tile_ref, sum_ref):
    nz, ny = mine_ref.shape[1:3]
    half = 8 * HALF
    stiff = jnp.zeros((8 * BLOCK, 8 * BLOCK), jnp.float32)
    sources = [(mine_ref, z) for z in range(nz)] + [(theirs_ref, z) for z in range(nz)]
    sources = sources + [(beyond_ref, z) for z in range(2)]
    for u in range(1, 2 * nz + 1):
        for start in range(0, ny, 8):
            part = slice(start, start + 8)

            def layer(k):
                source, z = sources[k]
                return source[:BLOCK, z, part, :]

            source, z = sources[u]
            change = (layer(u + 1) + layer(u - 1)) - 2.0 * layer(u)
            weight = source[BLOCK, z, part, :]
            stiff = stiff + inner(rows_of(change * weight[None]), rows_of(change))
    sum_ref[...] = (
        tile_ref[...] + folded(stiff[:half], 2 * BLOCK) + folded(stiff[half:], 3 * BLOCK)
    )


def apply_hessian(field, layers, stiff_layers, u, curvature, wide, stiff_wide):
    def flux(k):
        return stiff_layers(k) * ((layers(k + 1) + layers(k - 1)) - 2.0 * layers(k))

    total = curvature * field + (flux(u + 1) + flux(u - 1) - 2.0 * flux(u))
    change = second_x(stiff_layers(u) * second_x(field))
    total = total + change
    change = stiff_wide * (roll(wide, -1, 0) + roll(wide, 1, 0) - 2.0 * wide)
    change = roll(change, -1, 0) + roll(change, 1, 0) - 2.0 * change
    return total + change[8 : 8 + field.shape[0]]


def store_wide(wide_ref, index, field, pair_rows, core_rows):
    ny = field.shape[0]
    high = is_high() == 1
    wide_ref[index, 6:8, :] = jnp.where(high, pair_rows, core_rows)
    wide_ref[index, 8 : 8 + ny, :] = field
    wide_ref[index, 8 + ny : 10 + ny, :] = jnp.where(high, core_rows, pair_rows)


def first_images_kernel(
    mine_ref, theirs_ref, behind_ref, beyond_ref, pair_ref, core_ref,
    images_ref, inverse_ref, curvature_ref, stiff_layers_ref, stiff_wide_ref, wide_ref,
):
    depth, ny, nx = curvature_ref.shape
    nz = depth // 2
    wide_ref[...] = jnp.zeros(wide_ref.shape, jnp.float32)
    stiff_wide_ref[...] = jnp.zeros(stiff_wide_ref.shape, jnp.float32)
    sources = [(behind_ref, nz - 2), (behind_ref, nz - 1)]
    sources = sources + [(mine_ref, z) for z in range(nz)] + [(theirs_ref, z) for z in range(nz)]
    sources = sources + [(beyond_ref, 0), (beyond_ref, 1)]
    for k in range(depth + 2):
        source, z = sources[k + 1]
        stiff_layers_ref[k] = source[BLOCK, z]
    for u in range(depth):
        rows = slice(2 * u, 2 * u + 2)
        stiff = stiff_layers_ref[u + 1]
        store_wide(stiff_wide_ref, u, stiff, pair_ref[BLOCK, rows, :], core_ref[BLOCK, rows, :])
        source, z = sources[u + 2]
        concentration = source[BLOCK + 1, z]
        curvature = 3.0 * concentration * concentration - 1.0
        curvature_ref[u] = curvature
        total = (curvature + 2.0) + 12.0 * stiff
        total = total + (stiff_layers_ref[u] + stiff_layers_ref[u + 2])
        total = total + (stiff_wide_ref[u, 7 : 7 + ny, :] + stiff_wide_ref[u, 9 : 9 + ny, :])
        total = total + (roll(stiff, -1, 1) + roll(stiff, 1, 1))
        inverse_ref[u] = 1.0 / total

    @pl.loop(0, BLOCK)
    def _(a):
        layers = [source[a, z] for source, z in sources]
        for u in range(depth):
            rows = slice(2 * u, 2 * u + 2)
            store_wide(wide_ref, u, layers[u + 2], pair_ref[a, rows, :], core_ref[a, rows, :])
            images_ref[a, u] = apply_hessian(
                layers[u + 2], lambda k: layers[k + 2], lambda k: stiff_layers_ref[k + 1], u,
                curvature_ref[u], wide_ref[u], stiff_wide_ref[u],
            )


def update_kernel(
    mix_ref, theta_ref, mine_ref, theirs_ref, search_images_ref, inverse_ref,
    modes_ref, images_ref, near_ref, far_ref, to_pair_ref, to_core_ref,
):
    depth, ny, nx = inverse_ref.shape
    nz = depth // 2
    for start in range(0, nx, LANES):
        lanes = slice(start, start + LANES)
        for u in range(depth):
            source, z = (mine_ref, u) if u < nz else (theirs_ref, u - nz)
            vectors = [source[a, z, :, lanes] for a in range(BLOCK)]
            images = [search_images_ref[a, u, :, lanes] for a in range(BLOCK)]
            inverse = inverse_ref[u, :, lanes]
            for j in range(MODES):
                mode = mix_ref[j, 0:1, :] * vectors[0]
                image = mix_ref[j, 0:1, :] * images[0]
                for a in range(1, BLOCK):
                    mode = mode + mix_ref[j, a : a + 1, :] * vectors[a]
                    image = image + mix_ref[j, a : a + 1, :] * images[a]
                modes_ref[j, u, :, lanes] = mode
                images_ref[j, u, :, lanes] = image
                correction = (image - theta_ref[j : j + 1, :] * mode) * inverse
                if u < nz:
                    near_ref[j, u, :, lanes] = correction
                else:
                    far_ref[j, u - nz, :, lanes] = correction

    @pl.loop(0, MODES)
    def _(j):
        field = lambda u: near_ref[j, u] if u < nz else far_ref[j, u - nz]
        to_pair, to_core = edges(field, depth)
        for u in range(depth):
            to_pair_ref[j, 2 * u : 2 * u + 2, :] = to_pair[u]
            to_core_ref[j, 2 * u : 2 * u + 2, :] = to_core[u]


def second_local_kernel(modes_ref, images_ref, near_ref, far_ref, curvature_ref, stiff_layers_ref, tile_ref):
    depth, ny, nx = curvature_ref.shape
    nz = depth // 2
    half = 8 * HALF
    gram = jnp.zeros((2 * half, 2 * half), jnp.float32)
    cross = jnp.zeros((half, 2 * half), jnp.float32)
    back = jnp.zeros((half, half), jnp.float32)
    low = jnp.zeros((half, half), jnp.float32)
    for u in range(depth):
        for start in range(0, ny, 8):
            part = slice(start, start + 8)
            field = near_ref[:, u, part, :] if u < nz else far_ref[:, u - nz, part, :]
            weight = stiff_layers_ref[u + 1, part, :][None]
            second = rows_of(field)
            rows = jnp.concatenate([rows_of(modes_ref[:, u, part, :]), second], axis=0)
            images = rows_of(images_ref[:, u, part, :])
            along_x = second_x(second)
            gram = gram + inner(rows, rows)
            cross = cross + inner(images, rows)
            back = back + inner(second, images)
            low = low + inner(rows_of(field * curvature_ref[u, part, :][None]), second)
            low = low + inner(rows_of(along_x.reshape(field.shape) * weight), along_x)
    tile_ref[...] = (
        folded(gram[:half], 0)
        + folded(gram[half:], BLOCK)
        + folded(cross, 2 * BLOCK)
        + (folded(back, 3 * BLOCK) + folded(low, 3 * BLOCK + HALF))
    )


def second_across_kernel(
    near_ref, far_ref, beyond_ref, pair_ref, core_ref, stiff_layers_ref, tile_ref,
    sum_ref, wide_ref, change_ref,
):
    nz, ny = near_ref.shape[1:3]
    depth = 2 * nz
    wide_ref[...] = jnp.zeros(wide_ref.shape, jnp.float32)
    sources = [(near_ref, z) for z in range(nz)] + [(far_ref, z) for z in range(nz)]
    sources = sources + [(beyond_ref, 0), (beyond_ref, 1)]

    @pl.loop(0, MODES)
    def _(j):
        for u in range(depth):
            source, z = sources[u]
            rows = slice(2 * u, 2 * u + 2)
            store_wide(wide_ref, u, source[j, z], pair_ref[j, rows, :], core_ref[j, rows, :])
            wide = wide_ref[u]
            change = roll(wide, -1, 0) + roll(wide, 1, 0) - 2.0 * wide
            change_ref[j, u] = change[8 : 8 + ny]

    low = jnp.zeros((8 * MODES, 8 * MODES), jnp.float32)
    for u in range(depth):
        for start in range(0, ny, 8):
            part = slice(start, start + 8)

            def layer(k):
                source, z = sources[k]
                return source[:, z, part, :]

            change = change_ref[:, u, part, :]
            weight = stiff_layers_ref[u + 1, part, :][None]
            low = low + inner(rows_of(change * weight), rows_of(change))
            change = (layer(u + 2) + layer(u)) - 2.0 * layer(u + 1)
            weight = stiff_layers_ref[u + 2, part, :][None]
            low = low + inner(rows_of(change * weight), rows_of(change))
    sum_ref[...] = tile_ref[...] + folded(low, 3 * BLOCK + HALF)


def images_kernel(
    near_ref, far_ref, behind_ref, beyond_ref, pair_ref, core_ref,
    curvature_ref, stiff_layers_ref, stiff_wide_ref, images_ref, wide_ref,
):
    depth, ny, nx = curvature_ref.shape
    nz = depth // 2
    wide_ref[...] = jnp.zeros(wide_ref.shape, jnp.float32)
    sources = [(behind_ref, nz - 2), (behind_ref, nz - 1)]
    sources = sources + [(near_ref, z) for z in range(nz)] + [(far_ref, z) for z in range(nz)]
    sources = sources + [(beyond_ref, 0), (beyond_ref, 1)]

    @pl.loop(0, MODES)
    def _(j):
        layers = [source[j, z] for source, z in sources]
        for u in range(depth):
            rows = slice(2 * u, 2 * u + 2)
            store_wide(wide_ref, u, layers[u + 2], pair_ref[j, rows, :], core_ref[j, rows, :])
            images_ref[j, u] = apply_hessian(
                layers[u + 2], lambda k: layers[k + 2], lambda k: stiff_layers_ref[k + 1], u,
                curvature_ref[u], wide_ref[u], stiff_wide_ref[u],
            )


def density_kernel(
    factor, offset, mix_ref, theta_ref, modes_ref, corrections_ref, first_ref, second_ref, density_ref,
):
    nz, ny, nx = density_ref.shape[1:]
    for layer in range(nz):
        u = offset + layer
        place = layer if offset == 0 else nz - 1 - layer
        for start in range(0, nx, LANES):
            lanes = slice(start, start + LANES)
            vectors = [modes_ref[a, u, :, lanes] for a in range(MODES)]
            vectors = vectors + [corrections_ref[a, layer, :, lanes] for a in range(MODES)]
            images = [first_ref[a, u, :, lanes] for a in range(MODES)]
            images = images + [second_ref[a, u, :, lanes] for a in range(MODES)]
            mode_sum = jnp.zeros((ny, LANES), jnp.float32)
            residual_sum = jnp.zeros((ny, LANES), jnp.float32)
            for j in range(MODES):
                mode = mix_ref[j, 0:1, :] * vectors[0]
                image = mix_ref[j, 0:1, :] * images[0]
                for a in range(1, BLOCK):
                    mode = mode + mix_ref[j, a : a + 1, :] * vectors[a]
                    image = image + mix_ref[j, a : a + 1, :] * images[a]
                residual = image - theta_ref[j : j + 1, :] * mode
                mode_sum = mode_sum + mode * mode
                residual_sum = residual_sum + residual * residual
            density_ref[0, place, :, lanes] = factor * mode_sum
            density_ref[1, place, :, lanes] = factor * residual_sum


def merge_kernel(mine_ref, other_ref, modes_ref, residuals_ref):
    nz, ny, _ = modes_ref.shape
    half = ny // 2
    odd, high = is_odd() == 1, is_high() == 1
    for k, target in ((0, modes_ref), (1, residuals_ref)):
        for z in range(nz):
            mine = jnp.where(odd, mine_ref[k, nz - 1 - z], mine_ref[k, z])
            other = jnp.where(odd, other_ref[k, nz - 1 - z], other_ref[k, z])
            target[z, :half, :] = jnp.where(high, other, mine)
            target[z, half:, :] = jnp.where(high, mine, other)


def local(initial_block, concentration, stiffness):
    nz, ny, nx = concentration.shape
    half = ny // 2
    depth = 2 * nz
    cells_total = nz * ny * nx * lax.axis_size("gz") * lax.axis_size("gy")
    vector_rows = (BLOCK + 1, 2 * depth, nx)
    plane = (depth, half, nx)
    wide = (depth, half + 16, nx)
    mode_plane = (MODES,) + plane
    mode_half = (MODES, nz, half, nx)
    mode_rows = (MODES, 2 * depth, nx)

    mine, other = prepare(initial_block, stiffness, concentration)
    theirs = pair_swap(other)
    beyond = from_beyond(mine[:, :2])
    edge_rows = jnp.concatenate([initial_block[:, :, ny - 2 :], initial_block[:, :, :2]], axis=2)
    beside = core_swap(edge_rows)
    curvature = 3.0 * concentration * concentration - 1.0
    (tile,) = call(
        first_local_kernel,
        [(8, LANES)],
        [initial_block, beside, curvature, stiffness],
        scratch=[pltpu.VMEM((ny + 16, nx), jnp.float32), pltpu.VMEM((BLOCK, ny, nx), jnp.float32)],
        flops=100000000,
        name="first_local",
    )
    theirs, tile = lax.optimization_barrier((theirs, tile))
    to_pair, to_core = call(
        edges_kernel, [vector_rows, vector_rows], [mine, theirs], name="edges"
    )
    core_rows = core_swap(to_core)
    pair_rows = pair_swap(to_pair)
    held, beyond, to_pair, to_core = lax.optimization_barrier((theirs, beyond, to_pair, to_core))
    behind = from_behind(held[:, nz - 2 :])
    (tile,) = call(
        first_across_kernel,
        [(8, LANES)],
        [mine, theirs, beyond, tile],
        flops=25000000,
        name="first_across",
    )
    pencil, (behind, pair_rows, core_rows) = grid_sum(tile, (behind, pair_rows, core_rows))
    search_images, inverse, curvature, stiff_layers, stiff_wide = call(
        first_images_kernel,
        [(BLOCK,) + plane, plane, plane, (depth + 2, half, nx), wide],
        [mine, theirs, behind, beyond, pair_rows, core_rows],
        scratch=[pltpu.VMEM(wide, jnp.float32)],
        flops=6000000,
        name="first_images",
    )
    _, theta_rows, mix = ritz_pairs(pencil)
    modes, mode_images, near, far, to_pair, to_core = call(
        update_kernel,
        [mode_plane, mode_plane, mode_half, mode_half, mode_rows, mode_rows],
        [mix, theta_rows, mine, theirs, search_images, inverse],
        name="update",
    )

    beyond = from_beyond(near[:, :2])
    pair_rows = pair_swap(to_pair)
    core_rows = core_swap(to_core)
    (tile,) = call(
        second_local_kernel,
        [(8, LANES)],
        [modes, mode_images, near, far, curvature, stiff_layers],
        flops=80000000,
        name="second_local",
    )
    held, beyond, pair_rows, core_rows, tile = lax.optimization_barrier(
        (far, beyond, pair_rows, core_rows, tile)
    )
    behind = from_behind(held[:, nz - 2 :])
    (tile,) = call(
        second_across_kernel,
        [(8, LANES)],
        [near, far, beyond, pair_rows, core_rows, stiff_layers, tile],
        scratch=[pltpu.VMEM(wide, jnp.float32), pltpu.VMEM(mode_plane, jnp.float32)],
        flops=25000000,
        name="second_across",
    )
    pencil, behind = grid_sum(tile, behind)
    (correction_images,) = call(
        images_kernel,
        [mode_plane],
        [near, far, behind, beyond, pair_rows, core_rows, curvature, stiff_layers, stiff_wide],
        scratch=[pltpu.VMEM(wide, jnp.float32)],
        name="images",
    )
    theta, theta_rows, mix = ritz_pairs(pencil)
    shares = []
    for offset, corrections in ((nz, far), (0, near)):
        (share,) = call(
            functools.partial(density_kernel, float(cells_total / MODES), offset),
            [(2, nz, half, nx)],
            [mix, theta_rows, modes, corrections, mode_images, correction_images],
            name="densities",
        )
        shares.append(share)
    other = pair_swap(shares[0])
    mode_density, residual_density = call(
        merge_kernel, [(nz, ny, nx)] * 2, [shares[1], other], name="merge"
    )
    return (theta, mode_density, residual_density)


def solution(mesh):
    return jax.shard_map(
        local,
        mesh=mesh,
        in_specs=(P("img", "gz", "gy", None), P(("img", "gz"), "gy", None), P("gz", "gy", None)),
        out_specs=(P("img"), P(("img", "gz"), "gy", None), P(("img", "gz"), "gy", None)),
        check_vma=False,
    )
```

```python
import functools

import jax
import jax.numpy as jnp
from jax import lax
from jax.experimental import pallas as pl
from jax.experimental.pallas import tpu as pltpu
from jax.sharding import PartitionSpec as P

BLOCK = 16
MODES = 8
HALF = BLOCK // 2
LANES = 128
MAX_SWEEPS = 14
HIGHEST = lax.Precision.HIGHEST
VMEM = pl.BlockSpec(memory_space=pltpu.VMEM)


def call(kernel, out_shapes, args, scratch=(), flops=1000000, name=None):
    out_shape = tuple(jax.ShapeDtypeStruct(s, jnp.float32) for s in out_shapes)
    moved = 4 * sum(x.size for x in list(args) + list(out_shape))
    return pl.pallas_call(
        kernel,
        out_shape=out_shape,
        in_specs=[VMEM] * len(args),
        out_specs=[VMEM] * len(out_shape),
        scratch_shapes=list(scratch),
        compiler_params=pltpu.CompilerParams(vmem_limit_bytes=40 * 1024 * 1024),
        cost_estimate=pl.CostEstimate(flops=flops, bytes_accessed=moved, transcendentals=0),
        name=name,
    )(*args)


def pair_swap(x):
    return lax.ppermute(x, "gz", [(i, i ^ 1) for i in range(lax.axis_size("gz"))])


def core_swap(x):
    return lax.ppermute(x, "gy", [(0, 1), (1, 0)])


def from_beyond(x):
    size = lax.axis_size("gz")
    return lax.ppermute(x, "gz", [((i + (2 if i % 2 == 0 else size - 2)) % size, i) for i in range(size)])


def from_behind(x):
    size = lax.axis_size("gz")
    return lax.ppermute(x, "gz", [((i + (size - 2 if i % 2 == 0 else 2)) % size, i) for i in range(size)])


def grid_sum(x, later=()):
    axes = ("gz", "gy")
    total = lax.axis_size("gz") * lax.axis_size("gy")
    if total & (total - 1):
        return lax.psum(x, axes), later

    def other(mask):
        return lax.ppermute(x, axes, [(i, i ^ mask) for i in range(total)])

    mask = 1
    while mask < total:
        wide = mask >= 4 and 4 * mask <= total
        if mask * (4 if wide else 2) == total:
            x, later = lax.optimization_barrier((x, later))
        if wide:
            x = (x + other(mask)) + (other(2 * mask) + other(3 * mask))
            mask *= 4
        else:
            x = x + other(mask)
            mask *= 2
    return x, later


def spread_rows(x, k):
    return jnp.broadcast_to(x[k : k + 1, :], (8, LANES))


def every_row(x):
    x = x + pltpu.roll(x, 4, 0)
    x = x + pltpu.roll(x, 2, 0)
    return x + pltpu.roll(x, 1, 0)


def packed_sums(tiles, row):
    low4, low2, low1 = row < 4, (row & 2) == 0, (row & 1) == 0
    tiles = [
        jnp.where(low4, tiles[k], tiles[k + 4])
        + pltpu.roll(jnp.where(low4, tiles[k + 4], tiles[k]), 4, 0)
        for k in range(4)
    ]

    def fold(a, b, low, step):
        other = jnp.where(low, b, a)
        moved = jnp.where(low, pltpu.roll(other, 8 - step, 0), pltpu.roll(other, step, 0))
        return jnp.where(low, a, b) + moved

    tiles = [fold(tiles[k], tiles[k + 2], low2, 2) for k in range(2)]
    return fold(tiles[0], tiles[1], low1, 1)


def tournament():
    players = list(range(BLOCK))
    rounds = []
    for _ in range(BLOCK - 1):
        rounds.append([(players[k], players[BLOCK - 1 - k]) for k in range(HALF)])
        players = [players[0], players[-1]] + players[1:-1]
    return rounds


def ritz_kernel(pencil_ref, theta_ref, theta_rows_ref, mix_ref):
    total = pencil_ref[...]
    row = lax.broadcasted_iota(jnp.int32, (8, LANES), 0)
    lane = lax.broadcasted_iota(jnp.int32, (8, LANES), 1)

    def columns(upper, lower):
        return (
            [jnp.broadcast_to(upper[:, k : k + 1], (8, LANES)) for k in range(BLOCK)],
            [jnp.broadcast_to(lower[:, k : k + 1], (8, LANES)) for k in range(BLOCK)],
        )

    def entry(upper, lower, k):
        return spread_rows(upper, k) if k < 8 else spread_rows(lower, k - 8)

    gram_u, gram_l = columns(total[:, :BLOCK], total[:, BLOCK : 2 * BLOCK])
    zero = jnp.zeros((8, LANES), jnp.float32)
    inverse_u = [jnp.where(row == k, 1.0, 0.0).astype(jnp.float32) for k in range(8)] + [zero] * 8
    inverse_l = [zero] * 8 + [
        jnp.where(row == k, 1.0, 0.0).astype(jnp.float32) for k in range(8)
    ]
    for k in range(BLOCK):
        root = lax.rsqrt(entry(gram_u[k], gram_l[k], k))
        gram_u[k] = gram_u[k] * root
        gram_l[k] = gram_l[k] * root
        inverse_u[k] = inverse_u[k] * root
        inverse_l[k] = inverse_l[k] * root
        for i in range(k + 1, BLOCK):
            factor = entry(gram_u[k], gram_l[k], i)
            if i < 8:
                gram_u[i] = gram_u[i] - factor * gram_u[k]
            gram_l[i] = gram_l[i] - factor * gram_l[k]
            inverse_u[i] = inverse_u[i] - factor * inverse_u[k]
            if k >= 8:
                inverse_l[i] = inverse_l[i] - factor * inverse_l[k]
    transposed_u, transposed_l = zero, zero
    for k in range(BLOCK):
        transposed_u = jnp.where(lane == k, inverse_u[k], transposed_u)
        transposed_l = jnp.where(lane == k, inverse_l[k], transposed_l)
    transposed = jnp.concatenate([transposed_u, transposed_l], axis=0)[:, :BLOCK]

    dot = functools.partial(
        lax.dot_general, precision=HIGHEST, preferred_element_type=jnp.float32
    )
    stiff = jnp.concatenate(
        [total[:, 2 * BLOCK : 3 * BLOCK], total[:, 3 * BLOCK : 4 * BLOCK]], axis=0
    )
    half_way = dot(stiff, transposed, (((1,), (0,)), ((), ())))
    projected = dot(transposed, half_way, (((0,), (0,)), ((), ())))

    upper, lower = columns(projected[:8], projected[8:])
    diagonal = zero
    for k in range(8):
        diagonal = diagonal + jnp.where(row == k, upper[k] + lower[k + 8], 0.0)
    mean = every_row(diagonal) * (1.0 / BLOCK)
    size = zero
    for k in range(8):
        upper[k] = upper[k] - jnp.where(row == k, mean, 0.0)
        lower[k + 8] = lower[k + 8] - jnp.where(row == k, mean, 0.0)
    for k in range(BLOCK):
        size = size + (upper[k] * upper[k] + lower[k] * lower[k])
    scale = 1.25 * jnp.sqrt(every_row(size)) + 1e-30
    shrink = 1.0 / scale
    for k in range(BLOCK):
        upper[k] = upper[k] * shrink
        lower[k] = lower[k] * shrink
    for k in range(8):
        upper[k] = upper[k] + jnp.where(row == k, 1.0, 0.0)
        lower[k + 8] = lower[k + 8] + jnp.where(row == k, 1.0, 0.0)

    def squares(upper, lower):
        top = packed_sums([upper[k] * upper[k] + lower[k] * lower[k] for k in range(8)], row)
        bottom = packed_sums(
            [upper[15 - k] * upper[15 - k] + lower[15 - k] * lower[15 - k] for k in range(8)], row
        )
        return top, bottom

    def sweep(carry):
        count, _, upper, lower = carry
        upper, lower = list(upper), list(lower)
        top, bottom = squares(upper, lower)
        worst = zero
        for pairs in tournament():
            g = packed_sums([upper[i] * upper[j] + lower[i] * lower[j] for i, j in pairs], row)
            d = bottom - top
            g2 = g * g
            worst = jnp.maximum(worst, g2)
            dd = jnp.maximum(jnp.abs(d), 1e-18)
            ih = lax.rsqrt(g2 + 0.25 * (dd * dd))
            c2 = 0.5 + (0.25 * dd) * ih
            ic = lax.rsqrt(c2)
            c = c2 * ic
            s = (jnp.where(d >= 0.0, 0.5, -0.5) * g) * (ih * ic)
            move = (s * ic) * g
            top = top - move
            bottom = bottom + move
            for k, (i, j) in enumerate(pairs):
                ck, sk = spread_rows(c, k), spread_rows(s, k)
                ui, uj, li, lj = upper[i], upper[j], lower[i], lower[j]
                upper[i] = ck * ui - sk * uj
                lower[i] = ck * li - sk * lj
                upper[j] = sk * ui + ck * uj
                lower[j] = sk * li + ck * lj
            next_top = jnp.where(
                row == 0, top, jnp.where(row == 1, pltpu.roll(bottom, 1, 0), pltpu.roll(top, 1, 0))
            )
            bottom = jnp.where(row == 7, top, pltpu.roll(bottom, 7, 0))
            top = next_top
        return count + 1, jnp.max(worst), tuple(upper), tuple(lower)

    def unfinished(carry):
        count, worst, _, _ = carry
        return jnp.logical_and(count < MAX_SWEEPS, worst > 1.6e-7)

    _, _, upper, lower = lax.while_loop(
        unfinished, sweep, (jnp.int32(0), jnp.float32(1.0), tuple(upper), tuple(lower))
    )

    top, bottom = squares(upper, lower)
    rank_top, rank_bottom = zero, zero
    for k in range(BLOCK):
        mine = spread_rows(top, k) if k < 8 else spread_rows(bottom, 15 - k)
        before_top = (mine < top) | ((mine == top) & (k < row))
        before_bottom = (mine < bottom) | ((mine == bottom) & (k < 15 - row))
        rank_top = rank_top + jnp.where(before_top, 1.0, 0.0)
        rank_bottom = rank_bottom + jnp.where(before_bottom, 1.0, 0.0)
    inverse_top, inverse_bottom = lax.rsqrt(top), lax.rsqrt(bottom)
    value_top, value_bottom = top * inverse_top, bottom * inverse_bottom
    lane_float = lane.astype(jnp.float32)
    theta = zero
    vectors_u, vectors_l = zero, zero
    for k in range(BLOCK):

        def of(first, second):
            return spread_rows(first, k) if k < 8 else spread_rows(second, 15 - k)

        here = lane_float == of(rank_top, rank_bottom)
        inverse_norm = of(inverse_top, inverse_bottom)
        theta = jnp.where(here, of(value_top, value_bottom), theta)
        vectors_u = jnp.where(here, upper[k] * inverse_norm, vectors_u)
        vectors_l = jnp.where(here, lower[k] * inverse_norm, vectors_l)
    theta = mean + scale * (theta - 1.0)
    theta_ref[...] = theta[0, :MODES]
    on_row = jnp.sum(jnp.where(row == lane, theta, 0.0), axis=1, keepdims=True)
    theta_rows_ref[...] = jnp.broadcast_to(on_row, (8, LANES))
    vectors = jnp.concatenate([vectors_u, vectors_l], axis=0)
    mix = dot(transposed, vectors, (((1,), (0,)), ((), ())))
    for j in range(MODES):
        mix_ref[j] = jnp.broadcast_to(mix[:, j : j + 1], (BLOCK, LANES))


def ritz_pairs(pencil):
    return call(
        ritz_kernel,
        [(MODES,), (8, LANES), (MODES, BLOCK, LANES)],
        [pencil],
        flops=10000000,
        name="ritz_pairs",
    )


def inner(a, b):
    return lax.dot_general(
        a, b, (((1,), (1,)), ((), ())), precision=HIGHEST, preferred_element_type=jnp.float32
    )


def folded(products, offset):
    height, width = products.shape
    row = lax.broadcasted_iota(jnp.int32, (height, width), 0)
    column = lax.broadcasted_iota(jnp.int32, (height, width), 1)
    same = jnp.where((row & 7) == (column & 7), products, 0.0)
    sums = jnp.sum(same.reshape(height // 8, 8, width), axis=1)
    row = lax.broadcasted_iota(jnp.int32, (width, LANES), 0)
    lane = lax.broadcasted_iota(jnp.int32, (width, LANES), 1)
    place = jnp.where((row >> 3) + offset == lane, 1.0, 0.0).astype(jnp.float32)
    return jnp.dot(sums, place, precision=HIGHEST, preferred_element_type=jnp.float32)


def rows_of(x):
    return x.reshape(x.shape[0] * x.shape[1], x.shape[2])


def roll(x, shift, axis):
    return pltpu.roll(x, shift % x.shape[axis], axis)


def store_y_differences(source_ref, beside_ref, wide_ref, change_ref, z):
    count, _, ny, _ = source_ref.shape

    @pl.loop(0, count)
    def _(a):
        wide_ref[6:8, :] = beside_ref[a, z, :2]
        wide_ref[8 : 8 + ny, :] = source_ref[a, z]
        wide_ref[8 + ny : 10 + ny, :] = beside_ref[a, z, 2:]
        wide = wide_ref[...]
        change = roll(wide, -1, 0) + roll(wide, 1, 0) - 2.0 * wide
        change_ref[a] = change[8 : 8 + ny]


def second_x(rows):
    return roll(rows, -1, 1) + roll(rows, 1, 1) - 2.0 * rows


def is_odd():
    return lax.rem(lax.axis_index("gz"), 2)


def is_high():
    return lax.rem(1 + is_odd() + lax.axis_index("gy"), 2)


def prepare_kernel(block_ref, stiffness_ref, concentration_ref, mine_ref, other_ref, arrived):
    nz, ny, _ = concentration_ref.shape
    half = ny // 2
    odd, high = is_odd(), is_high()
    upper = pl.ds(pl.multiple_of(half * high, half), half)
    lower = pl.ds(pl.multiple_of(half * (1 - high), half), half)
    copies = []
    for z in range(nz):
        inward = z + odd * (nz - 1 - 2 * z)
        outward = nz - 1 - inward
        for layer, rows, target in ((inward, upper, mine_ref), (outward, lower, other_ref)):
            moves = (
                (block_ref.at[:, layer, rows, :], target.at[0:BLOCK, z]),
                (stiffness_ref.at[layer, rows, :], target.at[BLOCK, z]),
                (concentration_ref.at[layer, rows, :], target.at[BLOCK + 1, z]),
            )
            for source, place in moves:
                copies.append(pltpu.make_async_copy(source, place, arrived.at[len(copies)]))
    for copy in copies:
        copy.start()
    for copy in copies:
        copy.wait()


def prepare(block, stiffness, concentration):
    nz, ny, nx = concentration.shape
    shape = jax.ShapeDtypeStruct((BLOCK + 2, nz, ny // 2, nx), jnp.float32)
    return pl.pallas_call(
        prepare_kernel,
        out_shape=(shape, shape),
        in_specs=[pl.BlockSpec(memory_space=pltpu.HBM)] * 3,
        out_specs=[pl.BlockSpec(memory_space=pltpu.HBM)] * 2,
        scratch_shapes=[pltpu.SemaphoreType.DMA((6 * nz,))],
        compiler_params=pltpu.CompilerParams(vmem_limit_bytes=62 * 1024 * 1024),
        name="prepare",
    )(block, stiffness, concentration)


def first_local_kernel(block_ref, beside_ref, curvature_ref, stiffness_ref, tile_ref, wide_ref, change_ref):
    nz, ny, nx = curvature_ref.shape
    wide_ref[...] = jnp.zeros(wide_ref.shape, jnp.float32)
    gram = jnp.zeros((8 * BLOCK, 8 * BLOCK), jnp.float32)
    stiff = jnp.zeros((8 * BLOCK, 8 * BLOCK), jnp.float32)
    for z in range(nz):
        store_y_differences(block_ref, beside_ref, wide_ref, change_ref, z)
        for start in range(0, ny, 8):
            part = slice(start, start + 8)
            field = block_ref[:, z, part, :]
            weight = stiffness_ref[z, part, :][None]
            rows = rows_of(field)
            along_x = second_x(rows)
            along_y = change_ref[:, part, :]
            gram = gram + inner(rows, rows)
            stiff = stiff + inner(rows_of(field * curvature_ref[z, part, :][None]), rows)
            stiff = stiff + inner(rows_of(along_x.reshape(field.shape) * weight), along_x)
            stiff = stiff + inner(rows_of(along_y * weight), rows_of(along_y))
    half = 8 * HALF
    tile_ref[...] = (
        folded(gram[:half], 0)
        + folded(gram[half:], BLOCK)
        + folded(stiff[:half], 2 * BLOCK)
        + folded(stiff[half:], 3 * BLOCK)
    )


def edges(field, layers):
    high = is_high() == 1
    to_pair, to_core = [], []
    for u in range(layers):
        first, last = field(u)[:2], field(u)[-2:]
        to_pair.append(jnp.where(high, first, last))
        to_core.append(jnp.where(high, last, first))
    return to_pair[::-1], to_core


def edges_kernel(mine_ref, theirs_ref, pair_ref, core_ref):
    nz = mine_ref.shape[1]

    @pl.loop(0, BLOCK + 1)
    def _(a):
        field = lambda u: mine_ref[a, u] if u < nz else theirs_ref[a, u - nz]
        to_pair, to_core = edges(field, 2 * nz)
        for u in range(2 * nz):
            pair_ref[a, 2 * u : 2 * u + 2, :] = to_pair[u]
            core_ref[a, 2 * u : 2 * u + 2, :] = to_core[u]


def first_across_kernel(mine_ref, theirs_ref, beyond_ref, tile_ref, sum_ref):
    nz, ny = mine_ref.shape[1:3]
    half = 8 * HALF
    stiff = jnp.zeros((8 * BLOCK, 8 * BLOCK), jnp.float32)
    sources = [(mine_ref, z) for z in range(nz)] + [(theirs_ref, z) for z in range(nz)]
    sources = sources + [(beyond_ref, z) for z in range(2)]
    for u in range(1, 2 * nz + 1):
        for start in range(0, ny, 8):
            part = slice(start, start + 8)

            def layer(k):
                source, z = sources[k]
                return source[:BLOCK, z, part, :]

            source, z = sources[u]
            change = (layer(u + 1) + layer(u - 1)) - 2.0 * layer(u)
            weight = source[BLOCK, z, part, :]
            stiff = stiff + inner(rows_of(change * weight[None]), rows_of(change))
    sum_ref[...] = (
        tile_ref[...] + folded(stiff[:half], 2 * BLOCK) + folded(stiff[half:], 3 * BLOCK)
    )


def apply_hessian(field, layers, stiff_layers, u, curvature, wide, stiff_wide):
    def flux(k):
        return stiff_layers(k) * ((layers(k + 1) + layers(k - 1)) - 2.0 * layers(k))

    total = curvature * field + (flux(u + 1) + flux(u - 1) - 2.0 * flux(u))
    change = second_x(stiff_layers(u) * second_x(field))
    total = total + change
    change = stiff_wide * (roll(wide, -1, 0) + roll(wide, 1, 0) - 2.0 * wide)
    change = roll(change, -1, 0) + roll(change, 1, 0) - 2.0 * change
    return total + change[8 : 8 + field.shape[0]]


def store_wide(wide_ref, index, field, pair_rows, core_rows):
    ny = field.shape[0]
    high = is_high() == 1
    wide_ref[index, 6:8, :] = jnp.where(high, pair_rows, core_rows)
    wide_ref[index, 8 : 8 + ny, :] = field
    wide_ref[index, 8 + ny : 10 + ny, :] = jnp.where(high, core_rows, pair_rows)


def first_images_kernel(
    mine_ref, theirs_ref, behind_ref, beyond_ref, pair_ref, core_ref,
    images_ref, inverse_ref, curvature_ref, stiff_layers_ref, stiff_wide_ref, wide_ref,
):
    depth, ny, nx = curvature_ref.shape
    nz = depth // 2
    wide_ref[...] = jnp.zeros(wide_ref.shape, jnp.float32)
    stiff_wide_ref[...] = jnp.zeros(stiff_wide_ref.shape, jnp.float32)
    sources = [(behind_ref, nz - 2), (behind_ref, nz - 1)]
    sources = sources + [(mine_ref, z) for z in range(nz)] + [(theirs_ref, z) for z in range(nz)]
    sources = sources + [(beyond_ref, 0), (beyond_ref, 1)]
    for k in range(depth + 2):
        source, z = sources[k + 1]
        stiff_layers_ref[k] = source[BLOCK, z]
    for u in range(depth):
        rows = slice(2 * u, 2 * u + 2)
        stiff = stiff_layers_ref[u + 1]
        store_wide(stiff_wide_ref, u, stiff, pair_ref[BLOCK, rows, :], core_ref[BLOCK, rows, :])
        source, z = sources[u + 2]
        concentration = source[BLOCK + 1, z]
        curvature = 3.0 * concentration * concentration - 1.0
        curvature_ref[u] = curvature
        total = (curvature + 2.0) + 12.0 * stiff
        total = total + (stiff_layers_ref[u] + stiff_layers_ref[u + 2])
        total = total + (stiff_wide_ref[u, 7 : 7 + ny, :] + stiff_wide_ref[u, 9 : 9 + ny, :])
        total = total + (roll(stiff, -1, 1) + roll(stiff, 1, 1))
        inverse_ref[u] = 1.0 / total

    @pl.loop(0, BLOCK)
    def _(a):
        layers = [source[a, z] for source, z in sources]
        for u in range(depth):
            rows = slice(2 * u, 2 * u + 2)
            store_wide(wide_ref, u, layers[u + 2], pair_ref[a, rows, :], core_ref[a, rows, :])
            images_ref[a, u] = apply_hessian(
                layers[u + 2], lambda k: layers[k + 2], lambda k: stiff_layers_ref[k + 1], u,
                curvature_ref[u], wide_ref[u], stiff_wide_ref[u],
            )


def update_kernel(
    mix_ref, theta_ref, mine_ref, theirs_ref, search_images_ref, inverse_ref,
    modes_ref, images_ref, near_ref, far_ref, to_pair_ref, to_core_ref,
):
    depth, ny, nx = inverse_ref.shape
    nz = depth // 2
    for start in range(0, nx, LANES):
        lanes = slice(start, start + LANES)
        for u in range(depth):
            source, z = (mine_ref, u) if u < nz else (theirs_ref, u - nz)
            vectors = [source[a, z, :, lanes] for a in range(BLOCK)]
            images = [search_images_ref[a, u, :, lanes] for a in range(BLOCK)]
            inverse = inverse_ref[u, :, lanes]
            for j in range(MODES):
                mode = mix_ref[j, 0:1, :] * vectors[0]
                image = mix_ref[j, 0:1, :] * images[0]
                for a in range(1, BLOCK):
                    mode = mode + mix_ref[j, a : a + 1, :] * vectors[a]
                    image = image + mix_ref[j, a : a + 1, :] * images[a]
                modes_ref[j, u, :, lanes] = mode
                images_ref[j, u, :, lanes] = image
                correction = (image - theta_ref[j : j + 1, :] * mode) * inverse
                if u < nz:
                    near_ref[j, u, :, lanes] = correction
                else:
                    far_ref[j, u - nz, :, lanes] = correction

    @pl.loop(0, MODES)
    def _(j):
        field = lambda u: near_ref[j, u] if u < nz else far_ref[j, u - nz]
        to_pair, to_core = edges(field, depth)
        for u in range(depth):
            to_pair_ref[j, 2 * u : 2 * u + 2, :] = to_pair[u]
            to_core_ref[j, 2 * u : 2 * u + 2, :] = to_core[u]


def second_local_kernel(modes_ref, images_ref, near_ref, far_ref, curvature_ref, stiff_layers_ref, tile_ref):
    depth, ny, nx = curvature_ref.shape
    nz = depth // 2
    half = 8 * HALF
    products = jnp.zeros((4 * half, 3 * half), jnp.float32)
    low = jnp.zeros((half, half), jnp.float32)
    for u in range(depth):
        for start in range(0, ny, 8):
            part = slice(start, start + 8)
            field = near_ref[:, u, part, :] if u < nz else far_ref[:, u - nz, part, :]
            weight = stiff_layers_ref[u + 1, part, :][None]
            second = rows_of(field)
            rows = jnp.concatenate([rows_of(modes_ref[:, u, part, :]), second], axis=0)
            images = rows_of(images_ref[:, u, part, :])
            along_x = second_x(second)
            bent = rows_of(field * curvature_ref[u, part, :][None])
            products = products + inner(
                jnp.concatenate([rows, bent, images], axis=0), jnp.concatenate([rows, images], axis=0)
            )
            low = low + inner(rows_of(along_x.reshape(field.shape) * weight), along_x)
    gram = products[: 2 * half, : 2 * half]
    back = products[half : 2 * half, 2 * half :]
    low = low + products[2 * half : 3 * half, half : 2 * half]
    cross = products[3 * half :, : 2 * half]
    tile_ref[...] = (
        folded(gram[:half], 0)
        + folded(gram[half:], BLOCK)
        + folded(cross, 2 * BLOCK)
        + (folded(back, 3 * BLOCK) + folded(low, 3 * BLOCK + HALF))
    )


def second_across_kernel(
    near_ref, far_ref, beyond_ref, pair_ref, core_ref, stiff_layers_ref, tile_ref,
    sum_ref, wide_ref, change_ref,
):
    nz, ny = near_ref.shape[1:3]
    depth = 2 * nz
    wide_ref[...] = jnp.zeros(wide_ref.shape, jnp.float32)
    sources = [(near_ref, z) for z in range(nz)] + [(far_ref, z) for z in range(nz)]
    sources = sources + [(beyond_ref, 0), (beyond_ref, 1)]

    @pl.loop(0, MODES)
    def _(j):
        for u in range(depth):
            source, z = sources[u]
            rows = slice(2 * u, 2 * u + 2)
            store_wide(wide_ref, u, source[j, z], pair_ref[j, rows, :], core_ref[j, rows, :])
            wide = wide_ref[u]
            change = roll(wide, -1, 0) + roll(wide, 1, 0) - 2.0 * wide
            change_ref[j, u] = change[8 : 8 + ny]

    low = jnp.zeros((8 * MODES, 8 * MODES), jnp.float32)
    for u in range(depth):
        for start in range(0, ny, 8):
            part = slice(start, start + 8)

            def layer(k):
                source, z = sources[k]
                return source[:, z, part, :]

            change = change_ref[:, u, part, :]
            weight = stiff_layers_ref[u + 1, part, :][None]
            low = low + inner(rows_of(change * weight), rows_of(change))
            change = (layer(u + 2) + layer(u)) - 2.0 * layer(u + 1)
            weight = stiff_layers_ref[u + 2, part, :][None]
            low = low + inner(rows_of(change * weight), rows_of(change))
    sum_ref[...] = tile_ref[...] + folded(low, 3 * BLOCK + HALF)


def images_kernel(
    near_ref, far_ref, behind_ref, beyond_ref, pair_ref, core_ref,
    curvature_ref, stiff_layers_ref, stiff_wide_ref, images_ref, wide_ref,
):
    depth, ny, nx = curvature_ref.shape
    nz = depth // 2
    wide_ref[...] = jnp.zeros(wide_ref.shape, jnp.float32)
    sources = [(behind_ref, nz - 2), (behind_ref, nz - 1)]
    sources = sources + [(near_ref, z) for z in range(nz)] + [(far_ref, z) for z in range(nz)]
    sources = sources + [(beyond_ref, 0), (beyond_ref, 1)]

    @pl.loop(0, MODES)
    def _(j):
        layers = [source[j, z] for source, z in sources]
        for u in range(depth):
            rows = slice(2 * u, 2 * u + 2)
            store_wide(wide_ref, u, layers[u + 2], pair_ref[j, rows, :], core_ref[j, rows, :])
            images_ref[j, u] = apply_hessian(
                layers[u + 2], lambda k: layers[k + 2], lambda k: stiff_layers_ref[k + 1], u,
                curvature_ref[u], wide_ref[u], stiff_wide_ref[u],
            )


def density_kernel(
    factor, offset, mix_ref, theta_ref, modes_ref, corrections_ref, first_ref, second_ref, density_ref,
):
    nz, ny, nx = density_ref.shape[1:]
    for layer in range(nz):
        u = offset + layer
        place = layer if offset == 0 else nz - 1 - layer
        for start in range(0, nx, LANES):
            lanes = slice(start, start + LANES)
            vectors = [modes_ref[a, u, :, lanes] for a in range(MODES)]
            vectors = vectors + [corrections_ref[a, layer, :, lanes] for a in range(MODES)]
            images = [first_ref[a, u, :, lanes] for a in range(MODES)]
            images = images + [second_ref[a, u, :, lanes] for a in range(MODES)]
            mode_sum = jnp.zeros((ny, LANES), jnp.float32)
            residual_sum = jnp.zeros((ny, LANES), jnp.float32)
            for j in range(MODES):
                mode = mix_ref[j, 0:1, :] * vectors[0]
                image = mix_ref[j, 0:1, :] * images[0]
                for a in range(1, BLOCK):
                    mode = mode + mix_ref[j, a : a + 1, :] * vectors[a]
                    image = image + mix_ref[j, a : a + 1, :] * images[a]
                residual = image - theta_ref[j : j + 1, :] * mode
                mode_sum = mode_sum + mode * mode
                residual_sum = residual_sum + residual * residual
            density_ref[0, place, :, lanes] = factor * mode_sum
            density_ref[1, place, :, lanes] = factor * residual_sum


def merge_kernel(mine_ref, other_ref, modes_ref, residuals_ref):
    nz, ny, _ = modes_ref.shape
    half = ny // 2
    odd, high = is_odd() == 1, is_high() == 1
    for k, target in ((0, modes_ref), (1, residuals_ref)):
        for z in range(nz):
            mine = jnp.where(odd, mine_ref[k, nz - 1 - z], mine_ref[k, z])
            other = jnp.where(odd, other_ref[k, nz - 1 - z], other_ref[k, z])
            target[z, :half, :] = jnp.where(high, other, mine)
            target[z, half:, :] = jnp.where(high, mine, other)


def local(initial_block, concentration, stiffness):
    nz, ny, nx = concentration.shape
    half = ny // 2
    depth = 2 * nz
    cells_total = nz * ny * nx * lax.axis_size("gz") * lax.axis_size("gy")
    vector_rows = (BLOCK + 1, 2 * depth, nx)
    plane = (depth, half, nx)
    wide = (depth, half + 16, nx)
    mode_plane = (MODES,) + plane
    mode_half = (MODES, nz, half, nx)
    mode_rows = (MODES, 2 * depth, nx)

    mine, other = prepare(initial_block, stiffness, concentration)
    theirs = pair_swap(other)
    beyond = from_beyond(mine[:, :2])
    edge_rows = jnp.concatenate([initial_block[:, :, ny - 2 :], initial_block[:, :, :2]], axis=2)
    beside = core_swap(edge_rows)
    curvature = 3.0 * concentration * concentration - 1.0
    (tile,) = call(
        first_local_kernel,
        [(8, LANES)],
        [initial_block, beside, curvature, stiffness],
        scratch=[pltpu.VMEM((ny + 16, nx), jnp.float32), pltpu.VMEM((BLOCK, ny, nx), jnp.float32)],
        flops=100000000,
        name="first_local",
    )
    theirs, tile = lax.optimization_barrier((theirs, tile))
    to_pair, to_core = call(
        edges_kernel, [vector_rows, vector_rows], [mine, theirs], name="edges"
    )
    core_rows = core_swap(to_core)
    pair_rows = pair_swap(to_pair)
    held, beyond, to_pair, to_core = lax.optimization_barrier((theirs, beyond, to_pair, to_core))
    behind = from_behind(held[:, nz - 2 :])
    (tile,) = call(
        first_across_kernel,
        [(8, LANES)],
        [mine, theirs, beyond, tile],
        flops=25000000,
        name="first_across",
    )
    pencil, (behind, pair_rows, core_rows) = grid_sum(tile, (behind, pair_rows, core_rows))
    search_images, inverse, curvature, stiff_layers, stiff_wide = call(
        first_images_kernel,
        [(BLOCK,) + plane, plane, plane, (depth + 2, half, nx), wide],
        [mine, theirs, behind, beyond, pair_rows, core_rows],
        scratch=[pltpu.VMEM(wide, jnp.float32)],
        flops=6000000,
        name="first_images",
    )
    _, theta_rows, mix = ritz_pairs(pencil)
    modes, mode_images, near, far, to_pair, to_core = call(
        update_kernel,
        [mode_plane, mode_plane, mode_half, mode_half, mode_rows, mode_rows],
        [mix, theta_rows, mine, theirs, search_images, inverse],
        name="update",
    )

    beyond = from_beyond(near[:, :2])
    pair_rows = pair_swap(to_pair)
    core_rows = core_swap(to_core)
    (tile,) = call(
        second_local_kernel,
        [(8, LANES)],
        [modes, mode_images, near, far, curvature, stiff_layers],
        flops=80000000,
        name="second_local",
    )
    held, beyond, pair_rows, core_rows, tile = lax.optimization_barrier(
        (far, beyond, pair_rows, core_rows, tile)
    )
    behind = from_behind(held[:, nz - 2 :])
    (tile,) = call(
        second_across_kernel,
        [(8, LANES)],
        [near, far, beyond, pair_rows, core_rows, stiff_layers, tile],
        scratch=[pltpu.VMEM(wide, jnp.float32), pltpu.VMEM(mode_plane, jnp.float32)],
        flops=25000000,
        name="second_across",
    )
    pencil, behind = grid_sum(tile, behind)
    (correction_images,) = call(
        images_kernel,
        [mode_plane],
        [near, far, behind, beyond, pair_rows, core_rows, curvature, stiff_layers, stiff_wide],
        scratch=[pltpu.VMEM(wide, jnp.float32)],
        name="images",
    )
    theta, theta_rows, mix = ritz_pairs(pencil)
    shares = []
    for offset, corrections in ((nz, far), (0, near)):
        (share,) = call(
            functools.partial(density_kernel, float(cells_total / MODES), offset),
            [(2, nz, half, nx)],
            [mix, theta_rows, modes, corrections, mode_images, correction_images],
            name="densities",
        )
        shares.append(share)
    other = pair_swap(shares[0])
    mode_density, residual_density = call(
        merge_kernel, [(nz, ny, nx)] * 2, [shares[1], other], name="merge"
    )
    return (theta, mode_density, residual_density)


def solution(mesh):
    return jax.shard_map(
        local,
        mesh=mesh,
        in_specs=(P("img", "gz", "gy", None), P(("img", "gz"), "gy", None), P("gz", "gy", None)),
        out_specs=(P("img"), P(("img", "gz"), "gy", None), P(("img", "gz"), "gy", None)),
        check_vma=False,
    )
```

```python
import functools

import jax
import jax.numpy as jnp
from jax import lax
from jax.experimental import pallas as pl
from jax.experimental.pallas import tpu as pltpu
from jax.sharding import PartitionSpec as P

BLOCK = 16
MODES = 8
HALF = BLOCK // 2
LANES = 128
MAX_SWEEPS = 14
HIGHEST = lax.Precision.HIGHEST
VMEM = pl.BlockSpec(memory_space=pltpu.VMEM)


def call(kernel, out_shapes, args, scratch=(), flops=1000000, name=None):
    out_shape = tuple(jax.ShapeDtypeStruct(s, jnp.float32) for s in out_shapes)
    moved = 4 * sum(x.size for x in list(args) + list(out_shape))
    return pl.pallas_call(
        kernel,
        out_shape=out_shape,
        in_specs=[VMEM] * len(args),
        out_specs=[VMEM] * len(out_shape),
        scratch_shapes=list(scratch),
        compiler_params=pltpu.CompilerParams(vmem_limit_bytes=40 * 1024 * 1024),
        cost_estimate=pl.CostEstimate(flops=flops, bytes_accessed=moved, transcendentals=0),
        name=name,
    )(*args)


def pair_swap(x):
    return lax.ppermute(x, "gz", [(i, i ^ 1) for i in range(lax.axis_size("gz"))])


def core_swap(x):
    return lax.ppermute(x, "gy", [(0, 1), (1, 0)])


def from_beyond(x):
    size = lax.axis_size("gz")
    return lax.ppermute(x, "gz", [((i + (2 if i % 2 == 0 else size - 2)) % size, i) for i in range(size)])


def from_behind(x):
    size = lax.axis_size("gz")
    return lax.ppermute(x, "gz", [((i + (size - 2 if i % 2 == 0 else 2)) % size, i) for i in range(size)])


def grid_sum(x, later, by_four):
    axes = ("gz", "gy")
    total = lax.axis_size("gz") * lax.axis_size("gy")
    if total & (total - 1):
        return lax.psum(x, axes), later

    def other(mask):
        return lax.ppermute(x, axes, [(i, i ^ mask) for i in range(total)])

    mask = 1
    while mask < total:
        wide = by_four and mask >= 4 and 4 * mask <= total
        if mask * (4 if wide else 2) == total:
            x, later = lax.optimization_barrier((x, later))
        if wide:
            x = (x + other(mask)) + (other(2 * mask) + other(3 * mask))
            mask *= 4
        else:
            x = x + other(mask)
            mask *= 2
    return x, later


def spread_rows(x, k):
    return jnp.broadcast_to(x[k : k + 1, :], (8, LANES))


def every_row(x):
    x = x + pltpu.roll(x, 4, 0)
    x = x + pltpu.roll(x, 2, 0)
    return x + pltpu.roll(x, 1, 0)


def packed_sums(tiles, row):
    low4, low2, low1 = row < 4, (row & 2) == 0, (row & 1) == 0
    tiles = [
        jnp.where(low4, tiles[k], tiles[k + 4])
        + pltpu.roll(jnp.where(low4, tiles[k + 4], tiles[k]), 4, 0)
        for k in range(4)
    ]

    def fold(a, b, low, step):
        other = jnp.where(low, b, a)
        moved = jnp.where(low, pltpu.roll(other, 8 - step, 0), pltpu.roll(other, step, 0))
        return jnp.where(low, a, b) + moved

    tiles = [fold(tiles[k], tiles[k + 2], low2, 2) for k in range(2)]
    return fold(tiles[0], tiles[1], low1, 1)


def tournament():
    players = list(range(BLOCK))
    rounds = []
    for _ in range(BLOCK - 1):
        rounds.append([(players[k], players[BLOCK - 1 - k]) for k in range(HALF)])
        players = [players[0], players[-1]] + players[1:-1]
    return rounds


def ritz_kernel(pencil_ref, theta_ref, theta_rows_ref, mix_ref):
    total = pencil_ref[...]
    row = lax.broadcasted_iota(jnp.int32, (8, LANES), 0)
    lane = lax.broadcasted_iota(jnp.int32, (8, LANES), 1)

    def columns(upper, lower):
        return (
            [jnp.broadcast_to(upper[:, k : k + 1], (8, LANES)) for k in range(BLOCK)],
            [jnp.broadcast_to(lower[:, k : k + 1], (8, LANES)) for k in range(BLOCK)],
        )

    def entry(upper, lower, k):
        return spread_rows(upper, k) if k < 8 else spread_rows(lower, k - 8)

    gram_u, gram_l = columns(total[:, :BLOCK], total[:, BLOCK : 2 * BLOCK])
    zero = jnp.zeros((8, LANES), jnp.float32)
    inverse_u = [jnp.where(row == k, 1.0, 0.0).astype(jnp.float32) for k in range(8)] + [zero] * 8
    inverse_l = [zero] * 8 + [
        jnp.where(row == k, 1.0, 0.0).astype(jnp.float32) for k in range(8)
    ]
    for k in range(BLOCK):
        root = lax.rsqrt(entry(gram_u[k], gram_l[k], k))
        gram_u[k] = gram_u[k] * root
        gram_l[k] = gram_l[k] * root
        inverse_u[k] = inverse_u[k] * root
        inverse_l[k] = inverse_l[k] * root
        for i in range(k + 1, BLOCK):
            factor = entry(gram_u[k], gram_l[k], i)
            if i < 8:
                gram_u[i] = gram_u[i] - factor * gram_u[k]
            gram_l[i] = gram_l[i] - factor * gram_l[k]
            inverse_u[i] = inverse_u[i] - factor * inverse_u[k]
            if k >= 8:
                inverse_l[i] = inverse_l[i] - factor * inverse_l[k]
    transposed_u, transposed_l = zero, zero
    for k in range(BLOCK):
        transposed_u = jnp.where(lane == k, inverse_u[k], transposed_u)
        transposed_l = jnp.where(lane == k, inverse_l[k], transposed_l)
    transposed = jnp.concatenate([transposed_u, transposed_l], axis=0)[:, :BLOCK]

    dot = functools.partial(
        lax.dot_general, precision=HIGHEST, preferred_element_type=jnp.float32
    )
    stiff = jnp.concatenate(
        [total[:, 2 * BLOCK : 3 * BLOCK], total[:, 3 * BLOCK : 4 * BLOCK]], axis=0
    )
    half_way = dot(stiff, transposed, (((1,), (0,)), ((), ())))
    projected = dot(transposed, half_way, (((0,), (0,)), ((), ())))

    upper, lower = columns(projected[:8], projected[8:])
    diagonal = zero
    for k in range(8):
        diagonal = diagonal + jnp.where(row == k, upper[k] + lower[k + 8], 0.0)
    mean = every_row(diagonal) * (1.0 / BLOCK)
    size = zero
    for k in range(8):
        upper[k] = upper[k] - jnp.where(row == k, mean, 0.0)
        lower[k + 8] = lower[k + 8] - jnp.where(row == k, mean, 0.0)
    for k in range(BLOCK):
        size = size + (upper[k] * upper[k] + lower[k] * lower[k])
    scale = 1.25 * jnp.sqrt(every_row(size)) + 1e-30
    shrink = 1.0 / scale
    for k in range(BLOCK):
        upper[k] = upper[k] * shrink
        lower[k] = lower[k] * shrink
    for k in range(8):
        upper[k] = upper[k] + jnp.where(row == k, 1.0, 0.0)
        lower[k + 8] = lower[k + 8] + jnp.where(row == k, 1.0, 0.0)

    def squares(upper, lower):
        top = packed_sums([upper[k] * upper[k] + lower[k] * lower[k] for k in range(8)], row)
        bottom = packed_sums(
            [upper[15 - k] * upper[15 - k] + lower[15 - k] * lower[15 - k] for k in range(8)], row
        )
        return top, bottom

    def sweep(carry):
        count, _, upper, lower = carry
        upper, lower = list(upper), list(lower)
        top, bottom = squares(upper, lower)
        worst = zero
        for pairs in tournament():
            g = packed_sums([upper[i] * upper[j] + lower[i] * lower[j] for i, j in pairs], row)
            d = bottom - top
            g2 = g * g
            worst = jnp.maximum(worst, g2)
            dd = jnp.maximum(jnp.abs(d), 1e-18)
            ih = lax.rsqrt(g2 + 0.25 * (dd * dd))
            c2 = 0.5 + (0.25 * dd) * ih
            ic = lax.rsqrt(c2)
            c = c2 * ic
            s = (jnp.where(d >= 0.0, 0.5, -0.5) * g) * (ih * ic)
            move = (s * ic) * g
            top = top - move
            bottom = bottom + move
            for k, (i, j) in enumerate(pairs):
                ck, sk = spread_rows(c, k), spread_rows(s, k)
                ui, uj, li, lj = upper[i], upper[j], lower[i], lower[j]
                upper[i] = ck * ui - sk * uj
                lower[i] = ck * li - sk * lj
                upper[j] = sk * ui + ck * uj
                lower[j] = sk * li + ck * lj
            next_top = jnp.where(
                row == 0, top, jnp.where(row == 1, pltpu.roll(bottom, 1, 0), pltpu.roll(top, 1, 0))
            )
            bottom = jnp.where(row == 7, top, pltpu.roll(bottom, 7, 0))
            top = next_top
        return count + 1, jnp.max(worst), tuple(upper), tuple(lower)

    def unfinished(carry):
        count, worst, _, _ = carry
        return jnp.logical_and(count < MAX_SWEEPS, worst > 1.6e-7)

    _, _, upper, lower = lax.while_loop(
        unfinished, sweep, (jnp.int32(0), jnp.float32(1.0), tuple(upper), tuple(lower))
    )

    top, bottom = squares(upper, lower)
    rank_top, rank_bottom = zero, zero
    for k in range(BLOCK):
        mine = spread_rows(top, k) if k < 8 else spread_rows(bottom, 15 - k)
        before_top = (mine < top) | ((mine == top) & (k < row))
        before_bottom = (mine < bottom) | ((mine == bottom) & (k < 15 - row))
        rank_top = rank_top + jnp.where(before_top, 1.0, 0.0)
        rank_bottom = rank_bottom + jnp.where(before_bottom, 1.0, 0.0)
    inverse_top, inverse_bottom = lax.rsqrt(top), lax.rsqrt(bottom)
    value_top, value_bottom = top * inverse_top, bottom * inverse_bottom
    lane_float = lane.astype(jnp.float32)
    theta = zero
    vectors_u, vectors_l = zero, zero
    for k in range(BLOCK):

        def of(first, second):
            return spread_rows(first, k) if k < 8 else spread_rows(second, 15 - k)

        here = lane_float == of(rank_top, rank_bottom)
        inverse_norm = of(inverse_top, inverse_bottom)
        theta = jnp.where(here, of(value_top, value_bottom), theta)
        vectors_u = jnp.where(here, upper[k] * inverse_norm, vectors_u)
        vectors_l = jnp.where(here, lower[k] * inverse_norm, vectors_l)
    theta = mean + scale * (theta - 1.0)
    theta_ref[...] = theta[0, :MODES]
    on_row = jnp.sum(jnp.where(row == lane, theta, 0.0), axis=1, keepdims=True)
    theta_rows_ref[...] = jnp.broadcast_to(on_row, (8, LANES))
    vectors = jnp.concatenate([vectors_u, vectors_l], axis=0)
    mix = dot(transposed, vectors, (((1,), (0,)), ((), ())))
    for j in range(MODES):
        mix_ref[j] = jnp.broadcast_to(mix[:, j : j + 1], (BLOCK, LANES))


def ritz_pairs(pencil):
    return call(
        ritz_kernel,
        [(MODES,), (8, LANES), (MODES, BLOCK, LANES)],
        [pencil],
        flops=10000000,
        name="ritz_pairs",
    )


def inner(a, b):
    return lax.dot_general(
        a, b, (((1,), (1,)), ((), ())), precision=HIGHEST, preferred_element_type=jnp.float32
    )


def folded(products, offset):
    height, width = products.shape
    row = lax.broadcasted_iota(jnp.int32, (height, width), 0)
    column = lax.broadcasted_iota(jnp.int32, (height, width), 1)
    same = jnp.where((row & 7) == (column & 7), products, 0.0)
    sums = jnp.sum(same.reshape(height // 8, 8, width), axis=1)
    row = lax.broadcasted_iota(jnp.int32, (width, LANES), 0)
    lane = lax.broadcasted_iota(jnp.int32, (width, LANES), 1)
    place = jnp.where((row >> 3) + offset == lane, 1.0, 0.0).astype(jnp.float32)
    return jnp.dot(sums, place, precision=HIGHEST, preferred_element_type=jnp.float32)


def rows_of(x):
    return x.reshape(x.shape[0] * x.shape[1], x.shape[2])


def roll(x, shift, axis):
    return pltpu.roll(x, shift % x.shape[axis], axis)


def store_y_differences(source_ref, beside_ref, wide_ref, change_ref, z):
    count, _, ny, _ = source_ref.shape

    @pl.loop(0, count)
    def _(a):
        wide_ref[6:8, :] = beside_ref[a, z, :2]
        wide_ref[8 : 8 + ny, :] = source_ref[a, z]
        wide_ref[8 + ny : 10 + ny, :] = beside_ref[a, z, 2:]
        wide = wide_ref[...]
        change = roll(wide, -1, 0) + roll(wide, 1, 0) - 2.0 * wide
        change_ref[a] = change[8 : 8 + ny]


def second_x(rows):
    return roll(rows, -1, 1) + roll(rows, 1, 1) - 2.0 * rows


def is_odd():
    return lax.rem(lax.axis_index("gz"), 2)


def is_high():
    return lax.rem(1 + is_odd() + lax.axis_index("gy"), 2)


def prepare_kernel(block_ref, stiffness_ref, concentration_ref, mine_ref, other_ref, arrived):
    nz, ny, _ = concentration_ref.shape
    half = ny // 2
    odd, high = is_odd(), is_high()
    upper = pl.ds(pl.multiple_of(half * high, half), half)
    lower = pl.ds(pl.multiple_of(half * (1 - high), half), half)
    copies = []
    for z in range(nz):
        inward = z + odd * (nz - 1 - 2 * z)
        outward = nz - 1 - inward
        for layer, rows, target in ((inward, upper, mine_ref), (outward, lower, other_ref)):
            moves = (
                (block_ref.at[:, layer, rows, :], target.at[0:BLOCK, z]),
                (stiffness_ref.at[layer, rows, :], target.at[BLOCK, z]),
                (concentration_ref.at[layer, rows, :], target.at[BLOCK + 1, z]),
            )
            for source, place in moves:
                copies.append(pltpu.make_async_copy(source, place, arrived.at[len(copies)]))
    for copy in copies:
        copy.start()
    for copy in copies:
        copy.wait()


def prepare(block, stiffness, concentration):
    nz, ny, nx = concentration.shape
    shape = jax.ShapeDtypeStruct((BLOCK + 2, nz, ny // 2, nx), jnp.float32)
    return pl.pallas_call(
        prepare_kernel,
        out_shape=(shape, shape),
        in_specs=[pl.BlockSpec(memory_space=pltpu.HBM)] * 3,
        out_specs=[VMEM] * 2,
        scratch_shapes=[pltpu.SemaphoreType.DMA((6 * nz,))],
        compiler_params=pltpu.CompilerParams(vmem_limit_bytes=62 * 1024 * 1024),
        name="prepare",
    )(block, stiffness, concentration)


def first_local_kernel(block_ref, beside_ref, curvature_ref, stiffness_ref, tile_ref, wide_ref, change_ref):
    nz, ny, nx = curvature_ref.shape
    wide_ref[...] = jnp.zeros(wide_ref.shape, jnp.float32)
    gram = jnp.zeros((8 * BLOCK, 8 * BLOCK), jnp.float32)
    stiff = jnp.zeros((8 * BLOCK, 8 * BLOCK), jnp.float32)
    for z in range(nz):
        store_y_differences(block_ref, beside_ref, wide_ref, change_ref, z)
        for start in range(0, ny, 8):
            part = slice(start, start + 8)
            field = block_ref[:, z, part, :]
            weight = stiffness_ref[z, part, :][None]
            rows = rows_of(field)
            along_x = second_x(rows)
            along_y = change_ref[:, part, :]
            gram = gram + inner(rows, rows)
            stiff = stiff + inner(rows_of(field * curvature_ref[z, part, :][None]), rows)
            stiff = stiff + inner(rows_of(along_x.reshape(field.shape) * weight), along_x)
            stiff = stiff + inner(rows_of(along_y * weight), rows_of(along_y))
    half = 8 * HALF
    tile_ref[...] = (
        folded(gram[:half], 0)
        + folded(gram[half:], BLOCK)
        + folded(stiff[:half], 2 * BLOCK)
        + folded(stiff[half:], 3 * BLOCK)
    )


def edges(field, layers):
    high = is_high() == 1
    to_pair, to_core = [], []
    for u in range(layers):
        first, last = field(u)[:2], field(u)[-2:]
        to_pair.append(jnp.where(high, first, last))
        to_core.append(jnp.where(high, last, first))
    return to_pair[::-1], to_core


def edges_kernel(mine_ref, theirs_ref, pair_ref, core_ref):
    nz = mine_ref.shape[1]

    @pl.loop(0, BLOCK + 1)
    def _(a):
        field = lambda u: mine_ref[a, u] if u < nz else theirs_ref[a, u - nz]
        to_pair, to_core = edges(field, 2 * nz)
        for u in range(2 * nz):
            pair_ref[a, 2 * u : 2 * u + 2, :] = to_pair[u]
            core_ref[a, 2 * u : 2 * u + 2, :] = to_core[u]


def first_across_kernel(mine_ref, theirs_ref, beyond_ref, tile_ref, sum_ref):
    nz, ny = mine_ref.shape[1:3]
    half = 8 * HALF
    stiff = jnp.zeros((8 * BLOCK, 8 * BLOCK), jnp.float32)
    sources = [(mine_ref, z) for z in range(nz)] + [(theirs_ref, z) for z in range(nz)]
    sources = sources + [(beyond_ref, z) for z in range(2)]
    for u in range(1, 2 * nz + 1):
        for start in range(0, ny, 8):
            part = slice(start, start + 8)

            def layer(k):
                source, z = sources[k]
                return source[:BLOCK, z, part, :]

            source, z = sources[u]
            change = (layer(u + 1) + layer(u - 1)) - 2.0 * layer(u)
            weight = source[BLOCK, z, part, :]
            stiff = stiff + inner(rows_of(change * weight[None]), rows_of(change))
    sum_ref[...] = (
        tile_ref[...] + folded(stiff[:half], 2 * BLOCK) + folded(stiff[half:], 3 * BLOCK)
    )


def apply_hessian(field, layers, stiff_layers, u, curvature, wide, stiff_wide):
    def flux(k):
        return stiff_layers(k) * ((layers(k + 1) + layers(k - 1)) - 2.0 * layers(k))

    total = curvature * field + (flux(u + 1) + flux(u - 1) - 2.0 * flux(u))
    change = second_x(stiff_layers(u) * second_x(field))
    total = total + change
    change = stiff_wide * (roll(wide, -1, 0) + roll(wide, 1, 0) - 2.0 * wide)
    change = roll(change, -1, 0) + roll(change, 1, 0) - 2.0 * change
    return total + change[8 : 8 + field.shape[0]]


def store_wide(wide_ref, index, field, pair_rows, core_rows):
    ny = field.shape[0]
    high = is_high() == 1
    wide_ref[index, 6:8, :] = jnp.where(high, pair_rows, core_rows)
    wide_ref[index, 8 : 8 + ny, :] = field
    wide_ref[index, 8 + ny : 10 + ny, :] = jnp.where(high, core_rows, pair_rows)


def first_images_kernel(
    mine_ref, theirs_ref, behind_ref, beyond_ref, pair_ref, core_ref,
    images_ref, inverse_ref, curvature_ref, stiff_layers_ref, stiff_wide_ref, wide_ref,
):
    depth, ny, nx = curvature_ref.shape
    nz = depth // 2
    wide_ref[...] = jnp.zeros(wide_ref.shape, jnp.float32)
    stiff_wide_ref[...] = jnp.zeros(stiff_wide_ref.shape, jnp.float32)
    sources = [(behind_ref, nz - 2), (behind_ref, nz - 1)]
    sources = sources + [(mine_ref, z) for z in range(nz)] + [(theirs_ref, z) for z in range(nz)]
    sources = sources + [(beyond_ref, 0), (beyond_ref, 1)]
    for k in range(depth + 2):
        source, z = sources[k + 1]
        stiff_layers_ref[k] = source[BLOCK, z]
    for u in range(depth):
        rows = slice(2 * u, 2 * u + 2)
        stiff = stiff_layers_ref[u + 1]
        store_wide(stiff_wide_ref, u, stiff, pair_ref[BLOCK, rows, :], core_ref[BLOCK, rows, :])
        source, z = sources[u + 2]
        concentration = source[BLOCK + 1, z]
        curvature = 3.0 * concentration * concentration - 1.0
        curvature_ref[u] = curvature
        total = (curvature + 2.0) + 12.0 * stiff
        total = total + (stiff_layers_ref[u] + stiff_layers_ref[u + 2])
        total = total + (stiff_wide_ref[u, 7 : 7 + ny, :] + stiff_wide_ref[u, 9 : 9 + ny, :])
        total = total + (roll(stiff, -1, 1) + roll(stiff, 1, 1))
        inverse_ref[u] = 1.0 / total

    @pl.loop(0, BLOCK)
    def _(a):
        layers = [source[a, z] for source, z in sources]
        for u in range(depth):
            rows = slice(2 * u, 2 * u + 2)
            store_wide(wide_ref, u, layers[u + 2], pair_ref[a, rows, :], core_ref[a, rows, :])
            images_ref[a, u] = apply_hessian(
                layers[u + 2], lambda k: layers[k + 2], lambda k: stiff_layers_ref[k + 1], u,
                curvature_ref[u], wide_ref[u], stiff_wide_ref[u],
            )


def update_kernel(
    mix_ref, theta_ref, mine_ref, theirs_ref, search_images_ref, inverse_ref,
    modes_ref, images_ref, near_ref, far_ref, to_pair_ref, to_core_ref,
):
    depth, ny, nx = inverse_ref.shape
    nz = depth // 2
    for start in range(0, nx, LANES):
        lanes = slice(start, start + LANES)
        for u in range(depth):
            source, z = (mine_ref, u) if u < nz else (theirs_ref, u - nz)
            vectors = [source[a, z, :, lanes] for a in range(BLOCK)]
            images = [search_images_ref[a, u, :, lanes] for a in range(BLOCK)]
            inverse = inverse_ref[u, :, lanes]
            for j in range(MODES):
                mode = mix_ref[j, 0:1, :] * vectors[0]
                image = mix_ref[j, 0:1, :] * images[0]
                for a in range(1, BLOCK):
                    mode = mode + mix_ref[j, a : a + 1, :] * vectors[a]
                    image = image + mix_ref[j, a : a + 1, :] * images[a]
                modes_ref[j, u, :, lanes] = mode
                images_ref[j, u, :, lanes] = image
                correction = (image - theta_ref[j : j + 1, :] * mode) * inverse
                if u < nz:
                    near_ref[j, u, :, lanes] = correction
                else:
                    far_ref[j, u - nz, :, lanes] = correction

    @pl.loop(0, MODES)
    def _(j):
        field = lambda u: near_ref[j, u] if u < nz else far_ref[j, u - nz]
        to_pair, to_core = edges(field, depth)
        for u in range(depth):
            to_pair_ref[j, 2 * u : 2 * u + 2, :] = to_pair[u]
            to_core_ref[j, 2 * u : 2 * u + 2, :] = to_core[u]


def second_local_kernel(modes_ref, images_ref, near_ref, far_ref, curvature_ref, stiff_layers_ref, tile_ref):
    depth, ny, nx = curvature_ref.shape
    nz = depth // 2
    half = 8 * HALF
    products = jnp.zeros((4 * half, 3 * half), jnp.float32)
    low = jnp.zeros((half, half), jnp.float32)
    for u in range(depth):
        for start in range(0, ny, 8):
            part = slice(start, start + 8)
            field = near_ref[:, u, part, :] if u < nz else far_ref[:, u - nz, part, :]
            weight = stiff_layers_ref[u + 1, part, :][None]
            second = rows_of(field)
            rows = jnp.concatenate([rows_of(modes_ref[:, u, part, :]), second], axis=0)
            images = rows_of(images_ref[:, u, part, :])
            along_x = second_x(second)
            bent = rows_of(field * curvature_ref[u, part, :][None])
            products = products + inner(
                jnp.concatenate([rows, bent, images], axis=0), jnp.concatenate([rows, images], axis=0)
            )
            low = low + inner(rows_of(along_x.reshape(field.shape) * weight), along_x)
    gram = products[: 2 * half, : 2 * half]
    back = products[half : 2 * half, 2 * half :]
    low = low + products[2 * half : 3 * half, half : 2 * half]
    cross = products[3 * half :, : 2 * half]
    tile_ref[...] = (
        folded(gram[:half], 0)
        + folded(gram[half:], BLOCK)
        + folded(cross, 2 * BLOCK)
        + (folded(back, 3 * BLOCK) + folded(low, 3 * BLOCK + HALF))
    )


def second_across_kernel(
    near_ref, far_ref, beyond_ref, pair_ref, core_ref, stiff_layers_ref, tile_ref,
    sum_ref, wide_ref, change_ref,
):
    nz, ny = near_ref.shape[1:3]
    depth = 2 * nz
    wide_ref[...] = jnp.zeros(wide_ref.shape, jnp.float32)
    sources = [(near_ref, z) for z in range(nz)] + [(far_ref, z) for z in range(nz)]
    sources = sources + [(beyond_ref, 0), (beyond_ref, 1)]

    @pl.loop(0, MODES)
    def _(j):
        for u in range(depth):
            source, z = sources[u]
            rows = slice(2 * u, 2 * u + 2)
            store_wide(wide_ref, u, source[j, z], pair_ref[j, rows, :], core_ref[j, rows, :])
            wide = wide_ref[u]
            change = roll(wide, -1, 0) + roll(wide, 1, 0) - 2.0 * wide
            change_ref[j, u] = change[8 : 8 + ny]

    low = jnp.zeros((8 * MODES, 8 * MODES), jnp.float32)
    for u in range(depth):
        for start in range(0, ny, 8):
            part = slice(start, start + 8)

            def layer(k):
                source, z = sources[k]
                return source[:, z, part, :]

            change = change_ref[:, u, part, :]
            weight = stiff_layers_ref[u + 1, part, :][None]
            low = low + inner(rows_of(change * weight), rows_of(change))
            change = (layer(u + 2) + layer(u)) - 2.0 * layer(u + 1)
            weight = stiff_layers_ref[u + 2, part, :][None]
            low = low + inner(rows_of(change * weight), rows_of(change))
    sum_ref[...] = tile_ref[...] + folded(low, 3 * BLOCK + HALF)


def images_kernel(
    near_ref, far_ref, behind_ref, beyond_ref, pair_ref, core_ref,
    curvature_ref, stiff_layers_ref, stiff_wide_ref, images_ref, wide_ref,
):
    depth, ny, nx = curvature_ref.shape
    nz = depth // 2
    wide_ref[...] = jnp.zeros(wide_ref.shape, jnp.float32)
    sources = [(behind_ref, nz - 2), (behind_ref, nz - 1)]
    sources = sources + [(near_ref, z) for z in range(nz)] + [(far_ref, z) for z in range(nz)]
    sources = sources + [(beyond_ref, 0), (beyond_ref, 1)]

    @pl.loop(0, MODES)
    def _(j):
        layers = [source[j, z] for source, z in sources]
        for u in range(depth):
            rows = slice(2 * u, 2 * u + 2)
            store_wide(wide_ref, u, layers[u + 2], pair_ref[j, rows, :], core_ref[j, rows, :])
            images_ref[j, u] = apply_hessian(
                layers[u + 2], lambda k: layers[k + 2], lambda k: stiff_layers_ref[k + 1], u,
                curvature_ref[u], wide_ref[u], stiff_wide_ref[u],
            )


def density_kernel(
    factor, offset, mix_ref, theta_ref, modes_ref, corrections_ref, first_ref, second_ref, density_ref,
):
    nz, ny, nx = density_ref.shape[1:]
    for layer in range(nz):
        u = offset + layer
        place = layer if offset == 0 else nz - 1 - layer
        for start in range(0, nx, LANES):
            lanes = slice(start, start + LANES)
            vectors = [modes_ref[a, u, :, lanes] for a in range(MODES)]
            vectors = vectors + [corrections_ref[a, layer, :, lanes] for a in range(MODES)]
            images = [first_ref[a, u, :, lanes] for a in range(MODES)]
            images = images + [second_ref[a, u, :, lanes] for a in range(MODES)]
            mode_sum = jnp.zeros((ny, LANES), jnp.float32)
            residual_sum = jnp.zeros((ny, LANES), jnp.float32)
            for j in range(MODES):
                mode = mix_ref[j, 0:1, :] * vectors[0]
                image = mix_ref[j, 0:1, :] * images[0]
                for a in range(1, BLOCK):
                    mode = mode + mix_ref[j, a : a + 1, :] * vectors[a]
                    image = image + mix_ref[j, a : a + 1, :] * images[a]
                residual = image - theta_ref[j : j + 1, :] * mode
                mode_sum = mode_sum + mode * mode
                residual_sum = residual_sum + residual * residual
            density_ref[0, place, :, lanes] = factor * mode_sum
            density_ref[1, place, :, lanes] = factor * residual_sum


def merge_kernel(mine_ref, other_ref, modes_ref, residuals_ref):
    nz, ny, _ = modes_ref.shape
    half = ny // 2
    odd, high = is_odd() == 1, is_high() == 1
    for k, target in ((0, modes_ref), (1, residuals_ref)):
        for z in range(nz):
            mine = jnp.where(odd, mine_ref[k, nz - 1 - z], mine_ref[k, z])
            other = jnp.where(odd, other_ref[k, nz - 1 - z], other_ref[k, z])
            target[z, :half, :] = jnp.where(high, other, mine)
            target[z, half:, :] = jnp.where(high, mine, other)


def local(initial_block, concentration, stiffness):
    nz, ny, nx = concentration.shape
    half = ny // 2
    depth = 2 * nz
    cells_total = nz * ny * nx * lax.axis_size("gz") * lax.axis_size("gy")
    vector_rows = (BLOCK + 1, 2 * depth, nx)
    plane = (depth, half, nx)
    wide = (depth, half + 16, nx)
    mode_plane = (MODES,) + plane
    mode_half = (MODES, nz, half, nx)
    mode_rows = (MODES, 2 * depth, nx)

    mine, other = prepare(initial_block, stiffness, concentration)
    theirs = pair_swap(other)
    beyond = from_beyond(mine[:, :2])
    edge_rows = jnp.concatenate([initial_block[:, :, ny - 2 :], initial_block[:, :, :2]], axis=2)
    beside = core_swap(edge_rows)
    curvature = 3.0 * concentration * concentration - 1.0
    (tile,) = call(
        first_local_kernel,
        [(8, LANES)],
        [initial_block, beside, curvature, stiffness],
        scratch=[pltpu.VMEM((ny + 16, nx), jnp.float32), pltpu.VMEM((BLOCK, ny, nx), jnp.float32)],
        flops=100000000,
        name="first_local",
    )
    theirs, tile = lax.optimization_barrier((theirs, tile))
    to_pair, to_core = call(
        edges_kernel, [vector_rows, vector_rows], [mine, theirs], name="edges"
    )
    core_rows = core_swap(to_core)
    pair_rows = pair_swap(to_pair)
    held, beyond, to_pair, to_core = lax.optimization_barrier((theirs, beyond, to_pair, to_core))
    behind = from_behind(held[:, nz - 2 :])
    (tile,) = call(
        first_across_kernel,
        [(8, LANES)],
        [mine, theirs, beyond, tile],
        flops=25000000,
        name="first_across",
    )
    pencil, (behind, pair_rows, core_rows) = grid_sum(
        tile, (behind, pair_rows, core_rows), by_four=False
    )
    search_images, inverse, curvature, stiff_layers, stiff_wide = call(
        first_images_kernel,
        [(BLOCK,) + plane, plane, plane, (depth + 2, half, nx), wide],
        [mine, theirs, behind, beyond, pair_rows, core_rows],
        scratch=[pltpu.VMEM(wide, jnp.float32)],
        flops=6000000,
        name="first_images",
    )
    _, theta_rows, mix = ritz_pairs(pencil)
    modes, mode_images, near, far, to_pair, to_core = call(
        update_kernel,
        [mode_plane, mode_plane, mode_half, mode_half, mode_rows, mode_rows],
        [mix, theta_rows, mine, theirs, search_images, inverse],
        name="update",
    )

    beyond = from_beyond(near[:, :2])
    pair_rows = pair_swap(to_pair)
    core_rows = core_swap(to_core)
    (tile,) = call(
        second_local_kernel,
        [(8, LANES)],
        [modes, mode_images, near, far, curvature, stiff_layers],
        flops=80000000,
        name="second_local",
    )
    held, beyond, pair_rows, core_rows, tile = lax.optimization_barrier(
        (far, beyond, pair_rows, core_rows, tile)
    )
    behind = from_behind(held[:, nz - 2 :])
    (tile,) = call(
        second_across_kernel,
        [(8, LANES)],
        [near, far, beyond, pair_rows, core_rows, stiff_layers, tile],
        scratch=[pltpu.VMEM(wide, jnp.float32), pltpu.VMEM(mode_plane, jnp.float32)],
        flops=25000000,
        name="second_across",
    )
    pencil, behind = grid_sum(tile, behind, by_four=True)
    (correction_images,) = call(
        images_kernel,
        [mode_plane],
        [near, far, behind, beyond, pair_rows, core_rows, curvature, stiff_layers, stiff_wide],
        scratch=[pltpu.VMEM(wide, jnp.float32)],
        name="images",
    )
    theta, theta_rows, mix = ritz_pairs(pencil)
    shares = []
    for offset, corrections in ((nz, far), (0, near)):
        (share,) = call(
            functools.partial(density_kernel, float(cells_total / MODES), offset),
            [(2, nz, half, nx)],
            [mix, theta_rows, modes, corrections, mode_images, correction_images],
            name="densities",
        )
        shares.append(share)
    other = pair_swap(shares[0])
    mode_density, residual_density = call(
        merge_kernel, [(nz, ny, nx)] * 2, [shares[1], other], name="merge"
    )
    return (theta, mode_density, residual_density)


def solution(mesh):
    return jax.shard_map(
        local,
        mesh=mesh,
        in_specs=(P("img", "gz", "gy", None), P(("img", "gz"), "gy", None), P("gz", "gy", None)),
        out_specs=(P("img"), P(("img", "gz"), "gy", None), P(("img", "gz"), "gy", None)),
        check_vma=False,
    )
```

```python
import functools

import jax
import jax.numpy as jnp
from jax import lax
from jax.experimental import pallas as pl
from jax.experimental.pallas import tpu as pltpu
from jax.sharding import PartitionSpec as P

BLOCK = 16
MODES = 8
HALF = BLOCK // 2
LANES = 128
EARLY_SWEEPS = 4
MAX_SWEEPS = 14
HIGHEST = lax.Precision.HIGHEST
VMEM = pl.BlockSpec(memory_space=pltpu.VMEM)


def call(kernel, out_shapes, args, scratch=(), flops=1000000, name=None):
    out_shape = tuple(jax.ShapeDtypeStruct(s, jnp.float32) for s in out_shapes)
    moved = 4 * sum(x.size for x in list(args) + list(out_shape))
    return pl.pallas_call(
        kernel,
        out_shape=out_shape,
        in_specs=[VMEM] * len(args),
        out_specs=[VMEM] * len(out_shape),
        scratch_shapes=list(scratch),
        compiler_params=pltpu.CompilerParams(vmem_limit_bytes=40 * 1024 * 1024),
        cost_estimate=pl.CostEstimate(flops=flops, bytes_accessed=moved, transcendentals=0),
        name=name,
    )(*args)


def pair_swap(x):
    return lax.ppermute(x, "gz", [(i, i ^ 1) for i in range(lax.axis_size("gz"))])


def core_swap(x):
    return lax.ppermute(x, "gy", [(0, 1), (1, 0)])


def from_beyond(x):
    size = lax.axis_size("gz")
    return lax.ppermute(x, "gz", [((i + (2 if i % 2 == 0 else size - 2)) % size, i) for i in range(size)])


def from_behind(x):
    size = lax.axis_size("gz")
    return lax.ppermute(x, "gz", [((i + (size - 2 if i % 2 == 0 else 2)) % size, i) for i in range(size)])


def grid_sum(x, later, by_four):
    axes = ("gz", "gy")
    total = lax.axis_size("gz") * lax.axis_size("gy")
    if total & (total - 1):
        return lax.psum(x, axes), later

    def other(mask):
        return lax.ppermute(x, axes, [(i, i ^ mask) for i in range(total)])

    mask = 1
    while mask < total:
        wide = by_four and mask >= 4 and 4 * mask <= total
        if mask * (4 if wide else 2) == total:
            x, later = lax.optimization_barrier((x, later))
        if wide:
            x = (x + other(mask)) + (other(2 * mask) + other(3 * mask))
            mask *= 4
        else:
            x = x + other(mask)
            mask *= 2
    return x, later


def spread_rows(x, k):
    return jnp.broadcast_to(x[k : k + 1, :], (8, LANES))


def every_row(x):
    x = x + pltpu.roll(x, 4, 0)
    x = x + pltpu.roll(x, 2, 0)
    return x + pltpu.roll(x, 1, 0)


def packed_sums(tiles, row):
    low4, low2, low1 = row < 4, (row & 2) == 0, (row & 1) == 0
    tiles = [
        jnp.where(low4, tiles[k], tiles[k + 4])
        + pltpu.roll(jnp.where(low4, tiles[k + 4], tiles[k]), 4, 0)
        for k in range(4)
    ]

    def fold(a, b, low, step):
        other = jnp.where(low, b, a)
        moved = jnp.where(low, pltpu.roll(other, 8 - step, 0), pltpu.roll(other, step, 0))
        return jnp.where(low, a, b) + moved

    tiles = [fold(tiles[k], tiles[k + 2], low2, 2) for k in range(2)]
    return fold(tiles[0], tiles[1], low1, 1)


def tournament():
    players = list(range(BLOCK))
    rounds = []
    for _ in range(BLOCK - 1):
        rounds.append([(players[k], players[BLOCK - 1 - k]) for k in range(HALF)])
        players = [players[0], players[-1]] + players[1:-1]
    return rounds


def ritz_kernel(pencil_ref, theta_ref, theta_rows_ref, mix_ref):
    total = pencil_ref[...]
    row = lax.broadcasted_iota(jnp.int32, (8, LANES), 0)
    lane = lax.broadcasted_iota(jnp.int32, (8, LANES), 1)

    def columns(upper, lower):
        return (
            [jnp.broadcast_to(upper[:, k : k + 1], (8, LANES)) for k in range(BLOCK)],
            [jnp.broadcast_to(lower[:, k : k + 1], (8, LANES)) for k in range(BLOCK)],
        )

    def entry(upper, lower, k):
        return spread_rows(upper, k) if k < 8 else spread_rows(lower, k - 8)

    gram_u, gram_l = columns(total[:, :BLOCK], total[:, BLOCK : 2 * BLOCK])
    zero = jnp.zeros((8, LANES), jnp.float32)
    inverse_u = [jnp.where(row == k, 1.0, 0.0).astype(jnp.float32) for k in range(8)] + [zero] * 8
    inverse_l = [zero] * 8 + [
        jnp.where(row == k, 1.0, 0.0).astype(jnp.float32) for k in range(8)
    ]
    for k in range(BLOCK):
        root = lax.rsqrt(entry(gram_u[k], gram_l[k], k))
        gram_u[k] = gram_u[k] * root
        gram_l[k] = gram_l[k] * root
        inverse_u[k] = inverse_u[k] * root
        inverse_l[k] = inverse_l[k] * root
        for i in range(k + 1, BLOCK):
            factor = entry(gram_u[k], gram_l[k], i)
            if i < 8:
                gram_u[i] = gram_u[i] - factor * gram_u[k]
            gram_l[i] = gram_l[i] - factor * gram_l[k]
            inverse_u[i] = inverse_u[i] - factor * inverse_u[k]
            if k >= 8:
                inverse_l[i] = inverse_l[i] - factor * inverse_l[k]
    transposed_u, transposed_l = zero, zero
    for k in range(BLOCK):
        transposed_u = jnp.where(lane == k, inverse_u[k], transposed_u)
        transposed_l = jnp.where(lane == k, inverse_l[k], transposed_l)
    transposed = jnp.concatenate([transposed_u, transposed_l], axis=0)[:, :BLOCK]

    dot = functools.partial(
        lax.dot_general, precision=HIGHEST, preferred_element_type=jnp.float32
    )
    stiff = jnp.concatenate(
        [total[:, 2 * BLOCK : 3 * BLOCK], total[:, 3 * BLOCK : 4 * BLOCK]], axis=0
    )
    half_way = dot(stiff, transposed, (((1,), (0,)), ((), ())))
    projected = dot(transposed, half_way, (((0,), (0,)), ((), ())))

    upper, lower = columns(projected[:8], projected[8:])
    diagonal = zero
    for k in range(8):
        diagonal = diagonal + jnp.where(row == k, upper[k] + lower[k + 8], 0.0)
    mean = every_row(diagonal) * (1.0 / BLOCK)
    size = zero
    for k in range(8):
        upper[k] = upper[k] - jnp.where(row == k, mean, 0.0)
        lower[k + 8] = lower[k + 8] - jnp.where(row == k, mean, 0.0)
    for k in range(BLOCK):
        size = size + (upper[k] * upper[k] + lower[k] * lower[k])
    scale = 1.25 * jnp.sqrt(every_row(size)) + 1e-30
    shrink = 1.0 / scale
    for k in range(BLOCK):
        upper[k] = upper[k] * shrink
        lower[k] = lower[k] * shrink
    for k in range(8):
        upper[k] = upper[k] + jnp.where(row == k, 1.0, 0.0)
        lower[k + 8] = lower[k + 8] + jnp.where(row == k, 1.0, 0.0)

    def squares(upper, lower):
        top = packed_sums([upper[k] * upper[k] + lower[k] * lower[k] for k in range(8)], row)
        bottom = packed_sums(
            [upper[15 - k] * upper[15 - k] + lower[15 - k] * lower[15 - k] for k in range(8)], row
        )
        return top, bottom

    def sweep(upper, lower):
        upper, lower = list(upper), list(lower)
        top, bottom = squares(upper, lower)
        worst = zero
        for pairs in tournament():
            g = packed_sums([upper[i] * upper[j] + lower[i] * lower[j] for i, j in pairs], row)
            d = bottom - top
            g2 = g * g
            worst = jnp.maximum(worst, g2)
            dd = jnp.maximum(jnp.abs(d), 1e-18)
            ih = lax.rsqrt(g2 + 0.25 * (dd * dd))
            c2 = 0.5 + (0.25 * dd) * ih
            ic = lax.rsqrt(c2)
            c = c2 * ic
            s = (jnp.where(d >= 0.0, 0.5, -0.5) * g) * (ih * ic)
            move = (s * ic) * g
            top = top - move
            bottom = bottom + move
            for k, (i, j) in enumerate(pairs):
                ck, sk = spread_rows(c, k), spread_rows(s, k)
                ui, uj, li, lj = upper[i], upper[j], lower[i], lower[j]
                upper[i] = ck * ui - sk * uj
                lower[i] = ck * li - sk * lj
                upper[j] = sk * ui + ck * uj
                lower[j] = sk * li + ck * lj
            next_top = jnp.where(
                row == 0, top, jnp.where(row == 1, pltpu.roll(bottom, 1, 0), pltpu.roll(top, 1, 0))
            )
            bottom = jnp.where(row == 7, top, pltpu.roll(bottom, 7, 0))
            top = next_top
        return worst, tuple(upper), tuple(lower)

    def early(_, carry):
        return sweep(*carry)[1:]

    def late(carry):
        count, _, upper, lower = carry
        worst, upper, lower = sweep(upper, lower)
        for step in (4, 2, 1):
            worst = jnp.maximum(worst, pltpu.roll(worst, step, 0))
        return count + 1, worst[0, 0], upper, lower

    def unfinished(carry):
        count, worst, _, _ = carry
        return jnp.logical_and(count < MAX_SWEEPS, worst > 1.6e-7)

    upper, lower = lax.fori_loop(0, EARLY_SWEEPS, early, (tuple(upper), tuple(lower)))
    _, _, upper, lower = lax.while_loop(
        unfinished, late, (jnp.int32(EARLY_SWEEPS), jnp.float32(1.0), upper, lower)
    )

    top, bottom = squares(upper, lower)
    rank_top, rank_bottom = zero, zero
    for k in range(BLOCK):
        mine = spread_rows(top, k) if k < 8 else spread_rows(bottom, 15 - k)
        before_top = (mine < top) | ((mine == top) & (k < row))
        before_bottom = (mine < bottom) | ((mine == bottom) & (k < 15 - row))
        rank_top = rank_top + jnp.where(before_top, 1.0, 0.0)
        rank_bottom = rank_bottom + jnp.where(before_bottom, 1.0, 0.0)
    inverse_top, inverse_bottom = lax.rsqrt(top), lax.rsqrt(bottom)
    value_top, value_bottom = top * inverse_top, bottom * inverse_bottom
    lane_float = lane.astype(jnp.float32)
    theta = zero
    vectors_u, vectors_l = zero, zero
    for k in range(BLOCK):

        def of(first, second):
            return spread_rows(first, k) if k < 8 else spread_rows(second, 15 - k)

        here = lane_float == of(rank_top, rank_bottom)
        inverse_norm = of(inverse_top, inverse_bottom)
        theta = jnp.where(here, of(value_top, value_bottom), theta)
        vectors_u = jnp.where(here, upper[k] * inverse_norm, vectors_u)
        vectors_l = jnp.where(here, lower[k] * inverse_norm, vectors_l)
    theta = mean + scale * (theta - 1.0)
    theta_ref[...] = theta[0, :MODES]
    on_row = jnp.sum(jnp.where(row == lane, theta, 0.0), axis=1, keepdims=True)
    theta_rows_ref[...] = jnp.broadcast_to(on_row, (8, LANES))
    vectors = jnp.concatenate([vectors_u, vectors_l], axis=0)
    mix = dot(transposed, vectors, (((1,), (0,)), ((), ())))
    for j in range(MODES):
        mix_ref[j] = jnp.broadcast_to(mix[:, j : j + 1], (BLOCK, LANES))


def ritz_pairs(pencil):
    return call(
        ritz_kernel,
        [(MODES,), (8, LANES), (MODES, BLOCK, LANES)],
        [pencil],
        flops=10000000,
        name="ritz_pairs",
    )


def inner(a, b):
    return lax.dot_general(
        a, b, (((1,), (1,)), ((), ())), precision=HIGHEST, preferred_element_type=jnp.float32
    )


def folded(products, offset):
    height, width = products.shape
    row = lax.broadcasted_iota(jnp.int32, (height, width), 0)
    column = lax.broadcasted_iota(jnp.int32, (height, width), 1)
    same = jnp.where((row & 7) == (column & 7), products, 0.0)
    sums = jnp.sum(same.reshape(height // 8, 8, width), axis=1)
    row = lax.broadcasted_iota(jnp.int32, (width, LANES), 0)
    lane = lax.broadcasted_iota(jnp.int32, (width, LANES), 1)
    place = jnp.where((row >> 3) + offset == lane, 1.0, 0.0).astype(jnp.float32)
    return jnp.dot(sums, place, precision=HIGHEST, preferred_element_type=jnp.float32)


def rows_of(x):
    return x.reshape(x.shape[0] * x.shape[1], x.shape[2])


def roll(x, shift, axis):
    return pltpu.roll(x, shift % x.shape[axis], axis)


def store_y_differences(source_ref, beside_ref, wide_ref, change_ref, z):
    count, _, ny, _ = source_ref.shape

    @pl.loop(0, count)
    def _(a):
        wide_ref[6:8, :] = beside_ref[a, z, :2]
        wide_ref[8 : 8 + ny, :] = source_ref[a, z]
        wide_ref[8 + ny : 10 + ny, :] = beside_ref[a, z, 2:]
        wide = wide_ref[...]
        change = roll(wide, -1, 0) + roll(wide, 1, 0) - 2.0 * wide
        change_ref[a] = change[8 : 8 + ny]


def second_x(rows):
    return roll(rows, -1, 1) + roll(rows, 1, 1) - 2.0 * rows


def is_odd():
    return lax.rem(lax.axis_index("gz"), 2)


def is_high():
    return lax.rem(1 + is_odd() + lax.axis_index("gy"), 2)


def prepare_kernel(block_ref, stiffness_ref, concentration_ref, mine_ref, other_ref, arrived):
    nz, ny, _ = concentration_ref.shape
    half = ny // 2
    odd, high = is_odd(), is_high()
    upper = pl.ds(pl.multiple_of(half * high, half), half)
    lower = pl.ds(pl.multiple_of(half * (1 - high), half), half)
    copies = []
    for z in range(nz):
        inward = z + odd * (nz - 1 - 2 * z)
        outward = nz - 1 - inward
        for layer, rows, target in ((inward, upper, mine_ref), (outward, lower, other_ref)):
            moves = (
                (block_ref.at[:, layer, rows, :], target.at[0:BLOCK, z]),
                (stiffness_ref.at[layer, rows, :], target.at[BLOCK, z]),
                (concentration_ref.at[layer, rows, :], target.at[BLOCK + 1, z]),
            )
            for source, place in moves:
                copies.append(pltpu.make_async_copy(source, place, arrived.at[len(copies)]))
    for copy in copies:
        copy.start()
    for copy in copies:
        copy.wait()


def prepare(block, stiffness, concentration):
    nz, ny, nx = concentration.shape
    shape = jax.ShapeDtypeStruct((BLOCK + 2, nz, ny // 2, nx), jnp.float32)
    return pl.pallas_call(
        prepare_kernel,
        out_shape=(shape, shape),
        in_specs=[pl.BlockSpec(memory_space=pltpu.HBM)] * 3,
        out_specs=[VMEM] * 2,
        scratch_shapes=[pltpu.SemaphoreType.DMA((6 * nz,))],
        compiler_params=pltpu.CompilerParams(vmem_limit_bytes=62 * 1024 * 1024),
        name="prepare",
    )(block, stiffness, concentration)


def first_local_kernel(block_ref, beside_ref, curvature_ref, stiffness_ref, tile_ref, wide_ref, change_ref):
    nz, ny, nx = curvature_ref.shape
    wide_ref[...] = jnp.zeros(wide_ref.shape, jnp.float32)
    gram = jnp.zeros((8 * BLOCK, 8 * BLOCK), jnp.float32)
    stiff = jnp.zeros((8 * BLOCK, 8 * BLOCK), jnp.float32)
    for z in range(nz):
        store_y_differences(block_ref, beside_ref, wide_ref, change_ref, z)
        for start in range(0, ny, 8):
            part = slice(start, start + 8)
            field = block_ref[:, z, part, :]
            weight = stiffness_ref[z, part, :][None]
            rows = rows_of(field)
            along_x = second_x(rows)
            along_y = change_ref[:, part, :]
            gram = gram + inner(rows, rows)
            stiff = stiff + inner(rows_of(field * curvature_ref[z, part, :][None]), rows)
            stiff = stiff + inner(rows_of(along_x.reshape(field.shape) * weight), along_x)
            stiff = stiff + inner(rows_of(along_y * weight), rows_of(along_y))
    half = 8 * HALF
    tile_ref[...] = (
        folded(gram[:half], 0)
        + folded(gram[half:], BLOCK)
        + folded(stiff[:half], 2 * BLOCK)
        + folded(stiff[half:], 3 * BLOCK)
    )


def edges(field, layers):
    high = is_high() == 1
    to_pair, to_core = [], []
    for u in range(layers):
        first, last = field(u)[:2], field(u)[-2:]
        to_pair.append(jnp.where(high, first, last))
        to_core.append(jnp.where(high, last, first))
    return to_pair[::-1], to_core


def edges_kernel(mine_ref, theirs_ref, pair_ref, core_ref):
    nz = mine_ref.shape[1]

    @pl.loop(0, BLOCK + 1)
    def _(a):
        field = lambda u: mine_ref[a, u] if u < nz else theirs_ref[a, u - nz]
        to_pair, to_core = edges(field, 2 * nz)
        for u in range(2 * nz):
            pair_ref[a, 2 * u : 2 * u + 2, :] = to_pair[u]
            core_ref[a, 2 * u : 2 * u + 2, :] = to_core[u]


def first_across_kernel(mine_ref, theirs_ref, beyond_ref, tile_ref, sum_ref):
    nz, ny = mine_ref.shape[1:3]
    half = 8 * HALF
    stiff = jnp.zeros((8 * BLOCK, 8 * BLOCK), jnp.float32)
    sources = [(mine_ref, z) for z in range(nz)] + [(theirs_ref, z) for z in range(nz)]
    sources = sources + [(beyond_ref, z) for z in range(2)]
    for u in range(1, 2 * nz + 1):
        for start in range(0, ny, 8):
            part = slice(start, start + 8)

            def layer(k):
                source, z = sources[k]
                return source[:BLOCK, z, part, :]

            source, z = sources[u]
            change = (layer(u + 1) + layer(u - 1)) - 2.0 * layer(u)
            weight = source[BLOCK, z, part, :]
            stiff = stiff + inner(rows_of(change * weight[None]), rows_of(change))
    sum_ref[...] = (
        tile_ref[...] + folded(stiff[:half], 2 * BLOCK) + folded(stiff[half:], 3 * BLOCK)
    )


def apply_hessian(field, layers, stiff_layers, u, curvature, wide, stiff_wide):
    def flux(k):
        return stiff_layers(k) * ((layers(k + 1) + layers(k - 1)) - 2.0 * layers(k))

    total = curvature * field + (flux(u + 1) + flux(u - 1) - 2.0 * flux(u))
    change = second_x(stiff_layers(u) * second_x(field))
    total = total + change
    change = stiff_wide * (roll(wide, -1, 0) + roll(wide, 1, 0) - 2.0 * wide)
    change = roll(change, -1, 0) + roll(change, 1, 0) - 2.0 * change
    return total + change[8 : 8 + field.shape[0]]


def store_wide(wide_ref, index, field, pair_rows, core_rows):
    ny = field.shape[0]
    high = is_high() == 1
    wide_ref[index, 6:8, :] = jnp.where(high, pair_rows, core_rows)
    wide_ref[index, 8 : 8 + ny, :] = field
    wide_ref[index, 8 + ny : 10 + ny, :] = jnp.where(high, core_rows, pair_rows)


def first_images_kernel(
    mine_ref, theirs_ref, behind_ref, beyond_ref, pair_ref, core_ref,
    images_ref, inverse_ref, curvature_ref, stiff_layers_ref, stiff_wide_ref, wide_ref,
):
    depth, ny, nx = curvature_ref.shape
    nz = depth // 2
    wide_ref[...] = jnp.zeros(wide_ref.shape, jnp.float32)
    stiff_wide_ref[...] = jnp.zeros(stiff_wide_ref.shape, jnp.float32)
    sources = [(behind_ref, nz - 2), (behind_ref, nz - 1)]
    sources = sources + [(mine_ref, z) for z in range(nz)] + [(theirs_ref, z) for z in range(nz)]
    sources = sources + [(beyond_ref, 0), (beyond_ref, 1)]
    for k in range(depth + 2):
        source, z = sources[k + 1]
        stiff_layers_ref[k] = source[BLOCK, z]
    for u in range(depth):
        rows = slice(2 * u, 2 * u + 2)
        stiff = stiff_layers_ref[u + 1]
        store_wide(stiff_wide_ref, u, stiff, pair_ref[BLOCK, rows, :], core_ref[BLOCK, rows, :])
        source, z = sources[u + 2]
        concentration = source[BLOCK + 1, z]
        curvature = 3.0 * concentration * concentration - 1.0
        curvature_ref[u] = curvature
        total = (curvature + 2.0) + 12.0 * stiff
        total = total + (stiff_layers_ref[u] + stiff_layers_ref[u + 2])
        total = total + (stiff_wide_ref[u, 7 : 7 + ny, :] + stiff_wide_ref[u, 9 : 9 + ny, :])
        total = total + (roll(stiff, -1, 1) + roll(stiff, 1, 1))
        inverse_ref[u] = 1.0 / total

    @pl.loop(0, BLOCK)
    def _(a):
        layers = [source[a, z] for source, z in sources]
        for u in range(depth):
            rows = slice(2 * u, 2 * u + 2)
            store_wide(wide_ref, u, layers[u + 2], pair_ref[a, rows, :], core_ref[a, rows, :])
            images_ref[a, u] = apply_hessian(
                layers[u + 2], lambda k: layers[k + 2], lambda k: stiff_layers_ref[k + 1], u,
                curvature_ref[u], wide_ref[u], stiff_wide_ref[u],
            )


def update_kernel(
    mix_ref, theta_ref, mine_ref, theirs_ref, search_images_ref, inverse_ref,
    modes_ref, images_ref, near_ref, far_ref, to_pair_ref, to_core_ref,
):
    depth, ny, nx = inverse_ref.shape
    nz = depth // 2
    for start in range(0, nx, LANES):
        lanes = slice(start, start + LANES)
        for u in range(depth):
            source, z = (mine_ref, u) if u < nz else (theirs_ref, u - nz)
            vectors = [source[a, z, :, lanes] for a in range(BLOCK)]
            images = [search_images_ref[a, u, :, lanes] for a in range(BLOCK)]
            inverse = inverse_ref[u, :, lanes]
            for j in range(MODES):
                mode = mix_ref[j, 0:1, :] * vectors[0]
                image = mix_ref[j, 0:1, :] * images[0]
                for a in range(1, BLOCK):
                    mode = mode + mix_ref[j, a : a + 1, :] * vectors[a]
                    image = image + mix_ref[j, a : a + 1, :] * images[a]
                modes_ref[j, u, :, lanes] = mode
                images_ref[j, u, :, lanes] = image
                correction = (image - theta_ref[j : j + 1, :] * mode) * inverse
                if u < nz:
                    near_ref[j, u, :, lanes] = correction
                else:
                    far_ref[j, u - nz, :, lanes] = correction

    @pl.loop(0, MODES)
    def _(j):
        field = lambda u: near_ref[j, u] if u < nz else far_ref[j, u - nz]
        to_pair, to_core = edges(field, depth)
        for u in range(depth):
            to_pair_ref[j, 2 * u : 2 * u + 2, :] = to_pair[u]
            to_core_ref[j, 2 * u : 2 * u + 2, :] = to_core[u]


def second_local_kernel(modes_ref, images_ref, near_ref, far_ref, curvature_ref, stiff_layers_ref, tile_ref):
    depth, ny, nx = curvature_ref.shape
    nz = depth // 2
    half = 8 * HALF
    products = jnp.zeros((4 * half, 3 * half), jnp.float32)
    low = jnp.zeros((half, half), jnp.float32)
    for u in range(depth):
        for start in range(0, ny, 8):
            part = slice(start, start + 8)
            field = near_ref[:, u, part, :] if u < nz else far_ref[:, u - nz, part, :]
            weight = stiff_layers_ref[u + 1, part, :][None]
            second = rows_of(field)
            rows = jnp.concatenate([rows_of(modes_ref[:, u, part, :]), second], axis=0)
            images = rows_of(images_ref[:, u, part, :])
            along_x = second_x(second)
            bent = rows_of(field * curvature_ref[u, part, :][None])
            products = products + inner(
                jnp.concatenate([rows, bent, images], axis=0), jnp.concatenate([rows, images], axis=0)
            )
            low = low + inner(rows_of(along_x.reshape(field.shape) * weight), along_x)
    gram = products[: 2 * half, : 2 * half]
    back = products[half : 2 * half, 2 * half :]
    low = low + products[2 * half : 3 * half, half : 2 * half]
    cross = products[3 * half :, : 2 * half]
    tile_ref[...] = (
        folded(gram[:half], 0)
        + folded(gram[half:], BLOCK)
        + folded(cross, 2 * BLOCK)
        + (folded(back, 3 * BLOCK) + folded(low, 3 * BLOCK + HALF))
    )


def second_across_kernel(
    near_ref, far_ref, beyond_ref, pair_ref, core_ref, stiff_layers_ref, tile_ref,
    sum_ref, wide_ref, change_ref,
):
    nz, ny = near_ref.shape[1:3]
    depth = 2 * nz
    wide_ref[...] = jnp.zeros(wide_ref.shape, jnp.float32)
    sources = [(near_ref, z) for z in range(nz)] + [(far_ref, z) for z in range(nz)]
    sources = sources + [(beyond_ref, 0), (beyond_ref, 1)]

    @pl.loop(0, MODES)
    def _(j):
        for u in range(depth):
            source, z = sources[u]
            rows = slice(2 * u, 2 * u + 2)
            store_wide(wide_ref, u, source[j, z], pair_ref[j, rows, :], core_ref[j, rows, :])
            wide = wide_ref[u]
            change = roll(wide, -1, 0) + roll(wide, 1, 0) - 2.0 * wide
            change_ref[j, u] = change[8 : 8 + ny]

    low = jnp.zeros((8 * MODES, 8 * MODES), jnp.float32)
    for u in range(depth):
        for start in range(0, ny, 8):
            part = slice(start, start + 8)

            def layer(k):
                source, z = sources[k]
                return source[:, z, part, :]

            change = change_ref[:, u, part, :]
            weight = stiff_layers_ref[u + 1, part, :][None]
            low = low + inner(rows_of(change * weight), rows_of(change))
            change = (layer(u + 2) + layer(u)) - 2.0 * layer(u + 1)
            weight = stiff_layers_ref[u + 2, part, :][None]
            low = low + inner(rows_of(change * weight), rows_of(change))
    sum_ref[...] = tile_ref[...] + folded(low, 3 * BLOCK + HALF)


def images_kernel(
    near_ref, far_ref, behind_ref, beyond_ref, pair_ref, core_ref,
    curvature_ref, stiff_layers_ref, stiff_wide_ref, images_ref, wide_ref,
):
    depth, ny, nx = curvature_ref.shape
    nz = depth // 2
    wide_ref[...] = jnp.zeros(wide_ref.shape, jnp.float32)
    sources = [(behind_ref, nz - 2), (behind_ref, nz - 1)]
    sources = sources + [(near_ref, z) for z in range(nz)] + [(far_ref, z) for z in range(nz)]
    sources = sources + [(beyond_ref, 0), (beyond_ref, 1)]

    @pl.loop(0, MODES)
    def _(j):
        layers = [source[j, z] for source, z in sources]
        for u in range(depth):
            rows = slice(2 * u, 2 * u + 2)
            store_wide(wide_ref, u, layers[u + 2], pair_ref[j, rows, :], core_ref[j, rows, :])
            images_ref[j, u] = apply_hessian(
                layers[u + 2], lambda k: layers[k + 2], lambda k: stiff_layers_ref[k + 1], u,
                curvature_ref[u], wide_ref[u], stiff_wide_ref[u],
            )


def density_kernel(
    factor, offset, mix_ref, theta_ref, modes_ref, corrections_ref, first_ref, second_ref, density_ref,
):
    nz, ny, nx = density_ref.shape[1:]
    for layer in range(nz):
        u = offset + layer
        place = layer if offset == 0 else nz - 1 - layer
        for start in range(0, nx, LANES):
            lanes = slice(start, start + LANES)
            vectors = [modes_ref[a, u, :, lanes] for a in range(MODES)]
            vectors = vectors + [corrections_ref[a, layer, :, lanes] for a in range(MODES)]
            images = [first_ref[a, u, :, lanes] for a in range(MODES)]
            images = images + [second_ref[a, u, :, lanes] for a in range(MODES)]
            mode_sum = jnp.zeros((ny, LANES), jnp.float32)
            residual_sum = jnp.zeros((ny, LANES), jnp.float32)
            for j in range(MODES):
                mode = mix_ref[j, 0:1, :] * vectors[0]
                image = mix_ref[j, 0:1, :] * images[0]
                for a in range(1, BLOCK):
                    mode = mode + mix_ref[j, a : a + 1, :] * vectors[a]
                    image = image + mix_ref[j, a : a + 1, :] * images[a]
                residual = image - theta_ref[j : j + 1, :] * mode
                mode_sum = mode_sum + mode * mode
                residual_sum = residual_sum + residual * residual
            density_ref[0, place, :, lanes] = factor * mode_sum
            density_ref[1, place, :, lanes] = factor * residual_sum


def merge_kernel(mine_ref, other_ref, modes_ref, residuals_ref):
    nz, ny, _ = modes_ref.shape
    half = ny // 2
    odd, high = is_odd() == 1, is_high() == 1
    for k, target in ((0, modes_ref), (1, residuals_ref)):
        for z in range(nz):
            mine = jnp.where(odd, mine_ref[k, nz - 1 - z], mine_ref[k, z])
            other = jnp.where(odd, other_ref[k, nz - 1 - z], other_ref[k, z])
            target[z, :half, :] = jnp.where(high, other, mine)
            target[z, half:, :] = jnp.where(high, mine, other)


def local(initial_block, concentration, stiffness):
    nz, ny, nx = concentration.shape
    half = ny // 2
    depth = 2 * nz
    cells_total = nz * ny * nx * lax.axis_size("gz") * lax.axis_size("gy")
    vector_rows = (BLOCK + 1, 2 * depth, nx)
    plane = (depth, half, nx)
    wide = (depth, half + 16, nx)
    mode_plane = (MODES,) + plane
    mode_half = (MODES, nz, half, nx)
    mode_rows = (MODES, 2 * depth, nx)

    mine, other = prepare(initial_block, stiffness, concentration)
    theirs = pair_swap(other)
    beyond = from_beyond(mine[:, :2])
    edge_rows = jnp.concatenate([initial_block[:, :, ny - 2 :], initial_block[:, :, :2]], axis=2)
    beside = core_swap(edge_rows)
    curvature = 3.0 * concentration * concentration - 1.0
    (tile,) = call(
        first_local_kernel,
        [(8, LANES)],
        [initial_block, beside, curvature, stiffness],
        scratch=[pltpu.VMEM((ny + 16, nx), jnp.float32), pltpu.VMEM((BLOCK, ny, nx), jnp.float32)],
        flops=100000000,
        name="first_local",
    )
    theirs, tile = lax.optimization_barrier((theirs, tile))
    to_pair, to_core = call(
        edges_kernel, [vector_rows, vector_rows], [mine, theirs], name="edges"
    )
    core_rows = core_swap(to_core)
    pair_rows = pair_swap(to_pair)
    held, beyond, to_pair, to_core = lax.optimization_barrier((theirs, beyond, to_pair, to_core))
    behind = from_behind(held[:, nz - 2 :])
    (tile,) = call(
        first_across_kernel,
        [(8, LANES)],
        [mine, theirs, beyond, tile],
        flops=25000000,
        name="first_across",
    )
    pencil, (behind, pair_rows, core_rows) = grid_sum(
        tile, (behind, pair_rows, core_rows), by_four=False
    )
    search_images, inverse, curvature, stiff_layers, stiff_wide = call(
        first_images_kernel,
        [(BLOCK,) + plane, plane, plane, (depth + 2, half, nx), wide],
        [mine, theirs, behind, beyond, pair_rows, core_rows],
        scratch=[pltpu.VMEM(wide, jnp.float32)],
        flops=6000000,
        name="first_images",
    )
    _, theta_rows, mix = ritz_pairs(pencil)
    modes, mode_images, near, far, to_pair, to_core = call(
        update_kernel,
        [mode_plane, mode_plane, mode_half, mode_half, mode_rows, mode_rows],
        [mix, theta_rows, mine, theirs, search_images, inverse],
        name="update",
    )

    beyond = from_beyond(near[:, :2])
    pair_rows = pair_swap(to_pair)
    core_rows = core_swap(to_core)
    (tile,) = call(
        second_local_kernel,
        [(8, LANES)],
        [modes, mode_images, near, far, curvature, stiff_layers],
        flops=80000000,
        name="second_local",
    )
    held, beyond, pair_rows, core_rows, tile = lax.optimization_barrier(
        (far, beyond, pair_rows, core_rows, tile)
    )
    behind = from_behind(held[:, nz - 2 :])
    (tile,) = call(
        second_across_kernel,
        [(8, LANES)],
        [near, far, beyond, pair_rows, core_rows, stiff_layers, tile],
        scratch=[pltpu.VMEM(wide, jnp.float32), pltpu.VMEM(mode_plane, jnp.float32)],
        flops=25000000,
        name="second_across",
    )
    pencil, behind = grid_sum(tile, behind, by_four=True)
    (correction_images,) = call(
        images_kernel,
        [mode_plane],
        [near, far, behind, beyond, pair_rows, core_rows, curvature, stiff_layers, stiff_wide],
        scratch=[pltpu.VMEM(wide, jnp.float32)],
        name="images",
    )
    theta, theta_rows, mix = ritz_pairs(pencil)
    shares = []
    for offset, corrections in ((nz, far), (0, near)):
        (share,) = call(
            functools.partial(density_kernel, float(cells_total / MODES), offset),
            [(2, nz, half, nx)],
            [mix, theta_rows, modes, corrections, mode_images, correction_images],
            name="densities",
        )
        shares.append(share)
    other = pair_swap(shares[0])
    mode_density, residual_density = call(
        merge_kernel, [(nz, ny, nx)] * 2, [shares[1], other], name="merge"
    )
    return (theta, mode_density, residual_density)


def solution(mesh):
    return jax.shard_map(
        local,
        mesh=mesh,
        in_specs=(P("img", "gz", "gy", None), P(("img", "gz"), "gy", None), P("gz", "gy", None)),
        out_specs=(P("img"), P(("img", "gz"), "gy", None), P(("img", "gz"), "gy", None)),
        check_vma=False,
    )
```

```python
import functools

import jax
import jax.numpy as jnp
from jax import lax
from jax.experimental import pallas as pl
from jax.experimental.pallas import tpu as pltpu
from jax.sharding import PartitionSpec as P

BLOCK = 16
MODES = 8
HALF = BLOCK // 2
LANES = 128
EARLY_SWEEPS = 5
MAX_SWEEPS = 14
HIGHEST = lax.Precision.HIGHEST
VMEM = pl.BlockSpec(memory_space=pltpu.VMEM)


def call(kernel, out_shapes, args, scratch=(), flops=1000000, name=None):
    out_shape = tuple(jax.ShapeDtypeStruct(s, jnp.float32) for s in out_shapes)
    moved = 4 * sum(x.size for x in list(args) + list(out_shape))
    return pl.pallas_call(
        kernel,
        out_shape=out_shape,
        in_specs=[VMEM] * len(args),
        out_specs=[VMEM] * len(out_shape),
        scratch_shapes=list(scratch),
        compiler_params=pltpu.CompilerParams(vmem_limit_bytes=40 * 1024 * 1024),
        cost_estimate=pl.CostEstimate(flops=flops, bytes_accessed=moved, transcendentals=0),
        name=name,
    )(*args)


def pair_swap(x):
    return lax.ppermute(x, "gz", [(i, i ^ 1) for i in range(lax.axis_size("gz"))])


def core_swap(x):
    return lax.ppermute(x, "gy", [(0, 1), (1, 0)])


def from_beyond(x):
    size = lax.axis_size("gz")
    return lax.ppermute(x, "gz", [((i + (2 if i % 2 == 0 else size - 2)) % size, i) for i in range(size)])


def from_behind(x):
    size = lax.axis_size("gz")
    return lax.ppermute(x, "gz", [((i + (size - 2 if i % 2 == 0 else 2)) % size, i) for i in range(size)])


def grid_sum(x, later, by_four):
    axes = ("gz", "gy")
    total = lax.axis_size("gz") * lax.axis_size("gy")
    if total & (total - 1):
        return lax.psum(x, axes), later

    def other(mask):
        return lax.ppermute(x, axes, [(i, i ^ mask) for i in range(total)])

    mask = 1
    while mask < total:
        wide = by_four and mask >= 4 and 4 * mask <= total
        if mask * (4 if wide else 2) == total:
            x, later = lax.optimization_barrier((x, later))
        if wide:
            x = (x + other(mask)) + (other(2 * mask) + other(3 * mask))
            mask *= 4
        else:
            x = x + other(mask)
            mask *= 2
    return x, later


def spread_rows(x, k):
    return jnp.broadcast_to(x[k : k + 1, :], (8, LANES))


def every_row(x):
    x = x + pltpu.roll(x, 4, 0)
    x = x + pltpu.roll(x, 2, 0)
    return x + pltpu.roll(x, 1, 0)


def packed_sums(tiles, row):
    low4, low2, low1 = row < 4, (row & 2) == 0, (row & 1) == 0
    tiles = [
        jnp.where(low4, tiles[k], tiles[k + 4])
        + pltpu.roll(jnp.where(low4, tiles[k + 4], tiles[k]), 4, 0)
        for k in range(4)
    ]

    def fold(a, b, low, step):
        other = jnp.where(low, b, a)
        moved = jnp.where(low, pltpu.roll(other, 8 - step, 0), pltpu.roll(other, step, 0))
        return jnp.where(low, a, b) + moved

    tiles = [fold(tiles[k], tiles[k + 2], low2, 2) for k in range(2)]
    return fold(tiles[0], tiles[1], low1, 1)


def tournament():
    players = list(range(BLOCK))
    rounds = []
    for _ in range(BLOCK - 1):
        rounds.append([(players[k], players[BLOCK - 1 - k]) for k in range(HALF)])
        players = [players[0], players[-1]] + players[1:-1]
    return rounds


def ritz_kernel(pencil_ref, theta_ref, theta_rows_ref, mix_ref):
    total = pencil_ref[...]
    row = lax.broadcasted_iota(jnp.int32, (8, LANES), 0)
    lane = lax.broadcasted_iota(jnp.int32, (8, LANES), 1)

    def columns(upper, lower):
        return (
            [jnp.broadcast_to(upper[:, k : k + 1], (8, LANES)) for k in range(BLOCK)],
            [jnp.broadcast_to(lower[:, k : k + 1], (8, LANES)) for k in range(BLOCK)],
        )

    def entry(upper, lower, k):
        return spread_rows(upper, k) if k < 8 else spread_rows(lower, k - 8)

    gram_u, gram_l = columns(total[:, :BLOCK], total[:, BLOCK : 2 * BLOCK])
    zero = jnp.zeros((8, LANES), jnp.float32)
    inverse_u = [jnp.where(row == k, 1.0, 0.0).astype(jnp.float32) for k in range(8)] + [zero] * 8
    inverse_l = [zero] * 8 + [
        jnp.where(row == k, 1.0, 0.0).astype(jnp.float32) for k in range(8)
    ]
    for k in range(BLOCK):
        root = lax.rsqrt(entry(gram_u[k], gram_l[k], k))
        gram_u[k] = gram_u[k] * root
        gram_l[k] = gram_l[k] * root
        inverse_u[k] = inverse_u[k] * root
        inverse_l[k] = inverse_l[k] * root
        for i in range(k + 1, BLOCK):
            factor = entry(gram_u[k], gram_l[k], i)
            if i < 8:
                gram_u[i] = gram_u[i] - factor * gram_u[k]
            gram_l[i] = gram_l[i] - factor * gram_l[k]
            inverse_u[i] = inverse_u[i] - factor * inverse_u[k]
            if k >= 8:
                inverse_l[i] = inverse_l[i] - factor * inverse_l[k]
    transposed_u, transposed_l = zero, zero
    for k in range(BLOCK):
        transposed_u = jnp.where(lane == k, inverse_u[k], transposed_u)
        transposed_l = jnp.where(lane == k, inverse_l[k], transposed_l)
    transposed = jnp.concatenate([transposed_u, transposed_l], axis=0)[:, :BLOCK]

    dot = functools.partial(
        lax.dot_general, precision=HIGHEST, preferred_element_type=jnp.float32
    )
    stiff = jnp.concatenate(
        [total[:, 2 * BLOCK : 3 * BLOCK], total[:, 3 * BLOCK : 4 * BLOCK]], axis=0
    )
    half_way = dot(stiff, transposed, (((1,), (0,)), ((), ())))
    projected = dot(transposed, half_way, (((0,), (0,)), ((), ())))

    upper, lower = columns(projected[:8], projected[8:])
    diagonal = zero
    for k in range(8):
        diagonal = diagonal + jnp.where(row == k, upper[k] + lower[k + 8], 0.0)
    mean = every_row(diagonal) * (1.0 / BLOCK)
    size = zero
    for k in range(8):
        upper[k] = upper[k] - jnp.where(row == k, mean, 0.0)
        lower[k + 8] = lower[k + 8] - jnp.where(row == k, mean, 0.0)
    for k in range(BLOCK):
        size = size + (upper[k] * upper[k] + lower[k] * lower[k])
    scale = 1.25 * jnp.sqrt(every_row(size)) + 1e-30
    shrink = 1.0 / scale
    for k in range(BLOCK):
        upper[k] = upper[k] * shrink
        lower[k] = lower[k] * shrink
    for k in range(8):
        upper[k] = upper[k] + jnp.where(row == k, 1.0, 0.0)
        lower[k + 8] = lower[k + 8] + jnp.where(row == k, 1.0, 0.0)

    def squares(upper, lower):
        top = packed_sums([upper[k] * upper[k] + lower[k] * lower[k] for k in range(8)], row)
        bottom = packed_sums(
            [upper[15 - k] * upper[15 - k] + lower[15 - k] * lower[15 - k] for k in range(8)], row
        )
        return top, bottom

    def sweep(upper, lower):
        upper, lower = list(upper), list(lower)
        top, bottom = squares(upper, lower)
        worst = zero
        for pairs in tournament():
            g = packed_sums([upper[i] * upper[j] + lower[i] * lower[j] for i, j in pairs], row)
            d = bottom - top
            g2 = g * g
            worst = jnp.maximum(worst, g2)
            dd = jnp.maximum(jnp.abs(d), 1e-18)
            ih = lax.rsqrt(g2 + 0.25 * (dd * dd))
            c2 = 0.5 + (0.25 * dd) * ih
            ic = lax.rsqrt(c2)
            c = c2 * ic
            s = (jnp.where(d >= 0.0, 0.5, -0.5) * g) * (ih * ic)
            move = (s * ic) * g
            top = top - move
            bottom = bottom + move
            for k, (i, j) in enumerate(pairs):
                ck, sk = spread_rows(c, k), spread_rows(s, k)
                ui, uj, li, lj = upper[i], upper[j], lower[i], lower[j]
                upper[i] = ck * ui - sk * uj
                lower[i] = ck * li - sk * lj
                upper[j] = sk * ui + ck * uj
                lower[j] = sk * li + ck * lj
            next_top = jnp.where(
                row == 0, top, jnp.where(row == 1, pltpu.roll(bottom, 1, 0), pltpu.roll(top, 1, 0))
            )
            bottom = jnp.where(row == 7, top, pltpu.roll(bottom, 7, 0))
            top = next_top
        return worst, tuple(upper), tuple(lower)

    def early(_, carry):
        return sweep(*carry)[1:]

    def late(carry):
        count, _, upper, lower = carry
        worst, upper, lower = sweep(upper, lower)
        for step in (4, 2, 1):
            worst = jnp.maximum(worst, pltpu.roll(worst, step, 0))
        return count + 1, worst[0, 0], upper, lower

    def unfinished(carry):
        count, worst, _, _ = carry
        return jnp.logical_and(count < MAX_SWEEPS, worst > 1.6e-7)

    upper, lower = lax.fori_loop(0, EARLY_SWEEPS, early, (tuple(upper), tuple(lower)))
    _, _, upper, lower = lax.while_loop(
        unfinished, late, (jnp.int32(EARLY_SWEEPS), jnp.float32(1.0), upper, lower)
    )

    top, bottom = squares(upper, lower)
    rank_top, rank_bottom = zero, zero
    for k in range(BLOCK):
        mine = spread_rows(top, k) if k < 8 else spread_rows(bottom, 15 - k)
        before_top = (mine < top) | ((mine == top) & (k < row))
        before_bottom = (mine < bottom) | ((mine == bottom) & (k < 15 - row))
        rank_top = rank_top + jnp.where(before_top, 1.0, 0.0)
        rank_bottom = rank_bottom + jnp.where(before_bottom, 1.0, 0.0)
    inverse_top, inverse_bottom = lax.rsqrt(top), lax.rsqrt(bottom)
    value_top, value_bottom = top * inverse_top, bottom * inverse_bottom
    lane_float = lane.astype(jnp.float32)
    theta = zero
    vectors_u, vectors_l = zero, zero
    for k in range(BLOCK):

        def of(first, second):
            return spread_rows(first, k) if k < 8 else spread_rows(second, 15 - k)

        here = lane_float == of(rank_top, rank_bottom)
        inverse_norm = of(inverse_top, inverse_bottom)
        theta = jnp.where(here, of(value_top, value_bottom), theta)
        vectors_u = jnp.where(here, upper[k] * inverse_norm, vectors_u)
        vectors_l = jnp.where(here, lower[k] * inverse_norm, vectors_l)
    theta = mean + scale * (theta - 1.0)
    theta_ref[...] = theta[0, :MODES]
    on_row = jnp.sum(jnp.where(row == lane, theta, 0.0), axis=1, keepdims=True)
    theta_rows_ref[...] = jnp.broadcast_to(on_row, (8, LANES))
    vectors = jnp.concatenate([vectors_u, vectors_l], axis=0)
    mix = dot(transposed, vectors, (((1,), (0,)), ((), ())))
    for j in range(MODES):
        mix_ref[j] = jnp.broadcast_to(mix[:, j : j + 1], (BLOCK, LANES))


def ritz_pairs(pencil):
    return call(
        ritz_kernel,
        [(MODES,), (8, LANES), (MODES, BLOCK, LANES)],
        [pencil],
        flops=10000000,
        name="ritz_pairs",
    )


def inner(a, b):
    return lax.dot_general(
        a, b, (((1,), (1,)), ((), ())), precision=HIGHEST, preferred_element_type=jnp.float32
    )


def folded(products, offset):
    height, width = products.shape
    row = lax.broadcasted_iota(jnp.int32, (height, width), 0)
    column = lax.broadcasted_iota(jnp.int32, (height, width), 1)
    same = jnp.where((row & 7) == (column & 7), products, 0.0)
    sums = jnp.sum(same.reshape(height // 8, 8, width), axis=1)
    row = lax.broadcasted_iota(jnp.int32, (width, LANES), 0)
    lane = lax.broadcasted_iota(jnp.int32, (width, LANES), 1)
    place = jnp.where((row >> 3) + offset == lane, 1.0, 0.0).astype(jnp.float32)
    return jnp.dot(sums, place, precision=HIGHEST, preferred_element_type=jnp.float32)


def rows_of(x):
    return x.reshape(x.shape[0] * x.shape[1], x.shape[2])


def roll(x, shift, axis):
    return pltpu.roll(x, shift % x.shape[axis], axis)


def store_y_differences(source_ref, beside_ref, wide_ref, change_ref, z):
    count, _, ny, _ = source_ref.shape

    @pl.loop(0, count)
    def _(a):
        wide_ref[6:8, :] = beside_ref[a, z, :2]
        wide_ref[8 : 8 + ny, :] = source_ref[a, z]
        wide_ref[8 + ny : 10 + ny, :] = beside_ref[a, z, 2:]
        wide = wide_ref[...]
        change = roll(wide, -1, 0) + roll(wide, 1, 0) - 2.0 * wide
        change_ref[a] = change[8 : 8 + ny]


def second_x(rows):
    return roll(rows, -1, 1) + roll(rows, 1, 1) - 2.0 * rows


def is_odd():
    return lax.rem(lax.axis_index("gz"), 2)


def is_high():
    return lax.rem(1 + is_odd() + lax.axis_index("gy"), 2)


def prepare_kernel(block_ref, stiffness_ref, concentration_ref, mine_ref, other_ref, arrived):
    nz, ny, _ = concentration_ref.shape
    half = ny // 2
    odd, high = is_odd(), is_high()
    upper = pl.ds(pl.multiple_of(half * high, half), half)
    lower = pl.ds(pl.multiple_of(half * (1 - high), half), half)
    copies = []
    for z in range(nz):
        inward = z + odd * (nz - 1 - 2 * z)
        outward = nz - 1 - inward
        for layer, rows, target in ((inward, upper, mine_ref), (outward, lower, other_ref)):
            moves = (
                (block_ref.at[:, layer, rows, :], target.at[0:BLOCK, z]),
                (stiffness_ref.at[layer, rows, :], target.at[BLOCK, z]),
                (concentration_ref.at[layer, rows, :], target.at[BLOCK + 1, z]),
            )
            for source, place in moves:
                copies.append(pltpu.make_async_copy(source, place, arrived.at[len(copies)]))
    for copy in copies:
        copy.start()
    for copy in copies:
        copy.wait()


def prepare(block, stiffness, concentration):
    nz, ny, nx = concentration.shape
    shape = jax.ShapeDtypeStruct((BLOCK + 2, nz, ny // 2, nx), jnp.float32)
    return pl.pallas_call(
        prepare_kernel,
        out_shape=(shape, shape),
        in_specs=[pl.BlockSpec(memory_space=pltpu.HBM)] * 3,
        out_specs=[VMEM] * 2,
        scratch_shapes=[pltpu.SemaphoreType.DMA((6 * nz,))],
        compiler_params=pltpu.CompilerParams(vmem_limit_bytes=62 * 1024 * 1024),
        name="prepare",
    )(block, stiffness, concentration)


def first_local_kernel(block_ref, beside_ref, curvature_ref, stiffness_ref, tile_ref, wide_ref, change_ref):
    nz, ny, nx = curvature_ref.shape
    wide_ref[...] = jnp.zeros(wide_ref.shape, jnp.float32)
    gram = jnp.zeros((8 * BLOCK, 8 * BLOCK), jnp.float32)
    stiff = jnp.zeros((8 * BLOCK, 8 * BLOCK), jnp.float32)
    for z in range(nz):
        store_y_differences(block_ref, beside_ref, wide_ref, change_ref, z)
        for start in range(0, ny, 8):
            part = slice(start, start + 8)
            field = block_ref[:, z, part, :]
            weight = stiffness_ref[z, part, :][None]
            rows = rows_of(field)
            along_x = second_x(rows)
            along_y = change_ref[:, part, :]
            gram = gram + inner(rows, rows)
            stiff = stiff + inner(rows_of(field * curvature_ref[z, part, :][None]), rows)
            stiff = stiff + inner(rows_of(along_x.reshape(field.shape) * weight), along_x)
            stiff = stiff + inner(rows_of(along_y * weight), rows_of(along_y))
    half = 8 * HALF
    tile_ref[...] = (
        folded(gram[:half], 0)
        + folded(gram[half:], BLOCK)
        + folded(stiff[:half], 2 * BLOCK)
        + folded(stiff[half:], 3 * BLOCK)
    )


def edges(field, layers):
    high = is_high() == 1
    to_pair, to_core = [], []
    for u in range(layers):
        first, last = field(u)[:2], field(u)[-2:]
        to_pair.append(jnp.where(high, first, last))
        to_core.append(jnp.where(high, last, first))
    return to_pair[::-1], to_core


def edges_kernel(mine_ref, theirs_ref, pair_ref, core_ref):
    nz = mine_ref.shape[1]

    @pl.loop(0, BLOCK + 1)
    def _(a):
        field = lambda u: mine_ref[a, u] if u < nz else theirs_ref[a, u - nz]
        to_pair, to_core = edges(field, 2 * nz)
        for u in range(2 * nz):
            pair_ref[a, 2 * u : 2 * u + 2, :] = to_pair[u]
            core_ref[a, 2 * u : 2 * u + 2, :] = to_core[u]


def first_across_kernel(mine_ref, theirs_ref, beyond_ref, tile_ref, sum_ref):
    nz, ny = mine_ref.shape[1:3]
    half = 8 * HALF
    stiff = jnp.zeros((8 * BLOCK, 8 * BLOCK), jnp.float32)
    sources = [(mine_ref, z) for z in range(nz)] + [(theirs_ref, z) for z in range(nz)]
    sources = sources + [(beyond_ref, z) for z in range(2)]
    for u in range(1, 2 * nz + 1):
        for start in range(0, ny, 8):
            part = slice(start, start + 8)

            def layer(k):
                source, z = sources[k]
                return source[:BLOCK, z, part, :]

            source, z = sources[u]
            change = (layer(u + 1) + layer(u - 1)) - 2.0 * layer(u)
            weight = source[BLOCK, z, part, :]
            stiff = stiff + inner(rows_of(change * weight[None]), rows_of(change))
    sum_ref[...] = (
        tile_ref[...] + folded(stiff[:half], 2 * BLOCK) + folded(stiff[half:], 3 * BLOCK)
    )


def apply_hessian(field, layers, stiff_layers, u, curvature, wide, stiff_wide):
    def flux(k):
        return stiff_layers(k) * ((layers(k + 1) + layers(k - 1)) - 2.0 * layers(k))

    total = curvature * field + (flux(u + 1) + flux(u - 1) - 2.0 * flux(u))
    change = second_x(stiff_layers(u) * second_x(field))
    total = total + change
    change = stiff_wide * (roll(wide, -1, 0) + roll(wide, 1, 0) - 2.0 * wide)
    change = roll(change, -1, 0) + roll(change, 1, 0) - 2.0 * change
    return total + change[8 : 8 + field.shape[0]]


def store_wide(wide_ref, index, field, pair_rows, core_rows):
    ny = field.shape[0]
    high = is_high() == 1
    wide_ref[index, 6:8, :] = jnp.where(high, pair_rows, core_rows)
    wide_ref[index, 8 : 8 + ny, :] = field
    wide_ref[index, 8 + ny : 10 + ny, :] = jnp.where(high, core_rows, pair_rows)


def first_images_kernel(
    mine_ref, theirs_ref, behind_ref, beyond_ref, pair_ref, core_ref,
    images_ref, inverse_ref, curvature_ref, stiff_layers_ref, stiff_wide_ref, wide_ref,
):
    depth, ny, nx = curvature_ref.shape
    nz = depth // 2
    wide_ref[...] = jnp.zeros(wide_ref.shape, jnp.float32)
    stiff_wide_ref[...] = jnp.zeros(stiff_wide_ref.shape, jnp.float32)
    sources = [(behind_ref, nz - 2), (behind_ref, nz - 1)]
    sources = sources + [(mine_ref, z) for z in range(nz)] + [(theirs_ref, z) for z in range(nz)]
    sources = sources + [(beyond_ref, 0), (beyond_ref, 1)]
    for k in range(depth + 2):
        source, z = sources[k + 1]
        stiff_layers_ref[k] = source[BLOCK, z]
    for u in range(depth):
        rows = slice(2 * u, 2 * u + 2)
        stiff = stiff_layers_ref[u + 1]
        store_wide(stiff_wide_ref, u, stiff, pair_ref[BLOCK, rows, :], core_ref[BLOCK, rows, :])
        source, z = sources[u + 2]
        concentration = source[BLOCK + 1, z]
        curvature = 3.0 * concentration * concentration - 1.0
        curvature_ref[u] = curvature
        total = (curvature + 2.0) + 12.0 * stiff
        total = total + (stiff_layers_ref[u] + stiff_layers_ref[u + 2])
        total = total + (stiff_wide_ref[u, 7 : 7 + ny, :] + stiff_wide_ref[u, 9 : 9 + ny, :])
        total = total + (roll(stiff, -1, 1) + roll(stiff, 1, 1))
        inverse_ref[u] = 1.0 / total

    @pl.loop(0, BLOCK)
    def _(a):
        layers = [source[a, z] for source, z in sources]
        for u in range(depth):
            rows = slice(2 * u, 2 * u + 2)
            store_wide(wide_ref, u, layers[u + 2], pair_ref[a, rows, :], core_ref[a, rows, :])
            images_ref[a, u] = apply_hessian(
                layers[u + 2], lambda k: layers[k + 2], lambda k: stiff_layers_ref[k + 1], u,
                curvature_ref[u], wide_ref[u], stiff_wide_ref[u],
            )


def update_kernel(
    mix_ref, theta_ref, mine_ref, theirs_ref, search_images_ref, inverse_ref,
    modes_ref, images_ref, near_ref, far_ref, to_pair_ref, to_core_ref,
):
    depth, ny, nx = inverse_ref.shape
    nz = depth // 2
    for start in range(0, nx, LANES):
        lanes = slice(start, start + LANES)
        for u in range(depth):
            source, z = (mine_ref, u) if u < nz else (theirs_ref, u - nz)
            vectors = [source[a, z, :, lanes] for a in range(BLOCK)]
            images = [search_images_ref[a, u, :, lanes] for a in range(BLOCK)]
            inverse = inverse_ref[u, :, lanes]
            for j in range(MODES):
                mode = mix_ref[j, 0:1, :] * vectors[0]
                image = mix_ref[j, 0:1, :] * images[0]
                for a in range(1, BLOCK):
                    mode = mode + mix_ref[j, a : a + 1, :] * vectors[a]
                    image = image + mix_ref[j, a : a + 1, :] * images[a]
                modes_ref[j, u, :, lanes] = mode
                images_ref[j, u, :, lanes] = image
                correction = (image - theta_ref[j : j + 1, :] * mode) * inverse
                if u < nz:
                    near_ref[j, u, :, lanes] = correction
                else:
                    far_ref[j, u - nz, :, lanes] = correction

    @pl.loop(0, MODES)
    def _(j):
        field = lambda u: near_ref[j, u] if u < nz else far_ref[j, u - nz]
        to_pair, to_core = edges(field, depth)
        for u in range(depth):
            to_pair_ref[j, 2 * u : 2 * u + 2, :] = to_pair[u]
            to_core_ref[j, 2 * u : 2 * u + 2, :] = to_core[u]


def second_local_kernel(modes_ref, images_ref, near_ref, far_ref, curvature_ref, stiff_layers_ref, tile_ref):
    depth, ny, nx = curvature_ref.shape
    nz = depth // 2
    half = 8 * HALF
    products = jnp.zeros((4 * half, 3 * half), jnp.float32)
    low = jnp.zeros((half, half), jnp.float32)
    for u in range(depth):
        for start in range(0, ny, 8):
            part = slice(start, start + 8)
            field = near_ref[:, u, part, :] if u < nz else far_ref[:, u - nz, part, :]
            weight = stiff_layers_ref[u + 1, part, :][None]
            second = rows_of(field)
            rows = jnp.concatenate([rows_of(modes_ref[:, u, part, :]), second], axis=0)
            images = rows_of(images_ref[:, u, part, :])
            along_x = second_x(second)
            bent = rows_of(field * curvature_ref[u, part, :][None])
            products = products + inner(
                jnp.concatenate([rows, bent, images], axis=0), jnp.concatenate([rows, images], axis=0)
            )
            low = low + inner(rows_of(along_x.reshape(field.shape) * weight), along_x)
    gram = products[: 2 * half, : 2 * half]
    back = products[half : 2 * half, 2 * half :]
    low = low + products[2 * half : 3 * half, half : 2 * half]
    cross = products[3 * half :, : 2 * half]
    tile_ref[...] = (
        folded(gram[:half], 0)
        + folded(gram[half:], BLOCK)
        + folded(cross, 2 * BLOCK)
        + (folded(back, 3 * BLOCK) + folded(low, 3 * BLOCK + HALF))
    )


def second_across_kernel(
    near_ref, far_ref, beyond_ref, pair_ref, core_ref, stiff_layers_ref, tile_ref,
    sum_ref, wide_ref, change_ref,
):
    nz, ny = near_ref.shape[1:3]
    depth = 2 * nz
    wide_ref[...] = jnp.zeros(wide_ref.shape, jnp.float32)
    sources = [(near_ref, z) for z in range(nz)] + [(far_ref, z) for z in range(nz)]
    sources = sources + [(beyond_ref, 0), (beyond_ref, 1)]

    @pl.loop(0, MODES)
    def _(j):
        for u in range(depth):
            source, z = sources[u]
            rows = slice(2 * u, 2 * u + 2)
            store_wide(wide_ref, u, source[j, z], pair_ref[j, rows, :], core_ref[j, rows, :])
            wide = wide_ref[u]
            change = roll(wide, -1, 0) + roll(wide, 1, 0) - 2.0 * wide
            change_ref[j, u] = change[8 : 8 + ny]

    low = jnp.zeros((8 * MODES, 8 * MODES), jnp.float32)
    for u in range(depth):
        for start in range(0, ny, 8):
            part = slice(start, start + 8)

            def layer(k):
                source, z = sources[k]
                return source[:, z, part, :]

            change = change_ref[:, u, part, :]
            weight = stiff_layers_ref[u + 1, part, :][None]
            low = low + inner(rows_of(change * weight), rows_of(change))
            change = (layer(u + 2) + layer(u)) - 2.0 * layer(u + 1)
            weight = stiff_layers_ref[u + 2, part, :][None]
            low = low + inner(rows_of(change * weight), rows_of(change))
    sum_ref[...] = tile_ref[...] + folded(low, 3 * BLOCK + HALF)


def images_kernel(
    near_ref, far_ref, behind_ref, beyond_ref, pair_ref, core_ref,
    curvature_ref, stiff_layers_ref, stiff_wide_ref, images_ref, wide_ref,
):
    depth, ny, nx = curvature_ref.shape
    nz = depth // 2
    wide_ref[...] = jnp.zeros(wide_ref.shape, jnp.float32)
    sources = [(behind_ref, nz - 2), (behind_ref, nz - 1)]
    sources = sources + [(near_ref, z) for z in range(nz)] + [(far_ref, z) for z in range(nz)]
    sources = sources + [(beyond_ref, 0), (beyond_ref, 1)]

    @pl.loop(0, MODES)
    def _(j):
        layers = [source[j, z] for source, z in sources]
        for u in range(depth):
            rows = slice(2 * u, 2 * u + 2)
            store_wide(wide_ref, u, layers[u + 2], pair_ref[j, rows, :], core_ref[j, rows, :])
            images_ref[j, u] = apply_hessian(
                layers[u + 2], lambda k: layers[k + 2], lambda k: stiff_layers_ref[k + 1], u,
                curvature_ref[u], wide_ref[u], stiff_wide_ref[u],
            )


def density_kernel(
    factor, offset, mix_ref, theta_ref, modes_ref, corrections_ref, first_ref, second_ref, density_ref,
):
    nz, ny, nx = density_ref.shape[1:]
    for layer in range(nz):
        u = offset + layer
        place = layer if offset == 0 else nz - 1 - layer
        for start in range(0, nx, LANES):
            lanes = slice(start, start + LANES)
            vectors = [modes_ref[a, u, :, lanes] for a in range(MODES)]
            vectors = vectors + [corrections_ref[a, layer, :, lanes] for a in range(MODES)]
            images = [first_ref[a, u, :, lanes] for a in range(MODES)]
            images = images + [second_ref[a, u, :, lanes] for a in range(MODES)]
            mode_sum = jnp.zeros((ny, LANES), jnp.float32)
            residual_sum = jnp.zeros((ny, LANES), jnp.float32)
            for j in range(MODES):
                mode = mix_ref[j, 0:1, :] * vectors[0]
                image = mix_ref[j, 0:1, :] * images[0]
                for a in range(1, BLOCK):
                    mode = mode + mix_ref[j, a : a + 1, :] * vectors[a]
                    image = image + mix_ref[j, a : a + 1, :] * images[a]
                residual = image - theta_ref[j : j + 1, :] * mode
                mode_sum = mode_sum + mode * mode
                residual_sum = residual_sum + residual * residual
            density_ref[0, place, :, lanes] = factor * mode_sum
            density_ref[1, place, :, lanes] = factor * residual_sum


def merge_kernel(mine_ref, other_ref, modes_ref, residuals_ref):
    nz, ny, _ = modes_ref.shape
    half = ny // 2
    odd, high = is_odd() == 1, is_high() == 1
    for k, target in ((0, modes_ref), (1, residuals_ref)):
        for z in range(nz):
            mine = jnp.where(odd, mine_ref[k, nz - 1 - z], mine_ref[k, z])
            other = jnp.where(odd, other_ref[k, nz - 1 - z], other_ref[k, z])
            target[z, :half, :] = jnp.where(high, other, mine)
            target[z, half:, :] = jnp.where(high, mine, other)


def local(initial_block, concentration, stiffness):
    nz, ny, nx = concentration.shape
    half = ny // 2
    depth = 2 * nz
    cells_total = nz * ny * nx * lax.axis_size("gz") * lax.axis_size("gy")
    vector_rows = (BLOCK + 1, 2 * depth, nx)
    plane = (depth, half, nx)
    wide = (depth, half + 16, nx)
    mode_plane = (MODES,) + plane
    mode_half = (MODES, nz, half, nx)
    mode_rows = (MODES, 2 * depth, nx)

    mine, other = prepare(initial_block, stiffness, concentration)
    theirs = pair_swap(other)
    beyond = from_beyond(mine[:, :2])
    edge_rows = jnp.concatenate([initial_block[:, :, ny - 2 :], initial_block[:, :, :2]], axis=2)
    beside = core_swap(edge_rows)
    curvature = 3.0 * concentration * concentration - 1.0
    (tile,) = call(
        first_local_kernel,
        [(8, LANES)],
        [initial_block, beside, curvature, stiffness],
        scratch=[pltpu.VMEM((ny + 16, nx), jnp.float32), pltpu.VMEM((BLOCK, ny, nx), jnp.float32)],
        flops=100000000,
        name="first_local",
    )
    theirs, tile = lax.optimization_barrier((theirs, tile))
    to_pair, to_core = call(
        edges_kernel, [vector_rows, vector_rows], [mine, theirs], name="edges"
    )
    core_rows = core_swap(to_core)
    pair_rows = pair_swap(to_pair)
    held, beyond, to_pair, to_core = lax.optimization_barrier((theirs, beyond, to_pair, to_core))
    behind = from_behind(held[:, nz - 2 :])
    (tile,) = call(
        first_across_kernel,
        [(8, LANES)],
        [mine, theirs, beyond, tile],
        flops=25000000,
        name="first_across",
    )
    pencil, (behind, pair_rows, core_rows) = grid_sum(
        tile, (behind, pair_rows, core_rows), by_four=False
    )
    search_images, inverse, curvature, stiff_layers, stiff_wide = call(
        first_images_kernel,
        [(BLOCK,) + plane, plane, plane, (depth + 2, half, nx), wide],
        [mine, theirs, behind, beyond, pair_rows, core_rows],
        scratch=[pltpu.VMEM(wide, jnp.float32)],
        flops=6000000,
        name="first_images",
    )
    _, theta_rows, mix = ritz_pairs(pencil)
    modes, mode_images, near, far, to_pair, to_core = call(
        update_kernel,
        [mode_plane, mode_plane, mode_half, mode_half, mode_rows, mode_rows],
        [mix, theta_rows, mine, theirs, search_images, inverse],
        name="update",
    )

    beyond = from_beyond(near[:, :2])
    pair_rows = pair_swap(to_pair)
    core_rows = core_swap(to_core)
    (tile,) = call(
        second_local_kernel,
        [(8, LANES)],
        [modes, mode_images, near, far, curvature, stiff_layers],
        flops=80000000,
        name="second_local",
    )
    held, beyond, pair_rows, core_rows, tile = lax.optimization_barrier(
        (far, beyond, pair_rows, core_rows, tile)
    )
    behind = from_behind(held[:, nz - 2 :])
    (tile,) = call(
        second_across_kernel,
        [(8, LANES)],
        [near, far, beyond, pair_rows, core_rows, stiff_layers, tile],
        scratch=[pltpu.VMEM(wide, jnp.float32), pltpu.VMEM(mode_plane, jnp.float32)],
        flops=25000000,
        name="second_across",
    )
    pencil, behind = grid_sum(tile, behind, by_four=True)
    (correction_images,) = call(
        images_kernel,
        [mode_plane],
        [near, far, behind, beyond, pair_rows, core_rows, curvature, stiff_layers, stiff_wide],
        scratch=[pltpu.VMEM(wide, jnp.float32)],
        name="images",
    )
    theta, theta_rows, mix = ritz_pairs(pencil)
    shares = []
    for offset, corrections in ((nz, far), (0, near)):
        (share,) = call(
            functools.partial(density_kernel, float(cells_total / MODES), offset),
            [(2, nz, half, nx)],
            [mix, theta_rows, modes, corrections, mode_images, correction_images],
            name="densities",
        )
        shares.append(share)
    other = pair_swap(shares[0])
    mode_density, residual_density = call(
        merge_kernel, [(nz, ny, nx)] * 2, [shares[1], other], name="merge"
    )
    return (theta, mode_density, residual_density)


def solution(mesh):
    return jax.shard_map(
        local,
        mesh=mesh,
        in_specs=(P("img", "gz", "gy", None), P(("img", "gz"), "gy", None), P("gz", "gy", None)),
        out_specs=(P("img"), P(("img", "gz"), "gy", None), P(("img", "gz"), "gy", None)),
        check_vma=False,
    )
```
